32 devices in a mesh: gx: 4 (over y, core), gy: 4 (over z), gz: 2 (over x).
Axes of the slice: x: 2, y: 2, z: 4, core: 2. Of those that a mesh axis runs over, the one named last changes fastest.
Arguments:
- density: float32 [32, 64, 4096], P('gz', 'gx', 'gy'), may hold values from 0.1 to 10
Outputs:
- details_one: float32 [7, 16, 32, 2048], P(None, 'gz', 'gx', 'gy')
- details_two: float32 [7, 8, 16, 1024], P(None, 'gz', 'gx', 'gy')
- details_three: float32 [7, 4, 8, 512], P(None, 'gz', 'gx', 'gy')
- approximation: float32 [4, 8, 512], P('gz', 'gx', 'gy')
The draws below stay inside these ranges and needn't reach their ends.
All inputs are finite; a program needn't handle non-finite values.
Results may differ from the reference program's by a relative error of at most 0.00011.
Values sent between devices are 32-bit elements; how exact they have to be, the bound alone decides.
A program may use at most 128 MiB of HBM per device.

```python
import math
import jax
import jax.numpy as jnp

NX = 64
NY = 4096
NZ = 32


def shard_levels(own_key, dims, split, smallest, high):
    loudness, own = 1.0, jax.random.fold_in(own_key, 6)
    for axis_at, shards_of in split:
        heights = jnp.exp(jax.random.uniform(jax.random.fold_in(own, axis_at), (shards_of,), jnp.float32, smallest / len(split), high / len(split)))
        loudness = loudness * jnp.repeat(heights, dims[axis_at] // shards_of).reshape([-1 if axis == axis_at else 1 for axis in range(len(dims))])
    return loudness


def setup_inputs(seed: int = 0) -> dict:
    key_of = jax.random.split(jax.random.key(seed), 2)
    density = jnp.clip(jnp.exp(math.log(10.0) - 4.6051702 * jax.random.uniform(key_of[0], (NZ, NX, NY), jnp.float32) ** shard_levels(key_of[0], (NZ, NX, NY), ((0, 2), (1, 4), (2, 4)), -0.2, 0.2)), 0.1, 10.0)
    return dict(density=density)


ALPHA = -1.586134342
BETA = -0.05298011854
GAMMA = 0.8829110762
DELTA = 0.4435068522
ZETA = 1.149604398


def lift_padded(padded, dim):
    moved = jnp.moveaxis(padded, dim, -1)
    half = moved.shape[-1] // 2 - 4
    evens = moved[..., 0::2]
    odds = moved[..., 1::2]
    first_d = odds[..., :half + 3] + ALPHA * (evens[..., :half + 3] + evens[..., 1:half + 4])
    first_s = evens[..., 1:half + 3] + BETA * (first_d[..., :half + 2] + first_d[..., 1:half + 3])
    second_d = first_d[..., 1:half + 2] + GAMMA * (first_s[..., :half + 1] + first_s[..., 1:half + 2])
    second_s = first_s[..., 1:half + 1] + DELTA * (second_d[..., :half] + second_d[..., 1:half + 1])
    lower = jnp.moveaxis(second_s * ZETA, -1, dim)
    upper = jnp.moveaxis(second_d[..., 1:half + 1] / ZETA, -1, dim)
    return jnp.concatenate([lower, upper], axis=0)


def wrap_pad(data, dim):
    widths = [(0, 0)] * data.ndim
    widths[dim] = (4, 4)
    return jnp.pad(data, widths, mode="wrap")


def one_level(data):
    for dim in (2, 3, 1):
        data = lift_padded(wrap_pad(data, dim), dim)
    return data


def reference(density):
    data = density[None]
    results = []
    for level in range(3):
        data = one_level(data)
        results.append(data[1:])
        data = data[0:1]
    return results[0], results[1], results[2], data[0]
```

```python
import functools

import jax
import jax.numpy as jnp
from jax import lax
from jax.experimental import pallas as pl
from jax.experimental.pallas import tpu as pltpu
from jax.sharding import PartitionSpec as P

ALPHA = -1.586134342
BETA = -0.05298011854
GAMMA = 0.8829110762
DELTA = 0.4435068522
ZETA = 1.149604398

MESH = pl.DeviceIdType.MESH
LANES = 128
HALO = 32
F32 = jnp.float32
BF16 = jnp.bfloat16


def boundary_states(get, n):
    s0, last_s = get(0), get(n - 2)
    lead = get(1) + ALPHA * (s0 + get(2))
    trail = get(n - 3) + ALPHA * (get(n - 4) + last_s)
    return s0, s0 + BETA * lead, get(n - 1) + ALPHA * last_s, last_s + BETA * trail


def lift(get, n, from_left, from_right):
    m = n // 2
    s = [get(2 * i) for i in range(m)]
    d = [get(2 * i + 1) for i in range(m)]
    r, q = from_left
    s_next, p = from_right
    d1 = [r + ALPHA * s[0]]
    for i in range(m):
        d1.append(d[i] + ALPHA * (s[i] + (s[i + 1] if i + 1 < m else s_next)))
    s1 = [q + BETA * d1[0]]
    for i in range(m):
        s1.append(s[i] + BETA * (d1[i] + d1[i + 1]))
    s1.append(p + BETA * d1[m])
    d2 = [d1[i] + GAMMA * (s1[i] + s1[i + 1]) for i in range(m + 1)]
    low = [s1[i + 1] + DELTA * (d2[i] + d2[i + 1]) for i in range(m)]
    return low, d2[1:]


def lift_lanes(even, odd):
    width = even.shape[-1]
    after = lambda v: pltpu.roll(v, width - 1, 1)
    before = lambda v: pltpu.roll(v, 1, 1)
    d = odd + ALPHA * (even + after(even))
    s = even + BETA * (before(d) + d)
    d = d + GAMMA * (s + after(s))
    s = s + DELTA * (before(d) + d)
    return s, d


def exact_select(x, choose):
    total = None
    for _ in range(3):
        part = x.astype(BF16)
        x = x - part.astype(F32)
        term = jnp.dot(part, choose, preferred_element_type=F32)
        total = term if total is None else total + term
    return total


def split_matrix(depth):
    k = lax.broadcasted_iota(jnp.int32, (depth, 2 * LANES), 0)
    n = lax.broadcasted_iota(jnp.int32, (depth, 2 * LANES), 1)
    parity = (n >= LANES).astype(jnp.int32)
    n = n - LANES * parity
    if depth == LANES:
        n = jnp.where(n < LANES // 2, n, n - LANES // 2)
    return (k == 2 * n + parity).astype(BF16)


class Level:
    def __init__(self, index, nz, nx, pairs, source, refs, sems, sem_base, peers, chunks):
        self.index, self.nz, self.nx, self.pairs = index, nz, nx, pairs
        self.source = source
        (self.split, self.zs_l, self.zs_r, self.zr_l, self.zr_r, self.xs_l, self.xs_r, self.xr_l, self.xr_r,
         self.cs, self.cr, self.own_x, self.halo_x, self.both, self.staged) = refs
        self.send_sems, self.recv_sems = sems
        self.peers = peers
        self.chunks = chunks
        self.sem_base = sem_base
        self.copies = [self.make_copies(c) for c in range(len(chunks))]

    def make_copies(self, c):
        start, stop = self.chunks[c]
        tiles = pl.ds(2 * start, 2 * (stop - start))
        p = self.peers
        moves = [
            (self.zs_l.at[tiles], self.zr_r.at[tiles], p["z"][0]),
            (self.zs_r.at[tiles], self.zr_l.at[tiles], p["z"][1]),
        ]
        for sx in (0, 1):
            for sz in (0, 1):
                moves.append((self.cs.at[sx, sz, tiles], self.cr.at[1 - sx, 1 - sz, tiles], p["xz"][sx][sz]))
        moves.append((self.xs_l.at[tiles], self.xr_r.at[tiles], p["x"][0]))
        moves.append((self.xs_r.at[tiles], self.xr_l.at[tiles], p["x"][1]))
        return [
            pltpu.make_async_remote_copy(
                src_ref=src, dst_ref=dst,
                send_sem=self.send_sems.at[self.sem_base + 8 * c + i],
                recv_sem=self.recv_sems.at[self.sem_base + 8 * c + i],
                device_id=where, device_id_type=MESH,
            )
            for i, (src, dst, where) in enumerate(moves)
        ]

    def split_pair(self, j):
        if isinstance(j, int) and j == self.pairs:
            x = self.source[2 * self.pairs]
            both = exact_select(x, split_matrix(LANES))
        else:
            x = jnp.concatenate([self.source[2 * j], self.source[2 * j + 1]], axis=1)
            both = exact_select(x, split_matrix(2 * LANES))
        self.split[2 * j] = both[:, :LANES]
        self.split[2 * j + 1] = both[:, LANES:]

    def tile_states(self, t):
        nz, nx = self.nz, self.nx
        states = boundary_states(lambda z: self.split[t, z * nx:(z + 1) * nx, :], nz)
        self.zs_l[t, 0:nx, :] = states[0]
        self.zs_l[t, nx:2 * nx, :] = states[1]
        self.zs_r[t, 0:nx, :] = states[2]
        self.zs_r[t, nx:2 * nx, :] = states[3]
        states = boundary_states(lambda x: self.split[t, pl.ds(x, nz, stride=nx), :], nx)
        self.xs_l[t, 0] = states[0]
        self.xs_l[t, 1] = states[1]
        self.xs_r[t, 0] = states[2]
        self.xs_r[t, 1] = states[3]
        for sz, ref in enumerate((self.zs_l, self.zs_r)):
            states = boundary_states(lambda x: ref[t, pl.ds(x, 2, stride=nx), :], nx)
            for i, state in enumerate(states):
                self.cs[i // 2, sz, t, i % 2] = state

    def prepare(self, c):
        start, stop = self.chunks[c]
        main = min(stop, self.pairs)
        if main - start > 1:
            pl.loop(start, main)(self.split_pair)
        else:
            for j in range(start, main):
                self.split_pair(j)
        if stop > self.pairs:
            self.split_pair(self.pairs)
        pl.loop(2 * start, 2 * stop)(self.tile_states)

    def send(self, c):
        for copy in self.copies[c]:
            copy.start()

    def tile_planes(self, t):
        nz, nx = self.nz, self.nx
        mx = nx // 2
        bands = lift(
            lambda x: self.split[t, pl.ds(x, nz, stride=nx), :], nx,
            (self.xr_l[t, 0], self.xr_l[t, 1]), (self.xr_r[t, 0], self.xr_r[t, 1]),
        )
        for band, lines in enumerate(bands):
            for i, line in enumerate(lines):
                self.own_x[band, t, pl.ds(i, nz, stride=mx), :] = line
        for sz, ref in enumerate((self.zr_l, self.zr_r)):
            bands = lift(
                lambda x: ref[t, pl.ds(x, 2, stride=nx), :], nx,
                (self.cr[0, sz, t, 0], self.cr[0, sz, t, 1]), (self.cr[1, sz, t, 0], self.cr[1, sz, t, 1]),
            )
            for band, lines in enumerate(bands):
                for i, line in enumerate(lines):
                    self.halo_x[band, sz, t, pl.ds(i, 2, stride=mx), :] = line
        for xb in (0, 1):
            bands = lift(
                lambda z: self.own_x[xb, t, z * mx:(z + 1) * mx, :], nz,
                (self.halo_x[xb, 0, t, 0:mx, :], self.halo_x[xb, 0, t, mx:2 * mx, :]),
                (self.halo_x[xb, 1, t, 0:mx, :], self.halo_x[xb, 1, t, mx:2 * mx, :]),
            )
            for zb, lines in enumerate(bands):
                for i, line in enumerate(lines):
                    self.both[2 * zb + xb, t, i * mx:(i + 1) * mx, :] = line

    def receive(self, c):
        for copy in self.copies[c]:
            copy.wait_recv()
        start, stop = self.chunks[c]
        pl.loop(2 * start, 2 * stop)(self.tile_planes)

    def lines(self, band, rows_from, planes, approx):
        zb, xb = band // 2, band % 2
        mx = self.nx // 2
        rows = pl.ds(rows_from * mx, planes * mx)
        even = jnp.concatenate([self.both[band, 2 * j, rows, :] for j in range(self.pairs + 1)], axis=1)
        odd = jnp.concatenate([self.both[band, 2 * j + 1, rows, :] for j in range(self.pairs + 1)], axis=1)
        low, high = lift_lanes(even, odd)
        width = self.pairs * LANES
        low = low * ZETA ** (3 - 2 * (zb + xb))
        high = high[:, :width] * ZETA ** (1 - 2 * (zb + xb))
        if band == 0:
            for j in range(self.pairs + 1):
                approx[j, rows, :] = low[:, j * LANES:(j + 1) * LANES]
        for i in range(planes):
            if band > 0:
                self.staged[4 * zb + xb - 1, rows_from + i] = low[i * mx:(i + 1) * mx, :width]
            self.staged[4 * zb + 2 + xb - 1, rows_from + i] = high[i * mx:(i + 1) * mx]

    def all_lines(self, bands, approx=None):
        planes = self.nz // 2
        step = min(planes, 2)
        for band in bands:
            if planes // step > 1:
                pl.loop(0, planes // step)(lambda k, band=band: self.lines(band, k * step, step, approx))
            else:
                self.lines(band, 0, step, approx)


def buffers(nz, nx, pairs):
    tiles = 2 * (pairs + 1)
    shapes = [(tiles, nz * nx, LANES)]
    shapes += [(tiles, 2 * nx, LANES)] * 4
    shapes += [(tiles, 2, nz, LANES)] * 4
    shapes += [(2, 2, tiles, 2, 2, LANES)] * 2
    shapes += [(2, tiles, nz * nx // 2, LANES), (2, 2, tiles, nx, LANES)]
    shapes += [(4, tiles, nz * nx // 4, LANES)]
    shapes += [(7, nz // 2, nx // 2, pairs * LANES)]
    return [pltpu.VMEM(shape, F32) for shape in shapes]


def kernel(sizes, axes, u_ref, one_ref, two_ref, three_ref, approx_ref, *scratch):
    scratch = list(scratch)
    send_sems, recv_sems, in_sems, out_sems, raw, pack_l, pack_r, halo_l, halo_r, approx_four, approx_five, last = scratch[:12]
    rest = scratch[12:]
    per_level = len(rest) // 3
    gx, gy, gz = axes
    ix, iy, iz = (lax.axis_index(a) for a in ("gx", "gy", "gz"))
    around = lambda i, n: (lax.rem(i + n - 1, n), lax.rem(i + 1, n))
    near_x, near_y, near_z = around(ix, gx), around(iy, gy), around(iz, gz)
    peers = {
        "x": [(x, iy, iz) for x in near_x],
        "y": [(ix, y, iz) for y in near_y],
        "z": [(ix, iy, z) for z in near_z],
        "xz": [[(x, iy, z) for z in near_z] for x in near_x],
    }
    (nz, nx, pairs) = sizes[0]
    tiles = 2 * pairs

    loads = [
        pltpu.make_async_copy(u_ref.at[:, :, pl.ds(t * LANES, LANES)], raw.at[t], in_sems.at[t])
        for t in range(tiles)
    ]
    order = [0, tiles - 1] + list(range(1, tiles - 1))
    for t in order:
        loads[t].start()

    barrier = pltpu.get_barrier_semaphore()
    greeted = peers["x"] + peers["y"] + peers["z"] + peers["xz"][0] + peers["xz"][1]
    for where in greeted:
        pl.semaphore_signal(barrier, inc=1, device_id=where, device_id_type=MESH)

    half = pairs // 2
    levels = []
    base = 2
    for index, (lz, lx, lp) in enumerate(sizes):
        chunks = [(0, half), (half, lp), (lp, lp + 1)] if index == 0 else [(0, lp + 1)]
        source = [raw.reshape(tiles + 1, nz * nx, LANES), approx_four, approx_five][index]
        levels.append(Level(index, lz, lx, lp, source, rest[index * per_level:(index + 1) * per_level],
                            (send_sems, recv_sems), base, peers, chunks))
        base += 8 * len(chunks)
    first, second, third = levels

    groups = LANES // HALO
    part = nz * nx // groups
    lane = lax.broadcasted_iota(jnp.int32, (part, LANES), 1)
    loads[0].wait()
    loads[tiles - 1].wait()
    flat = first.source

    def gather(tile, offset):
        total = None
        for g in range(groups):
            rows = pltpu.roll(flat[tile, g * part:(g + 1) * part, :], (g * HALO - offset) % LANES, 1)
            total = rows if total is None else jnp.where(lane >= g * HALO, rows, total)
        return total

    pack_l[...] = gather(0, 0)
    pack_r[...] = gather(tiles - 1, LANES - HALO)
    for t in range(1, tiles - 1):
        loads[t].wait()
    first.prepare(0)

    pl.semaphore_wait(barrier, len(greeted))
    y_copies = [
        pltpu.make_async_remote_copy(src_ref=src, dst_ref=dst, send_sem=send_sems.at[i], recv_sem=recv_sems.at[i],
                                     device_id=where, device_id_type=MESH)
        for i, (src, dst, where) in enumerate(((pack_l, halo_r, peers["y"][0]), (pack_r, halo_l, peers["y"][1])))
    ]
    for copy in y_copies:
        copy.start()
    first.send(0)
    first.prepare(1)
    first.send(1)
    for copy in y_copies:
        copy.wait_recv()
    for g in range(groups):
        after = pltpu.roll(halo_r[...], (-g * HALO) % LANES, 1)
        before = pltpu.roll(halo_l[...], (LANES - HALO - g * HALO) % LANES, 1)
        flat[tiles, g * part:(g + 1) * part, :] = jnp.where(
            lane < HALO, after, jnp.where(lane >= LANES - HALO, before, 0.0)
        )
    first.prepare(2)
    first.send(2)
    for c in range(3):
        first.receive(c)
    first.all_lines([0], approx_four)

    second.prepare(0)
    second.send(0)
    first.all_lines([1, 2, 3])
    store_one = pltpu.make_async_copy(first.staged, one_ref, out_sems.at[0])
    store_one.start()
    second.receive(0)
    second.all_lines([0], approx_five)

    third.prepare(0)
    third.send(0)
    second.all_lines([1, 2, 3])
    store_two = pltpu.make_async_copy(second.staged, two_ref, out_sems.at[1])
    store_two.start()
    third.receive(0)
    third.all_lines([0, 1, 2, 3], last)
    store_three = pltpu.make_async_copy(third.staged, three_ref, out_sems.at[2])
    store_three.start()
    mz, mx = third.nz // 2, third.nx // 2
    stores = [store_one, store_two, store_three]
    for i in range(mz):
        store = pltpu.make_async_copy(last.at[0, pl.ds(i * mx, mx)], approx_ref.at[i], out_sems.at[3 + i])
        store.start()
        stores.append(store)

    for copy in y_copies:
        copy.wait_send()
    for level in levels:
        for copies in level.copies:
            for copy in copies:
                copy.wait_send()
    for store in stores:
        store.wait()


def solution(mesh):
    axes = tuple(mesh.shape[a] for a in ("gx", "gy", "gz"))

    def on_device(density):
        nz, nx, ny = density.shape
        sizes = [(nz >> i, nx >> i, (ny >> i) // (2 * LANES)) for i in range(3)]
        tiles = ny // LANES
        shapes = [(7, z // 2, x // 2, p * LANES) for z, x, p in sizes]
        shapes.append(shapes[-1][1:])
        n_sems = 2 + 8 * 5
        packed = (nz * nx * HALO // LANES, LANES)
        scratch = [
            pltpu.SemaphoreType.DMA((n_sems,)),
            pltpu.SemaphoreType.DMA((n_sems,)),
            pltpu.SemaphoreType.DMA((tiles,)),
            pltpu.SemaphoreType.DMA((3 + shapes[-1][0],)),
            pltpu.VMEM((tiles + 1, nz, nx, LANES), F32),
        ]
        scratch += [pltpu.VMEM(packed, F32)] * 4
        for z, x, p in sizes:
            scratch.append(pltpu.VMEM((p + 1, z * x // 4, LANES), F32))
        for z, x, p in sizes:
            scratch += buffers(z, x, p)
        return pl.pallas_call(
            functools.partial(kernel, sizes, axes),
            out_shape=[jax.ShapeDtypeStruct(shape, F32) for shape in shapes],
            in_specs=[pl.BlockSpec(memory_space=pl.ANY)],
            out_specs=[pl.BlockSpec(memory_space=pl.ANY)] * 4,
            scratch_shapes=scratch,
            compiler_params=pltpu.CompilerParams(
                collective_id=0, has_side_effects=True, vmem_limit_bytes=40 << 20
            ),
            cost_estimate=pl.CostEstimate(flops=20_000_000, bytes_accessed=2 << 20, transcendentals=0),
        )(density)

    return jax.shard_map(
        on_device,
        mesh=mesh,
        in_specs=(P("gz", "gx", "gy"),),
        out_specs=(
            P(None, "gz", "gx", "gy"),
            P(None, "gz", "gx", "gy"),
            P(None, "gz", "gx", "gy"),
            P("gz", "gx", "gy"),
        ),
        check_vma=False,
    )
```

```python
import functools

import jax
import jax.numpy as jnp
from jax import lax
from jax.experimental import pallas as pl
from jax.experimental.pallas import tpu as pltpu
from jax.sharding import PartitionSpec as P

ALPHA = -1.586134342
BETA = -0.05298011854
GAMMA = 0.8829110762
DELTA = 0.4435068522
ZETA = 1.149604398

MESH = pl.DeviceIdType.MESH
LANES = 128
HALO = 32
F32 = jnp.float32
BF16 = jnp.bfloat16


def boundary_states(get, n):
    s0, last_s = get(0), get(n - 2)
    lead = get(1) + ALPHA * (s0 + get(2))
    trail = get(n - 3) + ALPHA * (get(n - 4) + last_s)
    return s0, s0 + BETA * lead, get(n - 1) + ALPHA * last_s, last_s + BETA * trail


def lift(get, n, from_left, from_right):
    m = n // 2
    s = [get(2 * i) for i in range(m)]
    d = [get(2 * i + 1) for i in range(m)]
    r, q = from_left
    s_next, p = from_right
    d1 = [r + ALPHA * s[0]]
    for i in range(m):
        d1.append(d[i] + ALPHA * (s[i] + (s[i + 1] if i + 1 < m else s_next)))
    s1 = [q + BETA * d1[0]]
    for i in range(m):
        s1.append(s[i] + BETA * (d1[i] + d1[i + 1]))
    s1.append(p + BETA * d1[m])
    d2 = [d1[i] + GAMMA * (s1[i] + s1[i + 1]) for i in range(m + 1)]
    low = [s1[i + 1] + DELTA * (d2[i] + d2[i + 1]) for i in range(m)]
    return low, d2[1:]


def lift_lanes(even, odd):
    width = even.shape[-1]
    after = lambda v: pltpu.roll(v, width - 1, 1)
    before = lambda v: pltpu.roll(v, 1, 1)
    d = odd + ALPHA * (even + after(even))
    s = even + BETA * (before(d) + d)
    d = d + GAMMA * (s + after(s))
    s = s + DELTA * (before(d) + d)
    return s, d


def exact_select(x, choose):
    parts = []
    for _ in range(3):
        parts.append(x.astype(BF16))
        x = x - parts[-1].astype(F32)
    terms = jnp.dot(jnp.concatenate(parts, axis=0), choose, preferred_element_type=F32)
    n = x.shape[0]
    return terms[:n] + terms[n:2 * n] + terms[2 * n:]


def split_matrix(depth):
    k = lax.broadcasted_iota(jnp.int32, (depth, depth), 0)
    n = lax.broadcasted_iota(jnp.int32, (depth, depth), 1)
    return (k == jnp.where(n < depth // 2, 2 * n, 2 * n - depth + 1)).astype(BF16)


class Level:
    def __init__(self, index, nz, nx, pairs, source, refs, sems, sem_base, peers, chunks):
        self.index, self.nz, self.nx, self.pairs = index, nz, nx, pairs
        self.source = source
        (self.split, self.zs, self.zr, self.xs, self.xr, self.cs, self.cr,
         self.own_x, self.halo_x, self.both, self.staged) = refs
        self.send_sems, self.recv_sems = sems
        self.peers = peers
        self.chunks = chunks
        self.sem_base = sem_base
        self.copies = [self.make_copies(c) for c in range(len(chunks))]

    def tile_range(self, c):
        start, stop = self.chunks[c]
        return 2 * start, min(2 * stop, 2 * self.pairs + 1)

    def make_copies(self, c):
        start, stop = self.tile_range(c)
        tiles = pl.ds(start, stop - start)
        p = self.peers
        side = 2 * self.nx
        moves = [
            (self.zs.at[tiles, pl.ds(sz * side, side)], self.zr.at[tiles, pl.ds((1 - sz) * side, side)], p["z"][sz])
            for sz in (0, 1)
        ]
        for sx in (0, 1):
            for sz in (0, 1):
                moves.append((self.cs.at[sx, tiles, :, pl.ds(2 * sz, 2)],
                              self.cr.at[1 - sx, tiles, :, pl.ds(2 - 2 * sz, 2)], p["xz"][sx][sz]))
        for sx in (0, 1):
            moves.append((self.xs.at[sx, tiles], self.xr.at[1 - sx, tiles], p["x"][sx]))
        return [
            pltpu.make_async_remote_copy(
                src_ref=src, dst_ref=dst,
                send_sem=self.send_sems.at[self.sem_base + 8 * c + i],
                recv_sem=self.recv_sems.at[self.sem_base + 8 * c + i],
                device_id=where, device_id_type=MESH,
            )
            for i, (src, dst, where) in enumerate(moves)
        ]

    def split_chunk(self, c):
        start, stop = self.chunks[c]
        main = min(stop, self.pairs)
        rows = self.nz * self.nx
        if start == self.pairs:
            self.split[2 * start] = exact_select(self.source[2 * start], split_matrix(LANES))
            return
        firsts = [self.source[2 * j] for j in range(start, stop)]
        seconds = [self.source[2 * j + 1 if j < main else 2 * j] for j in range(start, stop)]
        x = jnp.concatenate([jnp.concatenate(firsts, axis=0), jnp.concatenate(seconds, axis=0)], axis=1)
        both = exact_select(x, split_matrix(2 * LANES))
        for i, j in enumerate(range(start, stop)):
            even = both[i * rows:(i + 1) * rows, :LANES]
            odd = both[i * rows:(i + 1) * rows, LANES:]
            if j < main:
                self.split[2 * j] = even
                self.split[2 * j + 1] = odd
            else:
                lane = lax.broadcasted_iota(jnp.int32, (rows, LANES), 1)
                self.split[2 * j] = jnp.where(lane < LANES // 2, even, odd)

    def tile_states(self, t):
        nz, nx = self.nz, self.nx
        states = boundary_states(lambda z: self.split[t, z * nx:(z + 1) * nx, :], nz)
        for i, state in enumerate(states):
            self.zs[t, i * nx:(i + 1) * nx, :] = state
        states = boundary_states(lambda x: self.split[t, pl.ds(x, nz, stride=nx), :], nx)
        for i, state in enumerate(states):
            self.xs[i // 2, t, i % 2] = state
        states = boundary_states(lambda x: self.zs[t, pl.ds(x, 4, stride=nx), :], nx)
        for i, state in enumerate(states):
            self.cs[i // 2, t, i % 2] = state

    def prepare(self, c):
        self.split_chunk(c)
        pl.loop(*self.tile_range(c))(self.tile_states)

    def send(self, c):
        for copy in self.copies[c]:
            copy.start()

    def tile_planes(self, t):
        nz, nx = self.nz, self.nx
        mx = nx // 2
        bands = lift(
            lambda x: self.split[t, pl.ds(x, nz, stride=nx), :], nx,
            (self.xr[0, t, 0], self.xr[0, t, 1]), (self.xr[1, t, 0], self.xr[1, t, 1]),
        )
        for band, lines in enumerate(bands):
            for i, line in enumerate(lines):
                self.own_x[band, t, pl.ds(i, nz, stride=mx), :] = line
        bands = lift(
            lambda x: self.zr[t, pl.ds(x, 4, stride=nx), :], nx,
            (self.cr[0, t, 0], self.cr[0, t, 1]), (self.cr[1, t, 0], self.cr[1, t, 1]),
        )
        for band, lines in enumerate(bands):
            for i, line in enumerate(lines):
                self.halo_x[band, t, pl.ds(i, 4, stride=mx), :] = line
        for xb in (0, 1):
            halo = [self.halo_x[xb, t, i * mx:(i + 1) * mx, :] for i in range(4)]
            bands = lift(lambda z: self.own_x[xb, t, z * mx:(z + 1) * mx, :], nz, halo[:2], halo[2:])
            for zb, lines in enumerate(bands):
                for i, line in enumerate(lines):
                    self.both[2 * zb + xb, t, i * mx:(i + 1) * mx, :] = line

    def receive(self, c):
        for copy in self.copies[c]:
            copy.wait_recv()
        pl.loop(*self.tile_range(c))(self.tile_planes)

    def lines(self, band, rows_from, planes, approx):
        zb, xb = band // 2, band % 2
        mx = self.nx // 2
        rows = pl.ds(rows_from * mx, planes * mx)
        ends = self.both[band, 2 * self.pairs, rows, :]
        turned = pltpu.roll(ends, LANES // 2, 1)
        near = lax.broadcasted_iota(jnp.int32, ends.shape, 1) < LANES // 2
        evens = [self.both[band, 2 * j, rows, :] for j in range(self.pairs)]
        odds = [self.both[band, 2 * j + 1, rows, :] for j in range(self.pairs)]
        even = jnp.concatenate(evens + [jnp.where(near, ends, turned)], axis=1)
        odd = jnp.concatenate(odds + [jnp.where(near, turned, ends)], axis=1)
        low, high = lift_lanes(even, odd)
        width = self.pairs * LANES
        low = low * ZETA ** (3 - 2 * (zb + xb))
        high = high[:, :width] * ZETA ** (1 - 2 * (zb + xb))
        if band == 0:
            for j in range(self.pairs + 1):
                approx[j, rows, :] = low[:, j * LANES:(j + 1) * LANES]
        for i in range(planes):
            if band > 0:
                self.staged[4 * zb + xb - 1, rows_from + i] = low[i * mx:(i + 1) * mx, :width]
            self.staged[4 * zb + 2 + xb - 1, rows_from + i] = high[i * mx:(i + 1) * mx]

    def all_lines(self, bands, approx=None):
        planes = self.nz // 2
        step = min(planes, 2)
        for band in bands:
            if planes // step > 1:
                pl.loop(0, planes // step)(lambda k, band=band: self.lines(band, k * step, step, approx))
            else:
                self.lines(band, 0, step, approx)


def buffers(nz, nx, pairs):
    tiles = 2 * pairs + 1
    shapes = [(tiles, nz * nx, LANES)]
    shapes += [(tiles, 4 * nx, LANES)] * 2
    shapes += [(2, tiles, 2, nz, LANES)] * 2
    shapes += [(2, tiles, 2, 4, LANES)] * 2
    shapes += [(2, tiles, nz * nx // 2, LANES), (2, tiles, 2 * nx, LANES)]
    shapes += [(4, tiles, nz * nx // 4, LANES)]
    shapes += [(7, nz // 2, nx // 2, pairs * LANES)]
    return [pltpu.VMEM(shape, F32) for shape in shapes]


def hand_out(*refs):
    sems = refs[-1]
    n = (len(refs) - 1) // 2
    copies = [pltpu.make_async_copy(refs[i], refs[n + i], sems.at[i]) for i in range(n)]
    for copy in copies:
        copy.start()
    for copy in copies:
        copy.wait()


def kernel(sizes, axes, u_ref, one_ref, two_ref, three_ref, approx_ref, *scratch):
    scratch = list(scratch)
    send_sems, recv_sems, in_sems, out_sems, raw, pack_l, pack_r, halo_l, halo_r, approx_four, approx_five, last = scratch[:12]
    rest = scratch[12:]
    per_level = len(rest) // 3
    gx, gy, gz = axes
    ix, iy, iz = (lax.axis_index(a) for a in ("gx", "gy", "gz"))
    around = lambda i, n: (lax.rem(i + n - 1, n), lax.rem(i + 1, n))
    near_x, near_y, near_z = around(ix, gx), around(iy, gy), around(iz, gz)
    peers = {
        "x": [(x, iy, iz) for x in near_x],
        "y": [(ix, y, iz) for y in near_y],
        "z": [(ix, iy, z) for z in near_z],
        "xz": [[(x, iy, z) for z in near_z] for x in near_x],
    }
    (nz, nx, pairs) = sizes[0]
    tiles = 2 * pairs

    loads = [
        pltpu.make_async_copy(u_ref.at[:, :, pl.ds(t * LANES, LANES)], raw.at[t], in_sems.at[t])
        for t in range(tiles)
    ]
    order = [0, tiles - 1] + list(range(1, tiles - 1))
    for t in order:
        loads[t].start()

    barrier = pltpu.get_barrier_semaphore()
    greeted = peers["x"] + peers["y"] + peers["z"] + peers["xz"][0] + peers["xz"][1]
    for where in greeted:
        pl.semaphore_signal(barrier, inc=1, device_id=where, device_id_type=MESH)

    half = pairs // 2
    levels = []
    base = 2
    for index, (lz, lx, lp) in enumerate(sizes):
        chunks = [(0, half), (half, lp), (lp, lp + 1)] if index == 0 else [(0, lp + 1)]
        source = [raw.reshape(tiles + 1, nz * nx, LANES), approx_four, approx_five][index]
        levels.append(Level(index, lz, lx, lp, source, rest[index * per_level:(index + 1) * per_level],
                            (send_sems, recv_sems), base, peers, chunks))
        base += 8 * len(chunks)
    first, second, third = levels

    groups = LANES // HALO
    part = nz * nx // groups
    lane = lax.broadcasted_iota(jnp.int32, (part, LANES), 1)
    loads[0].wait()
    loads[tiles - 1].wait()
    flat = first.source

    def gather(tile, offset):
        total = None
        for g in range(groups):
            rows = pltpu.roll(flat[tile, g * part:(g + 1) * part, :], (g * HALO - offset) % LANES, 1)
            total = rows if total is None else jnp.where(lane >= g * HALO, rows, total)
        return total

    pack_l[...] = gather(0, 0)
    pack_r[...] = gather(tiles - 1, LANES - HALO)
    for t in range(1, tiles - 1):
        loads[t].wait()
    first.prepare(0)

    pl.semaphore_wait(barrier, len(greeted))
    y_copies = [
        pltpu.make_async_remote_copy(src_ref=src, dst_ref=dst, send_sem=send_sems.at[i], recv_sem=recv_sems.at[i],
                                     device_id=where, device_id_type=MESH)
        for i, (src, dst, where) in enumerate(((pack_l, halo_r, peers["y"][0]), (pack_r, halo_l, peers["y"][1])))
    ]
    for copy in y_copies:
        copy.start()
    first.send(0)
    first.prepare(1)
    first.send(1)
    for copy in y_copies:
        copy.wait_recv()
    for g in range(groups):
        after = pltpu.roll(halo_r[...], (-g * HALO) % LANES, 1)
        before = pltpu.roll(halo_l[...], (LANES - HALO - g * HALO) % LANES, 1)
        flat[tiles, g * part:(g + 1) * part, :] = jnp.where(
            lane < HALO, after, jnp.where(lane >= LANES - HALO, before, 0.0)
        )
    first.prepare(2)
    first.send(2)
    for c in range(3):
        first.receive(c)
    first.all_lines([0], approx_four)

    second.prepare(0)
    second.send(0)
    first.all_lines([1, 2, 3])
    store_one = pltpu.make_async_copy(first.staged, one_ref, out_sems.at[0])
    store_one.start()
    second.receive(0)
    second.all_lines([0], approx_five)

    third.prepare(0)
    third.send(0)
    second.all_lines([1, 2, 3])
    store_two = pltpu.make_async_copy(second.staged, two_ref, out_sems.at[1])
    store_two.start()
    third.receive(0)
    third.all_lines([0, 1, 2, 3], last)
    store_three = pltpu.make_async_copy(third.staged, three_ref, out_sems.at[2])
    store_three.start()
    mz, mx = third.nz // 2, third.nx // 2
    stores = [store_one, store_two, store_three]
    for i in range(mz):
        store = pltpu.make_async_copy(last.at[0, pl.ds(i * mx, mx)], approx_ref.at[i], out_sems.at[3 + i])
        store.start()
        stores.append(store)

    for copy in y_copies:
        copy.wait_send()
    for level in levels:
        for copies in level.copies:
            for copy in copies:
                copy.wait_send()
    for store in stores:
        store.wait()


def solution(mesh):
    axes = tuple(mesh.shape[a] for a in ("gx", "gy", "gz"))

    def on_device(density):
        nz, nx, ny = density.shape
        sizes = [(nz >> i, nx >> i, (ny >> i) // (2 * LANES)) for i in range(3)]
        tiles = ny // LANES
        shapes = [(7, z // 2, x // 2, p * LANES) for z, x, p in sizes]
        shapes.append(shapes[-1][1:])
        n_sems = 2 + 8 * 5
        packed = (nz * nx * HALO // LANES, LANES)
        scratch = [
            pltpu.SemaphoreType.DMA((n_sems,)),
            pltpu.SemaphoreType.DMA((n_sems,)),
            pltpu.SemaphoreType.DMA((tiles,)),
            pltpu.SemaphoreType.DMA((3 + shapes[-1][0],)),
            pltpu.VMEM((tiles + 1, nz, nx, LANES), F32),
        ]
        scratch += [pltpu.VMEM(packed, F32)] * 4
        for z, x, p in sizes:
            scratch.append(pltpu.VMEM((p + 1, z * x // 4, LANES), F32))
        for z, x, p in sizes:
            scratch += buffers(z, x, p)
        outs = [jax.ShapeDtypeStruct(shape, F32) for shape in shapes]
        results = pl.pallas_call(
            functools.partial(kernel, sizes, axes),
            out_shape=outs,
            in_specs=[pl.BlockSpec(memory_space=pltpu.HBM)],
            out_specs=[pl.BlockSpec(memory_space=pl.ANY)] * 4,
            scratch_shapes=scratch,
            compiler_params=pltpu.CompilerParams(
                collective_id=0, has_side_effects=True, vmem_limit_bytes=40 << 20
            ),
            cost_estimate=pl.CostEstimate(flops=20_000_000, bytes_accessed=2 << 20, transcendentals=0),
        )(density)
        return pl.pallas_call(
            hand_out,
            out_shape=outs,
            in_specs=[pl.BlockSpec(memory_space=pl.ANY)] * 4,
            out_specs=[pl.BlockSpec(memory_space=pltpu.HBM)] * 4,
            scratch_shapes=[pltpu.SemaphoreType.DMA((4,))],
            cost_estimate=pl.CostEstimate(flops=0, bytes_accessed=2 << 20, transcendentals=0),
        )(*results)

    return jax.shard_map(
        on_device,
        mesh=mesh,
        in_specs=(P("gz", "gx", "gy"),),
        out_specs=(
            P(None, "gz", "gx", "gy"),
            P(None, "gz", "gx", "gy"),
            P(None, "gz", "gx", "gy"),
            P("gz", "gx", "gy"),
        ),
        check_vma=False,
    )
```

```python
import functools

import jax
import jax.numpy as jnp
from jax import lax
from jax.experimental import pallas as pl
from jax.experimental.pallas import tpu as pltpu
from jax.sharding import PartitionSpec as P

ALPHA = -1.586134342
BETA = -0.05298011854
GAMMA = 0.8829110762
DELTA = 0.4435068522
ZETA = 1.149604398

MESH = pl.DeviceIdType.MESH
LANES = 128
HALO = 32
F32 = jnp.float32
BF16 = jnp.bfloat16


def boundary_states(get, n):
    s0, last_s = get(0), get(n - 2)
    lead = get(1) + ALPHA * (s0 + get(2))
    trail = get(n - 3) + ALPHA * (get(n - 4) + last_s)
    return s0, s0 + BETA * lead, get(n - 1) + ALPHA * last_s, last_s + BETA * trail


def lift(get, n, from_left, from_right):
    m = n // 2
    s = [get(2 * i) for i in range(m)]
    d = [get(2 * i + 1) for i in range(m)]
    r, q = from_left
    s_next, p = from_right
    d1 = [r + ALPHA * s[0]]
    for i in range(m):
        d1.append(d[i] + ALPHA * (s[i] + (s[i + 1] if i + 1 < m else s_next)))
    s1 = [q + BETA * d1[0]]
    for i in range(m):
        s1.append(s[i] + BETA * (d1[i] + d1[i + 1]))
    s1.append(p + BETA * d1[m])
    d2 = [d1[i] + GAMMA * (s1[i] + s1[i + 1]) for i in range(m + 1)]
    low = [s1[i + 1] + DELTA * (d2[i] + d2[i + 1]) for i in range(m)]
    return low, d2[1:]


def lift_lanes(even, odd):
    width = even.shape[-1]
    after = lambda v: pltpu.roll(v, width - 1, 1)
    before = lambda v: pltpu.roll(v, 1, 1)
    d = odd + ALPHA * (even + after(even))
    s = even + BETA * (before(d) + d)
    d = d + GAMMA * (s + after(s))
    s = s + DELTA * (before(d) + d)
    return s, d


def exact_select(x, choose):
    parts = []
    for _ in range(3):
        parts.append(x.astype(BF16))
        x = x - parts[-1].astype(F32)
    terms = jnp.dot(jnp.concatenate(parts, axis=0), choose, preferred_element_type=F32)
    n = x.shape[0]
    return terms[:n] + terms[n:2 * n] + terms[2 * n:]


def split_matrix(depth):
    k = lax.broadcasted_iota(jnp.int32, (depth, depth), 0)
    n = lax.broadcasted_iota(jnp.int32, (depth, depth), 1)
    return (k == jnp.where(n < depth // 2, 2 * n, 2 * n - depth + 1)).astype(BF16)


class Level:
    def __init__(self, index, nz, nx, pairs, source, refs, details, sems, sem_base, peers, chunks):
        self.index, self.nz, self.nx, self.pairs = index, nz, nx, pairs
        self.source = source
        (self.split, self.zs, self.zr, self.xs, self.xr, self.cs, self.cr,
         self.own_x, self.halo_x, self.both) = refs
        self.details = details
        self.send_sems, self.recv_sems = sems
        self.peers = peers
        self.chunks = chunks
        self.sem_base = sem_base
        self.copies = [self.make_copies(c) for c in range(len(chunks))]

    def tile_range(self, c):
        start, stop = self.chunks[c]
        return 2 * start, min(2 * stop, 2 * self.pairs + 1)

    def make_copies(self, c):
        start, stop = self.tile_range(c)
        tiles = pl.ds(start, stop - start)
        p = self.peers
        side = 2 * self.nx
        moves = [
            (self.zs.at[tiles, pl.ds(sz * side, side)], self.zr.at[tiles, pl.ds((1 - sz) * side, side)], p["z"][sz])
            for sz in (0, 1)
        ]
        for sx in (0, 1):
            for sz in (0, 1):
                moves.append((self.cs.at[sx, tiles, :, pl.ds(2 * sz, 2)],
                              self.cr.at[1 - sx, tiles, :, pl.ds(2 - 2 * sz, 2)], p["xz"][sx][sz]))
        for sx in (0, 1):
            moves.append((self.xs.at[sx, tiles], self.xr.at[1 - sx, tiles], p["x"][sx]))
        return [
            pltpu.make_async_remote_copy(
                src_ref=src, dst_ref=dst,
                send_sem=self.send_sems.at[self.sem_base + 8 * c + i],
                recv_sem=self.recv_sems.at[self.sem_base + 8 * c + i],
                device_id=where, device_id_type=MESH,
            )
            for i, (src, dst, where) in enumerate(moves)
        ]

    def split_chunk(self, c):
        start, stop = self.chunks[c]
        main = min(stop, self.pairs)
        rows = self.nz * self.nx
        if start == self.pairs:
            self.split[2 * start] = exact_select(self.source[2 * start], split_matrix(LANES))
            return
        firsts = [self.source[2 * j] for j in range(start, stop)]
        seconds = [self.source[2 * j + 1 if j < main else 2 * j] for j in range(start, stop)]
        x = jnp.concatenate([jnp.concatenate(firsts, axis=0), jnp.concatenate(seconds, axis=0)], axis=1)
        both = exact_select(x, split_matrix(2 * LANES))
        for i, j in enumerate(range(start, stop)):
            even = both[i * rows:(i + 1) * rows, :LANES]
            odd = both[i * rows:(i + 1) * rows, LANES:]
            if j < main:
                self.split[2 * j] = even
                self.split[2 * j + 1] = odd
            else:
                lane = lax.broadcasted_iota(jnp.int32, (rows, LANES), 1)
                self.split[2 * j] = jnp.where(lane < LANES // 2, even, odd)

    def tile_states(self, t):
        nz, nx = self.nz, self.nx
        states = boundary_states(lambda z: self.split[t, z * nx:(z + 1) * nx, :], nz)
        for i, state in enumerate(states):
            self.zs[t, i * nx:(i + 1) * nx, :] = state
        states = boundary_states(lambda x: self.split[t, pl.ds(x, nz, stride=nx), :], nx)
        for i, state in enumerate(states):
            self.xs[i // 2, t, i % 2] = state
        states = boundary_states(lambda x: self.zs[t, pl.ds(x, 4, stride=nx), :], nx)
        for i, state in enumerate(states):
            self.cs[i // 2, t, i % 2] = state

    def prepare(self, c):
        self.split_chunk(c)
        pl.loop(*self.tile_range(c))(self.tile_states)

    def send(self, c):
        for copy in self.copies[c]:
            copy.start()

    def tile_planes(self, t):
        nz, nx = self.nz, self.nx
        mx = nx // 2
        bands = lift(
            lambda x: self.split[t, pl.ds(x, nz, stride=nx), :], nx,
            (self.xr[0, t, 0], self.xr[0, t, 1]), (self.xr[1, t, 0], self.xr[1, t, 1]),
        )
        for band, lines in enumerate(bands):
            for i, line in enumerate(lines):
                self.own_x[band, t, pl.ds(i, nz, stride=mx), :] = line
        bands = lift(
            lambda x: self.zr[t, pl.ds(x, 4, stride=nx), :], nx,
            (self.cr[0, t, 0], self.cr[0, t, 1]), (self.cr[1, t, 0], self.cr[1, t, 1]),
        )
        for band, lines in enumerate(bands):
            for i, line in enumerate(lines):
                self.halo_x[band, t, pl.ds(i, 4, stride=mx), :] = line
        for xb in (0, 1):
            halo = [self.halo_x[xb, t, i * mx:(i + 1) * mx, :] for i in range(4)]
            bands = lift(lambda z: self.own_x[xb, t, z * mx:(z + 1) * mx, :], nz, halo[:2], halo[2:])
            for zb, lines in enumerate(bands):
                for i, line in enumerate(lines):
                    self.both[2 * zb + xb, t, i * mx:(i + 1) * mx, :] = line

    def receive(self, c):
        for copy in self.copies[c]:
            copy.wait_recv()
        pl.loop(*self.tile_range(c))(self.tile_planes)

    def lines(self, band, rows_from, planes, approx):
        zb, xb = band // 2, band % 2
        mx = self.nx // 2
        rows = pl.ds(rows_from * mx, planes * mx)
        ends = self.both[band, 2 * self.pairs, rows, :]
        turned = pltpu.roll(ends, LANES // 2, 1)
        near = lax.broadcasted_iota(jnp.int32, ends.shape, 1) < LANES // 2
        evens = [self.both[band, 2 * j, rows, :] for j in range(self.pairs)]
        odds = [self.both[band, 2 * j + 1, rows, :] for j in range(self.pairs)]
        even = jnp.concatenate(evens + [jnp.where(near, ends, turned)], axis=1)
        odd = jnp.concatenate(odds + [jnp.where(near, turned, ends)], axis=1)
        low, high = lift_lanes(even, odd)
        width = self.pairs * LANES
        low = low * ZETA ** (3 - 2 * (zb + xb))
        high = high[:, :width] * ZETA ** (1 - 2 * (zb + xb))
        if band == 0 and self.index < 2:
            for j in range(self.pairs + 1):
                approx[j, rows, :] = low[:, j * LANES:(j + 1) * LANES]
        for i in range(planes):
            if band == 0 and self.index == 2:
                approx[rows_from + i] = low[i * mx:(i + 1) * mx, :width]
            if band > 0:
                self.details[4 * zb + xb - 1, rows_from + i] = low[i * mx:(i + 1) * mx, :width]
            self.details[4 * zb + 2 + xb - 1, rows_from + i] = high[i * mx:(i + 1) * mx]

    def all_lines(self, bands, approx=None):
        planes = self.nz // 2
        step = min(planes, 2)
        for band in bands:
            if planes // step > 1:
                pl.loop(0, planes // step)(lambda k, band=band: self.lines(band, k * step, step, approx))
            else:
                self.lines(band, 0, step, approx)


def buffers(nz, nx, pairs):
    tiles = 2 * pairs + 1
    shapes = [(tiles, nz * nx, LANES)]
    shapes += [(tiles, 4 * nx, LANES)] * 2
    shapes += [(2, tiles, 2, nz, LANES)] * 2
    shapes += [(2, tiles, 2, 4, LANES)] * 2
    shapes += [(2, tiles, nz * nx // 2, LANES), (2, tiles, 2 * nx, LANES)]
    shapes += [(4, tiles, nz * nx // 4, LANES)]
    return [pltpu.VMEM(shape, F32) for shape in shapes]


def hand_out(*refs):
    sems = refs[-1]
    n = (len(refs) - 1) // 2
    copies = [pltpu.make_async_copy(refs[i], refs[n + i], sems.at[i]) for i in range(n)]
    for copy in copies:
        copy.start()
    for copy in copies:
        copy.wait()


def kernel(sizes, axes, u_ref, one_ref, two_ref, three_ref, approx_ref, *scratch):
    scratch = list(scratch)
    send_sems, recv_sems, in_sems, raw, pack_l, pack_r, halo_l, halo_r, approx_four, approx_five = scratch[:10]
    rest = scratch[10:]
    per_level = len(rest) // 3
    gx, gy, gz = axes
    ix, iy, iz = (lax.axis_index(a) for a in ("gx", "gy", "gz"))
    around = lambda i, n: (lax.rem(i + n - 1, n), lax.rem(i + 1, n))
    near_x, near_y, near_z = around(ix, gx), around(iy, gy), around(iz, gz)
    peers = {
        "x": [(x, iy, iz) for x in near_x],
        "y": [(ix, y, iz) for y in near_y],
        "z": [(ix, iy, z) for z in near_z],
        "xz": [[(x, iy, z) for z in near_z] for x in near_x],
    }
    (nz, nx, pairs) = sizes[0]
    tiles = 2 * pairs

    loads = [
        pltpu.make_async_copy(u_ref.at[:, :, pl.ds(t * LANES, LANES)], raw.at[t], in_sems.at[t])
        for t in range(tiles)
    ]
    order = [0, tiles - 1] + list(range(1, tiles - 1))
    for t in order:
        loads[t].start()

    barrier = pltpu.get_barrier_semaphore()
    greeted = peers["x"] + peers["y"] + peers["z"] + peers["xz"][0] + peers["xz"][1]
    for where in greeted:
        pl.semaphore_signal(barrier, inc=1, device_id=where, device_id_type=MESH)

    half = pairs // 2
    levels = []
    base = 2
    for index, (lz, lx, lp) in enumerate(sizes):
        chunks = [(0, half), (half, lp), (lp, lp + 1)] if index == 0 else [(0, lp + 1)]
        source = [raw.reshape(tiles + 1, nz * nx, LANES), approx_four, approx_five][index]
        levels.append(Level(index, lz, lx, lp, source, rest[index * per_level:(index + 1) * per_level],
                            (one_ref, two_ref, three_ref)[index],
                            (send_sems, recv_sems), base, peers, chunks))
        base += 8 * len(chunks)
    first, second, third = levels

    groups = LANES // HALO
    part = nz * nx // groups
    lane = lax.broadcasted_iota(jnp.int32, (part, LANES), 1)
    loads[0].wait()
    loads[tiles - 1].wait()
    flat = first.source

    def gather(tile, offset):
        total = None
        for g in range(groups):
            rows = pltpu.roll(flat[tile, g * part:(g + 1) * part, :], (g * HALO - offset) % LANES, 1)
            total = rows if total is None else jnp.where(lane >= g * HALO, rows, total)
        return total

    pack_l[...] = gather(0, 0)
    pack_r[...] = gather(tiles - 1, LANES - HALO)
    for t in range(1, tiles - 1):
        loads[t].wait()
    first.prepare(0)

    pl.semaphore_wait(barrier, len(greeted))
    y_copies = [
        pltpu.make_async_remote_copy(src_ref=src, dst_ref=dst, send_sem=send_sems.at[i], recv_sem=recv_sems.at[i],
                                     device_id=where, device_id_type=MESH)
        for i, (src, dst, where) in enumerate(((pack_l, halo_r, peers["y"][0]), (pack_r, halo_l, peers["y"][1])))
    ]
    for copy in y_copies:
        copy.start()
    first.send(0)
    first.prepare(1)
    first.send(1)
    for copy in y_copies:
        copy.wait_recv()
    for g in range(groups):
        after = pltpu.roll(halo_r[...], (-g * HALO) % LANES, 1)
        before = pltpu.roll(halo_l[...], (LANES - HALO - g * HALO) % LANES, 1)
        flat[tiles, g * part:(g + 1) * part, :] = jnp.where(
            lane < HALO, after, jnp.where(lane >= LANES - HALO, before, 0.0)
        )
    first.prepare(2)
    first.send(2)
    for c in range(3):
        first.receive(c)
    first.all_lines([0], approx_four)

    second.prepare(0)
    second.send(0)
    first.all_lines([1, 2, 3])
    second.receive(0)
    second.all_lines([0], approx_five)

    third.prepare(0)
    third.send(0)
    second.all_lines([1, 2, 3])
    third.receive(0)
    third.all_lines([0, 1, 2, 3], approx_ref)

    for copy in y_copies:
        copy.wait_send()
    for level in levels:
        for copies in level.copies:
            for copy in copies:
                copy.wait_send()


def solution(mesh):
    axes = tuple(mesh.shape[a] for a in ("gx", "gy", "gz"))

    def on_device(density):
        nz, nx, ny = density.shape
        sizes = [(nz >> i, nx >> i, (ny >> i) // (2 * LANES)) for i in range(3)]
        tiles = ny // LANES
        shapes = [(7, z // 2, x // 2, p * LANES) for z, x, p in sizes]
        shapes.append(shapes[-1][1:])
        n_sems = 2 + 8 * 5
        packed = (nz * nx * HALO // LANES, LANES)
        scratch = [
            pltpu.SemaphoreType.DMA((n_sems,)),
            pltpu.SemaphoreType.DMA((n_sems,)),
            pltpu.SemaphoreType.DMA((tiles,)),
            pltpu.VMEM((tiles + 1, nz, nx, LANES), F32),
        ]
        scratch += [pltpu.VMEM(packed, F32)] * 4
        for z, x, p in sizes[:2]:
            scratch.append(pltpu.VMEM((p + 1, z * x // 4, LANES), F32))
        for z, x, p in sizes:
            scratch += buffers(z, x, p)
        outs = [jax.ShapeDtypeStruct(shape, F32) for shape in shapes]
        results = pl.pallas_call(
            functools.partial(kernel, sizes, axes),
            out_shape=[pltpu.VMEM(shape, F32) for shape in shapes],
            in_specs=[pl.BlockSpec(memory_space=pltpu.HBM)],
            out_specs=[pl.BlockSpec(memory_space=pltpu.VMEM)] * 4,
            scratch_shapes=scratch,
            compiler_params=pltpu.CompilerParams(
                collective_id=0, has_side_effects=True, vmem_limit_bytes=59 << 20
            ),
            cost_estimate=pl.CostEstimate(flops=20_000_000, bytes_accessed=2 << 20, transcendentals=0),
        )(density)
        return pl.pallas_call(
            hand_out,
            out_shape=outs,
            in_specs=[pl.BlockSpec(memory_space=pltpu.VMEM)] * 4,
            out_specs=[pl.BlockSpec(memory_space=pltpu.HBM)] * 4,
            scratch_shapes=[pltpu.SemaphoreType.DMA((4,))],
            compiler_params=pltpu.CompilerParams(vmem_limit_bytes=1 << 20),
            cost_estimate=pl.CostEstimate(flops=0, bytes_accessed=2 << 20, transcendentals=0),
        )(*results)

    return jax.shard_map(
        on_device,
        mesh=mesh,
        in_specs=(P("gz", "gx", "gy"),),
        out_specs=(
            P(None, "gz", "gx", "gy"),
            P(None, "gz", "gx", "gy"),
            P(None, "gz", "gx", "gy"),
            P("gz", "gx", "gy"),
        ),
        check_vma=False,
    )
```

```python
import functools

import jax
import jax.numpy as jnp
from jax import lax
from jax.experimental import pallas as pl
from jax.experimental.pallas import tpu as pltpu
from jax.sharding import PartitionSpec as P

ALPHA = -1.586134342
BETA = -0.05298011854
GAMMA = 0.8829110762
DELTA = 0.4435068522
ZETA = 1.149604398

MESH = pl.DeviceIdType.MESH
LANES = 128
HALO = 32
F32 = jnp.float32
BF16 = jnp.bfloat16


def boundary_states(get, n):
    s0, last_s = get(0), get(n - 2)
    lead = get(1) + ALPHA * (s0 + get(2))
    trail = get(n - 3) + ALPHA * (get(n - 4) + last_s)
    return s0, s0 + BETA * lead, get(n - 1) + ALPHA * last_s, last_s + BETA * trail


def lift(get, n, from_left, from_right):
    m = n // 2
    s = [get(2 * i) for i in range(m)]
    d = [get(2 * i + 1) for i in range(m)]
    r, q = from_left
    s_next, p = from_right
    d1 = [r + ALPHA * s[0]]
    for i in range(m):
        d1.append(d[i] + ALPHA * (s[i] + (s[i + 1] if i + 1 < m else s_next)))
    s1 = [q + BETA * d1[0]]
    for i in range(m):
        s1.append(s[i] + BETA * (d1[i] + d1[i + 1]))
    s1.append(p + BETA * d1[m])
    d2 = [d1[i] + GAMMA * (s1[i] + s1[i + 1]) for i in range(m + 1)]
    low = [s1[i + 1] + DELTA * (d2[i] + d2[i + 1]) for i in range(m)]
    return low, d2[1:]


def lift_lanes(even, odd):
    width = even.shape[-1]
    after = lambda v: pltpu.roll(v, width - 1, 1)
    before = lambda v: pltpu.roll(v, 1, 1)
    d = odd + ALPHA * (even + after(even))
    s = even + BETA * (before(d) + d)
    d = d + GAMMA * (s + after(s))
    s = s + DELTA * (before(d) + d)
    return s, d


def circle(tiles):
    ends = tiles[-1]
    turned = pltpu.roll(ends, LANES // 2, 1)
    near = lax.broadcasted_iota(jnp.int32, ends.shape, 1) < LANES // 2
    even = jnp.concatenate(tiles[0:-1:2] + [jnp.where(near, ends, turned)], axis=1)
    odd = jnp.concatenate(tiles[1:-1:2] + [jnp.where(near, turned, ends)], axis=1)
    return even, odd


def exact_select(x, choose):
    parts = []
    for _ in range(3):
        parts.append(x.astype(BF16))
        x = x - parts[-1].astype(F32)
    terms = jnp.dot(jnp.concatenate(parts, axis=0), choose, preferred_element_type=F32)
    n = x.shape[0]
    return terms[:n] + terms[n:2 * n] + terms[2 * n:]


def split_matrix(depth):
    k = lax.broadcasted_iota(jnp.int32, (depth, depth), 0)
    n = lax.broadcasted_iota(jnp.int32, (depth, depth), 1)
    return (k == jnp.where(n < depth // 2, 2 * n, 2 * n - depth + 1)).astype(BF16)


class Level:
    def __init__(self, index, nz, nx, pairs, source, refs, details, sems, sem_base, peers, chunks):
        self.index, self.nz, self.nx, self.pairs = index, nz, nx, pairs
        self.source = source
        (self.split, self.zs, self.zr, self.xs, self.xr, self.cs, self.cr,
         self.own_x, self.halo_x, self.both) = refs
        self.details = details
        self.send_sems, self.recv_sems = sems
        self.peers = peers
        self.chunks = chunks
        self.sem_base = sem_base
        self.copies = [self.make_copies(c) for c in range(len(chunks))]

    def tile_range(self, c):
        start, stop = self.chunks[c]
        return 2 * start, min(2 * stop, 2 * self.pairs + 1)

    def make_copies(self, c):
        start, stop = self.tile_range(c)
        tiles = pl.ds(start, stop - start)
        p = self.peers
        side = 2 * self.nx
        moves = [
            (self.zs.at[tiles, pl.ds(sz * side, side)], self.zr.at[tiles, pl.ds((1 - sz) * side, side)], p["z"][sz])
            for sz in (0, 1)
        ]
        for sx in (0, 1):
            for sz in (0, 1):
                moves.append((self.cs.at[sx, tiles, :, pl.ds(2 * sz, 2)],
                              self.cr.at[1 - sx, tiles, :, pl.ds(2 - 2 * sz, 2)], p["xz"][sx][sz]))
        for sx in (0, 1):
            moves.append((self.xs.at[sx, tiles], self.xr.at[1 - sx, tiles], p["x"][sx]))
        return [
            pltpu.make_async_remote_copy(
                src_ref=src, dst_ref=dst,
                send_sem=self.send_sems.at[self.sem_base + 8 * c + i],
                recv_sem=self.recv_sems.at[self.sem_base + 8 * c + i],
                device_id=where, device_id_type=MESH,
            )
            for i, (src, dst, where) in enumerate(moves)
        ]

    def split_chunk(self, c):
        start, stop = self.chunks[c]
        main = min(stop, self.pairs)
        rows = self.nz * self.nx
        if start == self.pairs:
            self.split[2 * start] = exact_select(self.source[2 * start], split_matrix(LANES))
            return
        firsts = [self.source[2 * j] for j in range(start, stop)]
        seconds = [self.source[2 * j + 1 if j < main else 2 * j] for j in range(start, stop)]
        x = jnp.concatenate([jnp.concatenate(firsts, axis=0), jnp.concatenate(seconds, axis=0)], axis=1)
        both = exact_select(x, split_matrix(2 * LANES))
        for i, j in enumerate(range(start, stop)):
            even = both[i * rows:(i + 1) * rows, :LANES]
            odd = both[i * rows:(i + 1) * rows, LANES:]
            if j < main:
                self.split[2 * j] = even
                self.split[2 * j + 1] = odd
            else:
                lane = lax.broadcasted_iota(jnp.int32, (rows, LANES), 1)
                self.split[2 * j] = jnp.where(lane < LANES // 2, even, odd)

    def tile_states(self, t):
        nz, nx = self.nz, self.nx
        states = boundary_states(lambda z: self.split[t, z * nx:(z + 1) * nx, :], nz)
        for i, state in enumerate(states):
            self.zs[t, i * nx:(i + 1) * nx, :] = state
        states = boundary_states(lambda x: self.split[t, pl.ds(x, nz, stride=nx), :], nx)
        for i, state in enumerate(states):
            self.xs[i // 2, t, i % 2] = state
        states = boundary_states(lambda x: self.zs[t, pl.ds(x, 4, stride=nx), :], nx)
        for i, state in enumerate(states):
            self.cs[i // 2, t, i % 2] = state

    def prepare(self, c):
        self.split_chunk(c)
        pl.loop(*self.tile_range(c))(self.tile_states)

    def send(self, c):
        for copy in self.copies[c]:
            copy.start()

    def tile_planes(self, t):
        nz, nx = self.nz, self.nx
        mx = nx // 2
        bands = lift(
            lambda x: self.split[t, pl.ds(x, nz, stride=nx), :], nx,
            (self.xr[0, t, 0], self.xr[0, t, 1]), (self.xr[1, t, 0], self.xr[1, t, 1]),
        )
        for band, lines in enumerate(bands):
            for i, line in enumerate(lines):
                self.own_x[band, t, pl.ds(i, nz, stride=mx), :] = line
        bands = lift(
            lambda x: self.zr[t, pl.ds(x, 4, stride=nx), :], nx,
            (self.cr[0, t, 0], self.cr[0, t, 1]), (self.cr[1, t, 0], self.cr[1, t, 1]),
        )
        for band, lines in enumerate(bands):
            for i, line in enumerate(lines):
                self.halo_x[band, t, pl.ds(i, 4, stride=mx), :] = line
        for xb in (0, 1):
            halo = [self.halo_x[xb, t, i * mx:(i + 1) * mx, :] for i in range(4)]
            bands = lift(lambda z: self.own_x[xb, t, z * mx:(z + 1) * mx, :], nz, halo[:2], halo[2:])
            for zb, lines in enumerate(bands):
                for i, line in enumerate(lines):
                    self.both[2 * zb + xb, t, i * mx:(i + 1) * mx, :] = line

    def receive(self, c):
        for copy in self.copies[c]:
            copy.wait_recv()
        pl.loop(*self.tile_range(c))(self.tile_planes)

    def lines(self, band, rows_from, planes, approx):
        zb, xb = band // 2, band % 2
        mx = self.nx // 2
        rows = pl.ds(rows_from * mx, planes * mx)
        even, odd = circle([self.both[band, t, rows, :] for t in range(2 * self.pairs + 1)])
        low, high = lift_lanes(even, odd)
        width = self.pairs * LANES
        low = low * ZETA ** (3 - 2 * (zb + xb))
        high = high[:, :width] * ZETA ** (1 - 2 * (zb + xb))
        if band == 0 and self.index < 2:
            for j in range(self.pairs + 1):
                approx[j, rows, :] = low[:, j * LANES:(j + 1) * LANES]
        for i in range(planes):
            if band == 0 and self.index == 2:
                approx[rows_from + i] = low[i * mx:(i + 1) * mx, :width]
            if band > 0:
                self.details[4 * zb + xb - 1, rows_from + i] = low[i * mx:(i + 1) * mx, :width]
            self.details[4 * zb + 2 + xb - 1, rows_from + i] = high[i * mx:(i + 1) * mx]

    def all_lines(self, bands, approx=None):
        planes = self.nz // 2
        step = min(planes, 2)
        for band in bands:
            if planes // step > 1:
                pl.loop(0, planes // step)(lambda k, band=band: self.lines(band, k * step, step, approx))
            else:
                self.lines(band, 0, step, approx)


class FirstLevel:
    def __init__(self, nz, nx, pairs, source, refs, details, sems, sem_base, peers, chunks):
        self.nz, self.nx, self.pairs, self.source, self.details = nz, nx, pairs, source, details
        self.split, self.xs, self.xr, self.own_x, self.flat, self.zs, self.zr = refs
        self.chunks = chunks
        send_sems, recv_sems = sems
        moves = []
        for c in range(len(chunks)):
            start, stop = self.tile_range(c)
            tiles = pl.ds(start, stop - start)
            moves.append([(self.xs.at[s, tiles], self.xr.at[1 - s, tiles], peers["x"][s]) for s in (0, 1)])
        for b in range(4):
            tiles = pl.ds(0, self.band_tiles(b))
            moves.append([
                (self.zs.at[b, s, tiles], self.zr.at[b, 1 - s, tiles], peers["z"][s]) for s in (0, 1)
            ])
        self.copies = []
        for k, pair in enumerate(moves):
            self.copies.append([
                pltpu.make_async_remote_copy(
                    src_ref=src, dst_ref=dst,
                    send_sem=send_sems.at[sem_base + 2 * k + i],
                    recv_sem=recv_sems.at[sem_base + 2 * k + i],
                    device_id=where, device_id_type=MESH,
                )
                for i, (src, dst, where) in enumerate(pair)
            ])

    tile_range = Level.tile_range
    split_chunk = Level.split_chunk

    def band_tiles(self, b):
        return self.pairs + (1 if b == 0 else 0)

    def tile_states(self, t):
        states = boundary_states(lambda x: self.split[t, pl.ds(x, self.nz, stride=self.nx), :], self.nx)
        for i, state in enumerate(states):
            self.xs[i // 2, t, i % 2] = state

    def prepare(self, c):
        self.split_chunk(c)
        pl.loop(*self.tile_range(c))(self.tile_states)

    def start(self, k):
        for copy in self.copies[k]:
            copy.start()

    def lift_x(self, t):
        nz, nx = self.nz, self.nx
        bands = lift(
            lambda x: self.split[t, pl.ds(x, nz, stride=nx), :], nx,
            (self.xr[0, t, 0], self.xr[0, t, 1]), (self.xr[1, t, 0], self.xr[1, t, 1]),
        )
        for band, lines in enumerate(bands):
            for i, line in enumerate(lines):
                self.own_x[band, t, pl.ds(i, nz, stride=nx // 2), :] = line

    def receive_x(self, c):
        for copy in self.copies[c]:
            copy.wait_recv()
        pl.loop(*self.tile_range(c))(self.lift_x)

    def lift_y(self, xb):
        count = self.nx

        def some(k):
            rows = pl.ds(pl.multiple_of(k * count, count), count)
            even, odd = circle([self.own_x[xb, t, rows, :] for t in range(2 * self.pairs + 1)])
            low, high = lift_lanes(even, odd)
            for j in range(self.band_tiles(xb)):
                self.flat[xb, j, rows, :] = low[:, j * LANES:(j + 1) * LANES]
            for j in range(self.pairs):
                self.flat[2 + xb, j, rows, :] = high[:, j * LANES:(j + 1) * LANES]

        pl.loop(0, self.nz // 2)(some)

    def send_z(self, b):
        mx, n = self.nx // 2, self.band_tiles(b)
        states = boundary_states(lambda z: self.flat[b, 0:n, z * mx:(z + 1) * mx, :], self.nz)
        for i, state in enumerate(states):
            self.zs[b, i // 2, 0:n, (i % 2) * mx:(i % 2 + 1) * mx, :] = state
        self.start(len(self.chunks) + b)

    def receive_z(self, b, approx=None):
        mx = self.nx // 2
        for copy in self.copies[len(self.chunks) + b]:
            copy.wait_recv()

        def tile(t, inside=True):
            halo = [self.zr[b, s, t, i * mx:(i + 1) * mx, :] for s in (0, 1) for i in (0, 1)]
            bands = lift(lambda z: self.flat[b, t, z * mx:(z + 1) * mx, :], self.nz, halo[:2], halo[2:])
            for zb, lines in enumerate(bands):
                scale = ZETA ** (3 - 2 * (zb + b // 2 + b % 2))
                for i, line in enumerate(lines):
                    if zb == 0 and b == 0:
                        approx[t, i * mx:(i + 1) * mx, :] = line * scale
                    elif inside:
                        lanes = pl.ds(pl.multiple_of(t * LANES, LANES), LANES)
                        self.details[4 * zb + b - 1, i, :, lanes] = line * scale

        pl.loop(0, self.pairs)(tile)
        if b == 0:
            tile(self.pairs, inside=False)


def first_buffers(nz, nx, pairs):
    tiles = 2 * pairs + 1
    shapes = [(tiles, nz * nx, LANES)]
    shapes += [(2, tiles, 2, nz, LANES)] * 2
    shapes += [(2, tiles, nz * nx // 2, LANES)]
    shapes += [(4, pairs + 1, nz * nx // 2, LANES)]
    shapes += [(4, 2, pairs + 1, nx, LANES)] * 2
    return [pltpu.VMEM(shape, F32) for shape in shapes]


def buffers(nz, nx, pairs):
    tiles = 2 * pairs + 1
    shapes = [(tiles, nz * nx, LANES)]
    shapes += [(tiles, 4 * nx, LANES)] * 2
    shapes += [(2, tiles, 2, nz, LANES)] * 2
    shapes += [(2, tiles, 2, 4, LANES)] * 2
    shapes += [(2, tiles, nz * nx // 2, LANES), (2, tiles, 2 * nx, LANES)]
    shapes += [(4, tiles, nz * nx // 4, LANES)]
    return [pltpu.VMEM(shape, F32) for shape in shapes]


def hand_out(*refs):
    sems = refs[-1]
    n = (len(refs) - 1) // 2
    copies = [pltpu.make_async_copy(refs[i], refs[n + i], sems.at[i]) for i in range(n)]
    for copy in copies:
        copy.start()
    for copy in copies:
        copy.wait()


def kernel(sizes, axes, u_ref, one_ref, two_ref, three_ref, approx_ref, *scratch):
    scratch = list(scratch)
    send_sems, recv_sems, in_sems, raw, pack_l, pack_r, halo_l, halo_r, approx_four, approx_five = scratch[:10]
    rest = scratch[10:]
    first_refs, rest = rest[:7], rest[7:]
    per_level = len(rest) // 2
    gx, gy, gz = axes
    ix, iy, iz = (lax.axis_index(a) for a in ("gx", "gy", "gz"))
    around = lambda i, n: (lax.rem(i + n - 1, n), lax.rem(i + 1, n))
    near_x, near_y, near_z = around(ix, gx), around(iy, gy), around(iz, gz)
    peers = {
        "x": [(x, iy, iz) for x in near_x],
        "y": [(ix, y, iz) for y in near_y],
        "z": [(ix, iy, z) for z in near_z],
        "xz": [[(x, iy, z) for z in near_z] for x in near_x],
    }
    (nz, nx, pairs) = sizes[0]
    tiles = 2 * pairs

    loads = [
        pltpu.make_async_copy(u_ref.at[:, :, pl.ds(t * LANES, LANES)], raw.at[t], in_sems.at[t])
        for t in range(tiles)
    ]
    order = [0, tiles - 1] + list(range(1, tiles - 1))
    for t in order:
        loads[t].start()

    barrier = pltpu.get_barrier_semaphore()
    greeted = peers["x"] + peers["y"] + peers["z"] + peers["xz"][0] + peers["xz"][1]
    for where in greeted:
        pl.semaphore_signal(barrier, inc=1, device_id=where, device_id_type=MESH)

    half = pairs // 2
    sems = (send_sems, recv_sems)
    chunks = [(0, half), (half, pairs), (pairs, pairs + 1)]
    first = FirstLevel(nz, nx, pairs, raw.reshape(tiles + 1, nz * nx, LANES), first_refs, one_ref, sems, 2, peers, chunks)
    second, third = (
        Level(i, *sizes[i], source, rest[(i - 1) * per_level:i * per_level], details, sems, 8 + 8 * i, peers,
              [(0, sizes[i][2] + 1)])
        for i, source, details in ((1, approx_four, two_ref), (2, approx_five, three_ref))
    )

    groups = LANES // HALO
    part = nz * nx // groups
    lane = lax.broadcasted_iota(jnp.int32, (part, LANES), 1)
    loads[0].wait()
    loads[tiles - 1].wait()
    flat = first.source

    def gather(tile, offset):
        total = None
        for g in range(groups):
            rows = pltpu.roll(flat[tile, g * part:(g + 1) * part, :], (g * HALO - offset) % LANES, 1)
            total = rows if total is None else jnp.where(lane >= g * HALO, rows, total)
        return total

    pack_l[...] = gather(0, 0)
    pack_r[...] = gather(tiles - 1, LANES - HALO)
    for t in range(1, tiles - 1):
        loads[t].wait()
    first.prepare(0)

    pl.semaphore_wait(barrier, len(greeted))
    y_copies = [
        pltpu.make_async_remote_copy(src_ref=src, dst_ref=dst, send_sem=send_sems.at[i], recv_sem=recv_sems.at[i],
                                     device_id=where, device_id_type=MESH)
        for i, (src, dst, where) in enumerate(((pack_l, halo_r, peers["y"][0]), (pack_r, halo_l, peers["y"][1])))
    ]
    for copy in y_copies:
        copy.start()
    first.start(0)
    first.prepare(1)
    first.start(1)
    for copy in y_copies:
        copy.wait_recv()
    for g in range(groups):
        after = pltpu.roll(halo_r[...], (-g * HALO) % LANES, 1)
        before = pltpu.roll(halo_l[...], (LANES - HALO - g * HALO) % LANES, 1)
        flat[tiles, g * part:(g + 1) * part, :] = jnp.where(
            lane < HALO, after, jnp.where(lane >= LANES - HALO, before, 0.0)
        )
    first.prepare(2)
    first.start(2)
    for c in range(3):
        first.receive_x(c)
    first.lift_y(0)
    first.send_z(0)
    first.send_z(2)
    first.lift_y(1)
    first.receive_z(0, approx_four)

    second.prepare(0)
    second.send(0)
    first.send_z(1)
    first.send_z(3)
    first.receive_z(2)
    second.receive(0)
    second.all_lines([0], approx_five)

    third.prepare(0)
    third.send(0)
    second.all_lines([1, 2, 3])
    first.receive_z(1)
    first.receive_z(3)
    third.receive(0)
    third.all_lines([0, 1, 2, 3], approx_ref)

    for copy in y_copies:
        copy.wait_send()
    for level in (first, second, third):
        for copies in level.copies:
            for copy in copies:
                copy.wait_send()


def solution(mesh):
    axes = tuple(mesh.shape[a] for a in ("gx", "gy", "gz"))

    def on_device(density):
        nz, nx, ny = density.shape
        sizes = [(nz >> i, nx >> i, (ny >> i) // (2 * LANES)) for i in range(3)]
        tiles = ny // LANES
        shapes = [(7, z // 2, x // 2, p * LANES) for z, x, p in sizes]
        shapes.append(shapes[-1][1:])
        n_sems = 32
        packed = (nz * nx * HALO // LANES, LANES)
        scratch = [
            pltpu.SemaphoreType.DMA((n_sems,)),
            pltpu.SemaphoreType.DMA((n_sems,)),
            pltpu.SemaphoreType.DMA((tiles,)),
            pltpu.VMEM((tiles + 1, nz, nx, LANES), F32),
        ]
        scratch += [pltpu.VMEM(packed, F32)] * 4
        for z, x, p in sizes[:2]:
            scratch.append(pltpu.VMEM((p + 1, z * x // 4, LANES), F32))
        scratch += first_buffers(*sizes[0])
        for z, x, p in sizes[1:]:
            scratch += buffers(z, x, p)
        outs = [jax.ShapeDtypeStruct(shape, F32) for shape in shapes]
        results = pl.pallas_call(
            functools.partial(kernel, sizes, axes),
            out_shape=[pltpu.VMEM(shape, F32) for shape in shapes],
            in_specs=[pl.BlockSpec(memory_space=pltpu.HBM)],
            out_specs=[pl.BlockSpec(memory_space=pltpu.VMEM)] * 4,
            scratch_shapes=scratch,
            compiler_params=pltpu.CompilerParams(
                collective_id=0, has_side_effects=True, vmem_limit_bytes=59 << 20
            ),
            cost_estimate=pl.CostEstimate(flops=20_000_000, bytes_accessed=2 << 20, transcendentals=0),
        )(density)
        return pl.pallas_call(
            hand_out,
            out_shape=outs,
            in_specs=[pl.BlockSpec(memory_space=pltpu.VMEM)] * 4,
            out_specs=[pl.BlockSpec(memory_space=pltpu.HBM)] * 4,
            scratch_shapes=[pltpu.SemaphoreType.DMA((4,))],
            compiler_params=pltpu.CompilerParams(vmem_limit_bytes=1 << 20),
            cost_estimate=pl.CostEstimate(flops=0, bytes_accessed=2 << 20, transcendentals=0),
        )(*results)

    return jax.shard_map(
        on_device,
        mesh=mesh,
        in_specs=(P("gz", "gx", "gy"),),
        out_specs=(
            P(None, "gz", "gx", "gy"),
            P(None, "gz", "gx", "gy"),
            P(None, "gz", "gx", "gy"),
            P("gz", "gx", "gy"),
        ),
        check_vma=False,
    )
```

```python
import functools

import jax
import jax.numpy as jnp
from jax import lax
from jax.experimental import pallas as pl
from jax.experimental.pallas import tpu as pltpu
from jax.sharding import PartitionSpec as P

ALPHA = -1.586134342
BETA = -0.05298011854
GAMMA = 0.8829110762
DELTA = 0.4435068522
ZETA = 1.149604398

MESH = pl.DeviceIdType.MESH
LANES = 128
HALO = 32
F32 = jnp.float32
BF16 = jnp.bfloat16


def boundary_states(get, n):
    s0, last_s = get(0), get(n - 2)
    lead = get(1) + ALPHA * (s0 + get(2))
    trail = get(n - 3) + ALPHA * (get(n - 4) + last_s)
    return s0, s0 + BETA * lead, get(n - 1) + ALPHA * last_s, last_s + BETA * trail


def lift(get, n, from_left, from_right):
    m = n // 2
    s = [get(2 * i) for i in range(m)]
    d = [get(2 * i + 1) for i in range(m)]
    r, q = from_left
    s_next, p = from_right
    d1 = [r + ALPHA * s[0]]
    for i in range(m):
        d1.append(d[i] + ALPHA * (s[i] + (s[i + 1] if i + 1 < m else s_next)))
    s1 = [q + BETA * d1[0]]
    for i in range(m):
        s1.append(s[i] + BETA * (d1[i] + d1[i + 1]))
    s1.append(p + BETA * d1[m])
    d2 = [d1[i] + GAMMA * (s1[i] + s1[i + 1]) for i in range(m + 1)]
    low = [s1[i + 1] + DELTA * (d2[i] + d2[i + 1]) for i in range(m)]
    return low, d2[1:]


def lift_lanes(even, odd):
    width = even.shape[-1]
    after = lambda v: pltpu.roll(v, width - 1, 1)
    before = lambda v: pltpu.roll(v, 1, 1)
    d = odd + ALPHA * (even + after(even))
    s = even + BETA * (before(d) + d)
    d = d + GAMMA * (s + after(s))
    s = s + DELTA * (before(d) + d)
    return s, d


def circle(tiles):
    ends = tiles[-1]
    turned = pltpu.roll(ends, LANES // 2, 1)
    near = lax.broadcasted_iota(jnp.int32, ends.shape, 1) < LANES // 2
    even = jnp.concatenate(tiles[0:-1:2] + [jnp.where(near, ends, turned)], axis=1)
    odd = jnp.concatenate(tiles[1:-1:2] + [jnp.where(near, turned, ends)], axis=1)
    return even, odd


def exact_select(x, choose):
    parts = []
    for _ in range(3):
        parts.append(x.astype(BF16))
        x = x - parts[-1].astype(F32)
    terms = jnp.dot(jnp.concatenate(parts, axis=0), choose, preferred_element_type=F32)
    n = x.shape[0]
    return terms[:n] + terms[n:2 * n] + terms[2 * n:]


def split_matrix(depth):
    k = lax.broadcasted_iota(jnp.int32, (depth, depth), 0)
    n = lax.broadcasted_iota(jnp.int32, (depth, depth), 1)
    return (k == jnp.where(n < depth // 2, 2 * n, 2 * n - depth + 1)).astype(BF16)


class Level:
    def __init__(self, index, nz, nx, pairs, source, refs, details, sems, sem_base, peers, chunks):
        self.index, self.nz, self.nx, self.pairs = index, nz, nx, pairs
        self.source = source
        (self.split, self.zs, self.zr, self.xs, self.xr, self.cs, self.cr,
         self.own_x, self.halo_x, self.both) = refs
        self.details = details
        self.send_sems, self.recv_sems = sems
        self.peers = peers
        self.chunks = chunks
        self.sem_base = sem_base
        self.copies = [self.make_copies(c) for c in range(len(chunks))]

    def tile_range(self, c):
        start, stop = self.chunks[c]
        return 2 * start, min(2 * stop, 2 * self.pairs + 1)

    def make_copies(self, c):
        start, stop = self.tile_range(c)
        tiles = pl.ds(start, stop - start)
        p = self.peers
        side = 2 * self.nx
        moves = [
            (self.zs.at[tiles, pl.ds(sz * side, side)], self.zr.at[tiles, pl.ds((1 - sz) * side, side)], p["z"][sz])
            for sz in (0, 1)
        ]
        for sx in (0, 1):
            for sz in (0, 1):
                moves.append((self.cs.at[sx, tiles, :, pl.ds(2 * sz, 2)],
                              self.cr.at[1 - sx, tiles, :, pl.ds(2 - 2 * sz, 2)], p["xz"][sx][sz]))
        for sx in (0, 1):
            moves.append((self.xs.at[sx, tiles], self.xr.at[1 - sx, tiles], p["x"][sx]))
        return [
            pltpu.make_async_remote_copy(
                src_ref=src, dst_ref=dst,
                send_sem=self.send_sems.at[self.sem_base + 8 * c + i],
                recv_sem=self.recv_sems.at[self.sem_base + 8 * c + i],
                device_id=where, device_id_type=MESH,
            )
            for i, (src, dst, where) in enumerate(moves)
        ]

    def split_chunk(self, c):
        start, stop = self.chunks[c]
        main = min(stop, self.pairs)
        rows = self.nz * self.nx
        if start == self.pairs:
            self.split[2 * start] = exact_select(self.source[2 * start], split_matrix(LANES))
            return
        firsts = [self.source[2 * j] for j in range(start, stop)]
        seconds = [self.source[2 * j + 1 if j < main else 2 * j] for j in range(start, stop)]
        x = jnp.concatenate([jnp.concatenate(firsts, axis=0), jnp.concatenate(seconds, axis=0)], axis=1)
        both = exact_select(x, split_matrix(2 * LANES))
        for i, j in enumerate(range(start, stop)):
            even = both[i * rows:(i + 1) * rows, :LANES]
            odd = both[i * rows:(i + 1) * rows, LANES:]
            if j < main:
                self.split[2 * j] = even
                self.split[2 * j + 1] = odd
            else:
                lane = lax.broadcasted_iota(jnp.int32, (rows, LANES), 1)
                self.split[2 * j] = jnp.where(lane < LANES // 2, even, odd)

    def prepare(self, c):
        self.split_chunk(c)
        nz, nx = self.nz, self.nx
        states = boundary_states(lambda z: self.split[:, z * nx:(z + 1) * nx, :], nz)
        for i, state in enumerate(states):
            self.zs[:, i * nx:(i + 1) * nx, :] = state
        states = boundary_states(lambda x: self.split[:, pl.ds(x, nz, stride=nx), :], nx)
        for i, state in enumerate(states):
            self.xs[i // 2, :, i % 2] = state
        states = boundary_states(lambda x: self.zs[:, pl.ds(x, 4, stride=nx), :], nx)
        for i, state in enumerate(states):
            self.cs[i // 2, :, i % 2] = state

    def send(self, c):
        for copy in self.copies[c]:
            copy.start()

    def receive(self, c):
        for copy in self.copies[c]:
            copy.wait_recv()
        nz, nx = self.nz, self.nx
        mx = nx // 2
        band_rows = nz * nx // 4
        for ref, n, source, ends in ((self.own_x, nz, self.split, self.xr), (self.halo_x, 4, self.zr, self.cr)):
            bands = lift(
                lambda x: source[:, pl.ds(x, n, stride=nx), :], nx,
                (ends[0, :, 0], ends[0, :, 1]), (ends[1, :, 0], ends[1, :, 1]),
            )
            for band, lines in enumerate(bands):
                for i, line in enumerate(lines):
                    ref[band, :, pl.ds(i, n, stride=mx), :] = line
        for xb in (0, 1):
            halo = [self.halo_x[xb, :, i * mx:(i + 1) * mx, :] for i in range(4)]
            bands = lift(lambda z: self.own_x[xb, :, z * mx:(z + 1) * mx, :], nz, halo[:2], halo[2:])
            for zb, lines in enumerate(bands):
                for i, line in enumerate(lines):
                    row = (2 * zb + xb) * band_rows + i * mx
                    self.both[:, row:row + mx, :] = line

    def lines(self, bands, approx=None):
        mx, mz = self.nx // 2, self.nz // 2
        band_rows = mx * mz
        first, last = bands[0], bands[-1] + 1
        even, odd = circle([self.both[t, first * band_rows:last * band_rows, :] for t in range(2 * self.pairs + 1)])
        lows, highs = lift_lanes(even, odd)
        width = self.pairs * LANES
        for k, band in enumerate(bands):
            zb, xb = band // 2, band % 2
            rows = slice(k * band_rows, (k + 1) * band_rows)
            low = lows[rows] * ZETA ** (3 - 2 * (zb + xb))
            high = highs[rows, :width] * ZETA ** (1 - 2 * (zb + xb))
            if band == 0 and self.index < 2:
                for j in range(self.pairs + 1):
                    approx[j] = low[:, j * LANES:(j + 1) * LANES]
            for i in range(mz):
                row = low[i * mx:(i + 1) * mx, :width]
                if band > 0:
                    self.details[4 * zb + xb - 1, i] = row
                elif self.index == 2:
                    approx[i] = row
                self.details[4 * zb + 2 + xb - 1, i] = high[i * mx:(i + 1) * mx]


class FirstLevel:
    def __init__(self, nz, nx, pairs, source, refs, details, sems, sem_base, peers, chunks):
        self.nz, self.nx, self.pairs, self.source, self.details = nz, nx, pairs, source, details
        self.split, self.xs, self.xr, self.own_x, self.flat, self.zs, self.zr = refs
        self.chunks = chunks
        send_sems, recv_sems = sems
        moves = []
        for c in range(len(chunks)):
            start, stop = self.tile_range(c)
            tiles = pl.ds(start, stop - start)
            moves.append([(self.xs.at[s, tiles], self.xr.at[1 - s, tiles], peers["x"][s]) for s in (0, 1)])
        for b in range(4):
            tiles = pl.ds(0, self.band_tiles(b))
            moves.append([
                (self.zs.at[b, s, tiles], self.zr.at[b, 1 - s, tiles], peers["z"][s]) for s in (0, 1)
            ])
        self.copies = []
        for k, pair in enumerate(moves):
            self.copies.append([
                pltpu.make_async_remote_copy(
                    src_ref=src, dst_ref=dst,
                    send_sem=send_sems.at[sem_base + 2 * k + i],
                    recv_sem=recv_sems.at[sem_base + 2 * k + i],
                    device_id=where, device_id_type=MESH,
                )
                for i, (src, dst, where) in enumerate(pair)
            ])

    tile_range = Level.tile_range
    split_chunk = Level.split_chunk

    def band_tiles(self, b):
        return self.pairs + (1 if b == 0 else 0)

    def prepare(self, c):
        self.split_chunk(c)
        start, stop = self.tile_range(c)
        states = boundary_states(lambda x: self.split[start:stop, pl.ds(x, self.nz, stride=self.nx), :], self.nx)
        for i, state in enumerate(states):
            self.xs[i // 2, start:stop, i % 2] = state

    def start(self, k):
        for copy in self.copies[k]:
            copy.start()

    def lift_x(self, t):
        nz, nx = self.nz, self.nx
        bands = lift(
            lambda x: self.split[t, pl.ds(x, nz, stride=nx), :], nx,
            (self.xr[0, t, 0], self.xr[0, t, 1]), (self.xr[1, t, 0], self.xr[1, t, 1]),
        )
        for band, lines in enumerate(bands):
            for i, line in enumerate(lines):
                self.own_x[band, t, pl.ds(i, nz, stride=nx // 2), :] = line

    def receive_x(self, c):
        for copy in self.copies[c]:
            copy.wait_recv()
        start, stop = self.tile_range(c)
        pl.loop(start, stop, unroll=min(2, stop - start))(self.lift_x)

    def lift_y(self, xb):
        count = self.nx * self.nz // 4

        def some(k):
            rows = pl.ds(pl.multiple_of(k * count, count), count)
            even, odd = circle([self.own_x[xb, t, rows, :] for t in range(2 * self.pairs + 1)])
            low, high = lift_lanes(even, odd)
            for j in range(self.band_tiles(xb)):
                self.flat[xb, j, rows, :] = low[:, j * LANES:(j + 1) * LANES]
            for j in range(self.pairs):
                self.flat[2 + xb, j, rows, :] = high[:, j * LANES:(j + 1) * LANES]

        pl.loop(0, 2)(some)

    def send_z(self, b):
        mx, n = self.nx // 2, self.band_tiles(b)
        states = boundary_states(lambda z: self.flat[b, 0:n, z * mx:(z + 1) * mx, :], self.nz)
        for i, state in enumerate(states):
            self.zs[b, i // 2, 0:n, (i % 2) * mx:(i % 2 + 1) * mx, :] = state
        self.start(len(self.chunks) + b)

    def receive_z(self, b, approx=None):
        mx = self.nx // 2
        for copy in self.copies[len(self.chunks) + b]:
            copy.wait_recv()

        n = self.band_tiles(b)
        halo = [self.zr[b, s, 0:n, i * mx:(i + 1) * mx, :] for s in (0, 1) for i in (0, 1)]
        bands = lift(lambda z: self.flat[b, 0:n, z * mx:(z + 1) * mx, :], self.nz, halo[:2], halo[2:])
        for zb, lines in enumerate(bands):
            scale = ZETA ** (3 - 2 * (zb + b // 2 + b % 2))
            for i, line in enumerate(lines):
                line = line * scale
                if zb == 0 and b == 0:
                    approx[:, i * mx:(i + 1) * mx, :] = line
                else:
                    self.details[4 * zb + b - 1, i] = jnp.concatenate([line[t] for t in range(self.pairs)], axis=1)


def first_buffers(nz, nx, pairs):
    tiles = 2 * pairs + 1
    shapes = [(tiles, nz * nx, LANES)]
    shapes += [(2, tiles, 2, nz, LANES)] * 2
    shapes += [(2, tiles, nz * nx // 2, LANES)]
    shapes += [(4, pairs + 1, nz * nx // 2, LANES)]
    shapes += [(4, 2, pairs + 1, nx, LANES)] * 2
    return [pltpu.VMEM(shape, F32) for shape in shapes]


def buffers(nz, nx, pairs):
    tiles = 2 * pairs + 1
    shapes = [(tiles, nz * nx, LANES)]
    shapes += [(tiles, 4 * nx, LANES)] * 2
    shapes += [(2, tiles, 2, nz, LANES)] * 2
    shapes += [(2, tiles, 2, 4, LANES)] * 2
    shapes += [(2, tiles, nz * nx // 2, LANES), (2, tiles, 2 * nx, LANES)]
    shapes += [(tiles, nz * nx, LANES)]
    return [pltpu.VMEM(shape, F32) for shape in shapes]


def hand_out(*refs):
    sems = refs[-1]
    n = (len(refs) - 1) // 2
    copies = [pltpu.make_async_copy(refs[i], refs[n + i], sems.at[i]) for i in range(n)]
    for copy in copies:
        copy.start()
    for copy in copies:
        copy.wait()


def kernel(sizes, axes, u_ref, one_ref, two_ref, three_ref, approx_ref, *scratch):
    scratch = list(scratch)
    send_sems, recv_sems, in_sems, raw, pack_l, pack_r, halo_l, halo_r, approx_four, approx_five = scratch[:10]
    rest = scratch[10:]
    first_refs, rest = rest[:7], rest[7:]
    per_level = len(rest) // 2
    gx, gy, gz = axes
    ix, iy, iz = (lax.axis_index(a) for a in ("gx", "gy", "gz"))
    around = lambda i, n: (lax.rem(i + n - 1, n), lax.rem(i + 1, n))
    near_x, near_y, near_z = around(ix, gx), around(iy, gy), around(iz, gz)
    peers = {
        "x": [(x, iy, iz) for x in near_x],
        "y": [(ix, y, iz) for y in near_y],
        "z": [(ix, iy, z) for z in near_z],
        "xz": [[(x, iy, z) for z in near_z] for x in near_x],
    }
    (nz, nx, pairs) = sizes[0]
    tiles = 2 * pairs

    loads = [
        pltpu.make_async_copy(u_ref.at[:, :, pl.ds(t * LANES, LANES)], raw.at[t], in_sems.at[t])
        for t in range(tiles)
    ]
    order = [0, tiles - 1] + list(range(1, tiles - 1))
    for t in order:
        loads[t].start()

    barrier = pltpu.get_barrier_semaphore()
    greeted = peers["x"] + peers["y"] + peers["z"] + peers["xz"][0] + peers["xz"][1]
    for where in greeted:
        pl.semaphore_signal(barrier, inc=1, device_id=where, device_id_type=MESH)

    half = pairs // 2
    sems = (send_sems, recv_sems)
    chunks = [(0, half), (half, pairs), (pairs, pairs + 1)]
    first = FirstLevel(nz, nx, pairs, raw.reshape(tiles + 1, nz * nx, LANES), first_refs, one_ref, sems, 2, peers, chunks)
    second, third = (
        Level(i, *sizes[i], source, rest[(i - 1) * per_level:i * per_level], details, sems, 8 + 8 * i, peers,
              [(0, sizes[i][2] + 1)])
        for i, source, details in ((1, approx_four, two_ref), (2, approx_five, three_ref))
    )

    groups = LANES // HALO
    part = nz * nx // groups
    lane = lax.broadcasted_iota(jnp.int32, (part, LANES), 1)
    loads[0].wait()
    loads[tiles - 1].wait()
    flat = first.source

    def gather(tile, offset):
        total = None
        for g in range(groups):
            rows = pltpu.roll(flat[tile, g * part:(g + 1) * part, :], (g * HALO - offset) % LANES, 1)
            total = rows if total is None else jnp.where(lane >= g * HALO, rows, total)
        return total

    pack_l[...] = gather(0, 0)
    pack_r[...] = gather(tiles - 1, LANES - HALO)
    for t in range(1, tiles - 1):
        loads[t].wait()
    first.prepare(0)

    pl.semaphore_wait(barrier, len(greeted))
    y_copies = [
        pltpu.make_async_remote_copy(src_ref=src, dst_ref=dst, send_sem=send_sems.at[i], recv_sem=recv_sems.at[i],
                                     device_id=where, device_id_type=MESH)
        for i, (src, dst, where) in enumerate(((pack_l, halo_r, peers["y"][0]), (pack_r, halo_l, peers["y"][1])))
    ]
    for copy in y_copies:
        copy.start()
    first.start(0)
    first.prepare(1)
    first.start(1)
    for copy in y_copies:
        copy.wait_recv()
    for g in range(groups):
        after = pltpu.roll(halo_r[...], (-g * HALO) % LANES, 1)
        before = pltpu.roll(halo_l[...], (LANES - HALO - g * HALO) % LANES, 1)
        flat[tiles, g * part:(g + 1) * part, :] = jnp.where(
            lane < HALO, after, jnp.where(lane >= LANES - HALO, before, 0.0)
        )
    first.prepare(2)
    first.start(2)
    for c in range(3):
        first.receive_x(c)
    first.lift_y(0)
    first.send_z(0)
    first.send_z(2)
    first.lift_y(1)
    first.receive_z(0, approx_four)

    second.prepare(0)
    second.send(0)
    first.send_z(1)
    first.send_z(3)
    first.receive_z(2)
    second.receive(0)
    second.lines([0], approx_five)

    third.prepare(0)
    third.send(0)
    second.lines([1, 2, 3])
    first.receive_z(1)
    first.receive_z(3)
    third.receive(0)
    third.lines([0, 1, 2, 3], approx_ref)

    for copy in y_copies:
        copy.wait_send()
    for level in (first, second, third):
        for copies in level.copies:
            for copy in copies:
                copy.wait_send()


def solution(mesh):
    axes = tuple(mesh.shape[a] for a in ("gx", "gy", "gz"))

    def on_device(density):
        nz, nx, ny = density.shape
        sizes = [(nz >> i, nx >> i, (ny >> i) // (2 * LANES)) for i in range(3)]
        tiles = ny // LANES
        shapes = [(7, z // 2, x // 2, p * LANES) for z, x, p in sizes]
        shapes.append(shapes[-1][1:])
        n_sems = 32
        packed = (nz * nx * HALO // LANES, LANES)
        scratch = [
            pltpu.SemaphoreType.DMA((n_sems,)),
            pltpu.SemaphoreType.DMA((n_sems,)),
            pltpu.SemaphoreType.DMA((tiles,)),
            pltpu.VMEM((tiles + 1, nz, nx, LANES), F32),
        ]
        scratch += [pltpu.VMEM(packed, F32)] * 4
        for z, x, p in sizes[:2]:
            scratch.append(pltpu.VMEM((p + 1, z * x // 4, LANES), F32))
        scratch += first_buffers(*sizes[0])
        for z, x, p in sizes[1:]:
            scratch += buffers(z, x, p)
        outs = [jax.ShapeDtypeStruct(shape, F32) for shape in shapes]
        results = pl.pallas_call(
            functools.partial(kernel, sizes, axes),
            out_shape=[pltpu.VMEM(shape, F32) for shape in shapes],
            in_specs=[pl.BlockSpec(memory_space=pltpu.HBM)],
            out_specs=[pl.BlockSpec(memory_space=pltpu.VMEM)] * 4,
            scratch_shapes=scratch,
            compiler_params=pltpu.CompilerParams(
                collective_id=0, has_side_effects=True, vmem_limit_bytes=59 << 20
            ),
            cost_estimate=pl.CostEstimate(flops=20_000_000, bytes_accessed=2 << 20, transcendentals=0),
        )(density)
        return pl.pallas_call(
            hand_out,
            out_shape=outs,
            in_specs=[pl.BlockSpec(memory_space=pltpu.VMEM)] * 4,
            out_specs=[pl.BlockSpec(memory_space=pltpu.HBM)] * 4,
            scratch_shapes=[pltpu.SemaphoreType.DMA((4,))],
            compiler_params=pltpu.CompilerParams(vmem_limit_bytes=1 << 20),
            cost_estimate=pl.CostEstimate(flops=0, bytes_accessed=2 << 20, transcendentals=0),
        )(*results)

    return jax.shard_map(
        on_device,
        mesh=mesh,
        in_specs=(P("gz", "gx", "gy"),),
        out_specs=(
            P(None, "gz", "gx", "gy"),
            P(None, "gz", "gx", "gy"),
            P(None, "gz", "gx", "gy"),
            P("gz", "gx", "gy"),
        ),
        check_vma=False,
    )
```

```python
import functools

import jax
import jax.numpy as jnp
from jax import lax
from jax.experimental import pallas as pl
from jax.experimental.pallas import tpu as pltpu
from jax.sharding import PartitionSpec as P

ALPHA = -1.586134342
BETA = -0.05298011854
GAMMA = 0.8829110762
DELTA = 0.4435068522
ZETA = 1.149604398

MESH = pl.DeviceIdType.MESH
LANES = 128
HALO = 32
F32 = jnp.float32
BF16 = jnp.bfloat16


def boundary_states(get, n):
    s0, last_s = get(0), get(n - 2)
    lead = get(1) + ALPHA * (s0 + get(2))
    trail = get(n - 3) + ALPHA * (get(n - 4) + last_s)
    return s0, s0 + BETA * lead, get(n - 1) + ALPHA * last_s, last_s + BETA * trail


def lift(get, n, from_left, from_right):
    m = n // 2
    s = [get(2 * i) for i in range(m)]
    d = [get(2 * i + 1) for i in range(m)]
    r, q = from_left
    s_next, p = from_right
    d1 = [r + ALPHA * s[0]]
    for i in range(m):
        d1.append(d[i] + ALPHA * (s[i] + (s[i + 1] if i + 1 < m else s_next)))
    s1 = [q + BETA * d1[0]]
    for i in range(m):
        s1.append(s[i] + BETA * (d1[i] + d1[i + 1]))
    s1.append(p + BETA * d1[m])
    d2 = [d1[i] + GAMMA * (s1[i] + s1[i + 1]) for i in range(m + 1)]
    low = [s1[i + 1] + DELTA * (d2[i] + d2[i + 1]) for i in range(m)]
    return low, d2[1:]


def lift_lanes(even, odd):
    width = even.shape[-1]
    after = lambda v: pltpu.roll(v, width - 1, 1)
    before = lambda v: pltpu.roll(v, 1, 1)
    d = odd + ALPHA * (even + after(even))
    s = even + BETA * (before(d) + d)
    d = d + GAMMA * (s + after(s))
    s = s + DELTA * (before(d) + d)
    return s, d


def circle(tiles):
    ends = tiles[-1]
    turned = pltpu.roll(ends, LANES // 2, 1)
    near = lax.broadcasted_iota(jnp.int32, ends.shape, 1) < LANES // 2
    even = jnp.concatenate(tiles[0:-1:2] + [jnp.where(near, ends, turned)], axis=1)
    odd = jnp.concatenate(tiles[1:-1:2] + [jnp.where(near, turned, ends)], axis=1)
    return even, odd


def exact_select(x, choose):
    parts = []
    for _ in range(3):
        parts.append(x.astype(BF16))
        x = x - parts[-1].astype(F32)
    terms = jnp.dot(jnp.concatenate(parts, axis=0), choose, preferred_element_type=F32)
    n = x.shape[0]
    return terms[:n] + terms[n:2 * n] + terms[2 * n:]


def split_matrix(depth):
    k = lax.broadcasted_iota(jnp.int32, (depth, depth), 0)
    n = lax.broadcasted_iota(jnp.int32, (depth, depth), 1)
    return (k == jnp.where(n < depth // 2, 2 * n, 2 * n - depth + 1)).astype(BF16)


class Level:
    def __init__(self, index, nz, nx, pairs, source, refs, details, sems, sem_base, peers, chunks):
        self.index, self.nz, self.nx, self.pairs = index, nz, nx, pairs
        self.source = source
        (self.split, self.zs, self.zr, self.xs, self.xr, self.cs, self.cr,
         self.own_x, self.halo_x, self.both) = refs
        self.details = details
        self.send_sems, self.recv_sems = sems
        self.peers = peers
        self.chunks = chunks
        self.sem_base = sem_base
        self.copies = [self.make_copies(c) for c in range(len(chunks))]

    def tile_range(self, c):
        start, stop = self.chunks[c]
        return 2 * start, min(2 * stop, 2 * self.pairs + 1)

    def make_copies(self, c):
        start, stop = self.tile_range(c)
        tiles = pl.ds(start, stop - start)
        p = self.peers
        side = 2 * self.nx
        moves = [
            (self.zs.at[tiles, pl.ds(sz * side, side)], self.zr.at[tiles, pl.ds((1 - sz) * side, side)], p["z"][sz])
            for sz in (0, 1)
        ]
        for sx in (0, 1):
            for sz in (0, 1):
                moves.append((self.cs.at[sx, tiles, :, pl.ds(2 * sz, 2)],
                              self.cr.at[1 - sx, tiles, :, pl.ds(2 - 2 * sz, 2)], p["xz"][sx][sz]))
        for sx in (0, 1):
            moves.append((self.xs.at[sx, tiles], self.xr.at[1 - sx, tiles], p["x"][sx]))
        return [
            pltpu.make_async_remote_copy(
                src_ref=src, dst_ref=dst,
                send_sem=self.send_sems.at[self.sem_base + 8 * c + i],
                recv_sem=self.recv_sems.at[self.sem_base + 8 * c + i],
                device_id=where, device_id_type=MESH,
            )
            for i, (src, dst, where) in enumerate(moves)
        ]

    def split_chunk(self, c):
        start, stop = self.chunks[c]
        main = min(stop, self.pairs)
        rows = self.nz * self.nx
        if start == self.pairs:
            self.split[2 * start] = exact_select(self.source[2 * start], split_matrix(LANES))
            return
        firsts = [self.source[2 * j] for j in range(start, stop)]
        seconds = [self.source[2 * j + 1 if j < main else 2 * j] for j in range(start, stop)]
        x = jnp.concatenate([jnp.concatenate(firsts, axis=0), jnp.concatenate(seconds, axis=0)], axis=1)
        both = exact_select(x, split_matrix(2 * LANES))
        for i, j in enumerate(range(start, stop)):
            even = both[i * rows:(i + 1) * rows, :LANES]
            odd = both[i * rows:(i + 1) * rows, LANES:]
            if j < main:
                self.split[2 * j] = even
                self.split[2 * j + 1] = odd
            else:
                lane = lax.broadcasted_iota(jnp.int32, (rows, LANES), 1)
                self.split[2 * j] = jnp.where(lane < LANES // 2, even, odd)

    def prepare(self, c):
        self.split_chunk(c)
        nz, nx = self.nz, self.nx
        states = boundary_states(lambda z: self.split[:, z * nx:(z + 1) * nx, :], nz)
        for i, state in enumerate(states):
            self.zs[:, i * nx:(i + 1) * nx, :] = state
        states = boundary_states(lambda x: self.split[:, pl.ds(x, nz, stride=nx), :], nx)
        for i, state in enumerate(states):
            self.xs[i // 2, :, i % 2] = state
        states = boundary_states(lambda x: self.zs[:, pl.ds(x, 4, stride=nx), :], nx)
        for i, state in enumerate(states):
            self.cs[i // 2, :, i % 2] = state

    def send(self, c):
        for copy in self.copies[c]:
            copy.start()

    def receive(self, c):
        for copy in self.copies[c]:
            copy.wait_recv()
        nz, nx = self.nz, self.nx
        mx = nx // 2
        band_rows = nz * nx // 4
        for ref, n, source, ends in ((self.own_x, nz, self.split, self.xr), (self.halo_x, 4, self.zr, self.cr)):
            bands = lift(
                lambda x: source[:, pl.ds(x, n, stride=nx), :], nx,
                (ends[0, :, 0], ends[0, :, 1]), (ends[1, :, 0], ends[1, :, 1]),
            )
            for band, lines in enumerate(bands):
                for i, line in enumerate(lines):
                    ref[band, :, pl.ds(i, n, stride=mx), :] = line
        for xb in (0, 1):
            halo = [self.halo_x[xb, :, i * mx:(i + 1) * mx, :] for i in range(4)]
            bands = lift(lambda z: self.own_x[xb, :, z * mx:(z + 1) * mx, :], nz, halo[:2], halo[2:])
            for zb, lines in enumerate(bands):
                for i, line in enumerate(lines):
                    row = (2 * zb + xb) * band_rows + i * mx
                    self.both[:, row:row + mx, :] = line

    def lines(self, bands, approx=None):
        mx, mz = self.nx // 2, self.nz // 2
        band_rows = mx * mz
        first, last = bands[0], bands[-1] + 1
        even, odd = circle([self.both[t, first * band_rows:last * band_rows, :] for t in range(2 * self.pairs + 1)])
        lows, highs = lift_lanes(even, odd)
        width = self.pairs * LANES
        for k, band in enumerate(bands):
            zb, xb = band // 2, band % 2
            rows = slice(k * band_rows, (k + 1) * band_rows)
            low = lows[rows] * ZETA ** (3 - 2 * (zb + xb))
            high = highs[rows, :width] * ZETA ** (1 - 2 * (zb + xb))
            if band == 0 and self.index < 2:
                for j in range(self.pairs + 1):
                    approx[j] = low[:, j * LANES:(j + 1) * LANES]
            for i in range(mz):
                row = low[i * mx:(i + 1) * mx, :width]
                if band > 0:
                    self.details[4 * zb + xb - 1, i] = row
                elif self.index == 2:
                    approx[i] = row
                self.details[4 * zb + 2 + xb - 1, i] = high[i * mx:(i + 1) * mx]


class FirstLevel:
    def __init__(self, nz, nx, pairs, source, refs, details, sems, sem_base, peers, chunks):
        self.nz, self.nx, self.pairs, self.source, self.details = nz, nx, pairs, source, details
        self.split, self.xs, self.xr, self.xe, self.own_x, self.flat, self.zs, self.zr = refs
        self.chunks = chunks
        send_sems, recv_sems = sems
        moves = []
        for c in range(len(chunks)):
            start, stop = self.tile_range(c)
            tiles = pl.ds(start, stop - start)
            moves.append([(self.xs.at[s, tiles], self.xr.at[1 - s, tiles], peers["x"][s]) for s in (0, 1)])
        for b in range(4):
            tiles = pl.ds(0, self.band_tiles(b))
            moves.append([
                (self.zs.at[b, s, tiles], self.zr.at[b, 1 - s, tiles], peers["z"][s]) for s in (0, 1)
            ])
        self.copies = []
        for k, pair in enumerate(moves):
            self.copies.append([
                pltpu.make_async_remote_copy(
                    src_ref=src, dst_ref=dst,
                    send_sem=send_sems.at[sem_base + 2 * k + i],
                    recv_sem=recv_sems.at[sem_base + 2 * k + i],
                    device_id=where, device_id_type=MESH,
                )
                for i, (src, dst, where) in enumerate(pair)
            ])

    tile_range = Level.tile_range
    split_chunk = Level.split_chunk

    def band_tiles(self, b):
        return self.pairs + (1 if b == 0 else 0)

    def states(self, start, stop):
        states = boundary_states(lambda x: self.source[start:stop, pl.ds(x, self.nz, stride=self.nx), :], self.nx)
        for i, state in enumerate(states):
            self.xs[i // 2, start:stop, i % 2] = state

    def split_states(self, c):
        start, stop = self.chunks[c]
        rows = 2 * self.nz
        take = lambda side, t: self.xr[side, t].reshape(rows, LANES)
        if start == self.pairs:
            x = jnp.concatenate([take(side, 2 * start) for side in (0, 1)], axis=0)
            both = exact_select(x, split_matrix(LANES))
            for side in (0, 1):
                self.xe[side, 2 * start] = both[side * rows:(side + 1) * rows].reshape(2, self.nz, LANES)
            return
        order = [(side, j) for j in range(start, stop) for side in (0, 1)]
        x = jnp.concatenate([
            jnp.concatenate([take(side, 2 * j + odd) for side, j in order], axis=0) for odd in (0, 1)
        ], axis=1)
        both = exact_select(x, split_matrix(2 * LANES))
        for i, (side, j) in enumerate(order):
            for odd in (0, 1):
                part = both[i * rows:(i + 1) * rows, odd * LANES:(odd + 1) * LANES]
                self.xe[side, 2 * j + odd] = part.reshape(2, self.nz, LANES)

    def start(self, k):
        for copy in self.copies[k]:
            copy.start()

    def lift_x(self, t):
        nz, nx = self.nz, self.nx
        bands = lift(
            lambda x: self.split[t, pl.ds(x, nz, stride=nx), :], nx,
            (self.xe[0, t, 0], self.xe[0, t, 1]), (self.xe[1, t, 0], self.xe[1, t, 1]),
        )
        for band, lines in enumerate(bands):
            for i, line in enumerate(lines):
                self.own_x[band, t, pl.ds(i, nz, stride=nx // 2), :] = line

    def receive_x(self, c):
        for copy in self.copies[c]:
            copy.wait_recv()
        self.split_states(c)
        start, stop = self.tile_range(c)
        pl.loop(start, stop, unroll=min(2, stop - start))(self.lift_x)

    def lift_y(self, xb):
        count = self.nx * self.nz // 4

        def some(k):
            rows = pl.ds(pl.multiple_of(k * count, count), count)
            even, odd = circle([self.own_x[xb, t, rows, :] for t in range(2 * self.pairs + 1)])
            low, high = lift_lanes(even, odd)
            for j in range(self.band_tiles(xb)):
                self.flat[xb, j, rows, :] = low[:, j * LANES:(j + 1) * LANES]
            for j in range(self.pairs):
                self.flat[2 + xb, j, rows, :] = high[:, j * LANES:(j + 1) * LANES]

        pl.loop(0, 2)(some)

    def send_z(self, b):
        mx, n = self.nx // 2, self.band_tiles(b)
        states = boundary_states(lambda z: self.flat[b, 0:n, z * mx:(z + 1) * mx, :], self.nz)
        for i, state in enumerate(states):
            self.zs[b, i // 2, 0:n, (i % 2) * mx:(i % 2 + 1) * mx, :] = state
        self.start(len(self.chunks) + b)

    def receive_z(self, b, approx=None):
        mx = self.nx // 2
        for copy in self.copies[len(self.chunks) + b]:
            copy.wait_recv()

        n = self.band_tiles(b)
        halo = [self.zr[b, s, 0:n, i * mx:(i + 1) * mx, :] for s in (0, 1) for i in (0, 1)]
        bands = lift(lambda z: self.flat[b, 0:n, z * mx:(z + 1) * mx, :], self.nz, halo[:2], halo[2:])
        for zb, lines in enumerate(bands):
            scale = ZETA ** (3 - 2 * (zb + b // 2 + b % 2))
            for i, line in enumerate(lines):
                line = line * scale
                if zb == 0 and b == 0:
                    approx[:, i * mx:(i + 1) * mx, :] = line
                else:
                    self.details[4 * zb + b - 1, i] = jnp.concatenate([line[t] for t in range(self.pairs)], axis=1)


def first_buffers(nz, nx, pairs):
    tiles = 2 * pairs + 1
    shapes = [(tiles, nz * nx, LANES)]
    shapes += [(2, tiles, 2, nz, LANES)] * 3
    shapes += [(2, tiles, nz * nx // 2, LANES)]
    shapes += [(4, pairs + 1, nz * nx // 2, LANES)]
    shapes += [(4, 2, pairs + 1, nx, LANES)] * 2
    return [pltpu.VMEM(shape, F32) for shape in shapes]


def buffers(nz, nx, pairs):
    tiles = 2 * pairs + 1
    shapes = [(tiles, nz * nx, LANES)]
    shapes += [(tiles, 4 * nx, LANES)] * 2
    shapes += [(2, tiles, 2, nz, LANES)] * 2
    shapes += [(2, tiles, 2, 4, LANES)] * 2
    shapes += [(2, tiles, nz * nx // 2, LANES), (2, tiles, 2 * nx, LANES)]
    shapes += [(tiles, nz * nx, LANES)]
    return [pltpu.VMEM(shape, F32) for shape in shapes]


def hand_out(*refs):
    sems = refs[-1]
    n = (len(refs) - 1) // 2
    copies = [pltpu.make_async_copy(refs[i], refs[n + i], sems.at[i]) for i in range(n)]
    for copy in copies:
        copy.start()
    for copy in copies:
        copy.wait()


def kernel(sizes, axes, u_ref, one_ref, two_ref, three_ref, approx_ref, *scratch):
    scratch = list(scratch)
    send_sems, recv_sems, in_sems, raw, pack_l, pack_r, halo_l, halo_r, approx_four, approx_five = scratch[:10]
    rest = scratch[10:]
    first_refs, rest = rest[:8], rest[8:]
    per_level = len(rest) // 2
    gx, gy, gz = axes
    ix, iy, iz = (lax.axis_index(a) for a in ("gx", "gy", "gz"))
    around = lambda i, n: (lax.rem(i + n - 1, n), lax.rem(i + 1, n))
    near_x, near_y, near_z = around(ix, gx), around(iy, gy), around(iz, gz)
    peers = {
        "x": [(x, iy, iz) for x in near_x],
        "y": [(ix, y, iz) for y in near_y],
        "z": [(ix, iy, z) for z in near_z],
        "xz": [[(x, iy, z) for z in near_z] for x in near_x],
    }
    (nz, nx, pairs) = sizes[0]
    tiles = 2 * pairs

    loads = [
        pltpu.make_async_copy(u_ref.at[:, :, pl.ds(t * LANES, LANES)], raw.at[t], in_sems.at[t])
        for t in range(tiles)
    ]
    order = [0, tiles - 1] + list(range(1, tiles - 1))
    for t in order:
        loads[t].start()

    barrier = pltpu.get_barrier_semaphore()
    greeted = peers["x"] + peers["y"] + peers["z"] + peers["xz"][0] + peers["xz"][1]
    for where in greeted:
        pl.semaphore_signal(barrier, inc=1, device_id=where, device_id_type=MESH)

    half = pairs // 2
    sems = (send_sems, recv_sems)
    chunks = [(0, half), (half, pairs), (pairs, pairs + 1)]
    first = FirstLevel(nz, nx, pairs, raw.reshape(tiles + 1, nz * nx, LANES), first_refs, one_ref, sems, 2, peers, chunks)
    second, third = (
        Level(i, *sizes[i], source, rest[(i - 1) * per_level:i * per_level], details, sems, 8 + 8 * i, peers,
              [(0, sizes[i][2] + 1)])
        for i, source, details in ((1, approx_four, two_ref), (2, approx_five, three_ref))
    )

    groups = LANES // HALO
    part = nz * nx // groups
    lane = lax.broadcasted_iota(jnp.int32, (part, LANES), 1)
    loads[0].wait()
    loads[tiles - 1].wait()
    flat = first.source

    def gather(tile, offset):
        total = None
        for g in range(groups):
            rows = pltpu.roll(flat[tile, g * part:(g + 1) * part, :], (g * HALO - offset) % LANES, 1)
            total = rows if total is None else jnp.where(lane >= g * HALO, rows, total)
        return total

    pack_l[...] = gather(0, 0)
    pack_r[...] = gather(tiles - 1, LANES - HALO)
    pl.semaphore_wait(barrier, len(greeted))
    y_copies = [
        pltpu.make_async_remote_copy(src_ref=src, dst_ref=dst, send_sem=send_sems.at[i], recv_sem=recv_sems.at[i],
                                     device_id=where, device_id_type=MESH)
        for i, (src, dst, where) in enumerate(((pack_l, halo_r, peers["y"][0]), (pack_r, halo_l, peers["y"][1])))
    ]
    for copy in y_copies:
        copy.start()
    for t in range(1, tiles - 1):
        loads[t].wait()
    first.states(0, 2 * half)
    first.start(0)
    first.states(2 * half, tiles)
    first.start(1)
    first.split_chunk(0)
    for copy in y_copies:
        copy.wait_recv()
    for g in range(groups):
        after = pltpu.roll(halo_r[...], (-g * HALO) % LANES, 1)
        before = pltpu.roll(halo_l[...], (LANES - HALO - g * HALO) % LANES, 1)
        flat[tiles, g * part:(g + 1) * part, :] = jnp.where(
            lane < HALO, after, jnp.where(lane >= LANES - HALO, before, 0.0)
        )
    first.states(tiles, tiles + 1)
    first.start(2)
    first.split_chunk(1)
    first.split_chunk(2)
    for c in range(3):
        first.receive_x(c)
    first.lift_y(0)
    first.send_z(0)
    first.send_z(2)
    first.lift_y(1)
    first.receive_z(0, approx_four)

    second.prepare(0)
    second.send(0)
    first.send_z(1)
    first.send_z(3)
    first.receive_z(2)
    second.receive(0)
    second.lines([0], approx_five)

    third.prepare(0)
    third.send(0)
    second.lines([1, 2, 3])
    first.receive_z(1)
    first.receive_z(3)
    third.receive(0)
    third.lines([0, 1, 2, 3], approx_ref)

    for copy in y_copies:
        copy.wait_send()
    for level in (first, second, third):
        for copies in level.copies:
            for copy in copies:
                copy.wait_send()


def solution(mesh):
    axes = tuple(mesh.shape[a] for a in ("gx", "gy", "gz"))

    def on_device(density):
        nz, nx, ny = density.shape
        sizes = [(nz >> i, nx >> i, (ny >> i) // (2 * LANES)) for i in range(3)]
        tiles = ny // LANES
        shapes = [(7, z // 2, x // 2, p * LANES) for z, x, p in sizes]
        shapes.append(shapes[-1][1:])
        n_sems = 32
        packed = (nz * nx * HALO // LANES, LANES)
        scratch = [
            pltpu.SemaphoreType.DMA((n_sems,)),
            pltpu.SemaphoreType.DMA((n_sems,)),
            pltpu.SemaphoreType.DMA((tiles,)),
            pltpu.VMEM((tiles + 1, nz, nx, LANES), F32),
        ]
        scratch += [pltpu.VMEM(packed, F32)] * 4
        for z, x, p in sizes[:2]:
            scratch.append(pltpu.VMEM((p + 1, z * x // 4, LANES), F32))
        scratch += first_buffers(*sizes[0])
        for z, x, p in sizes[1:]:
            scratch += buffers(z, x, p)
        outs = [jax.ShapeDtypeStruct(shape, F32) for shape in shapes]
        results = pl.pallas_call(
            functools.partial(kernel, sizes, axes),
            out_shape=[pltpu.VMEM(shape, F32) for shape in shapes],
            in_specs=[pl.BlockSpec(memory_space=pltpu.HBM)],
            out_specs=[pl.BlockSpec(memory_space=pltpu.VMEM)] * 4,
            scratch_shapes=scratch,
            compiler_params=pltpu.CompilerParams(
                collective_id=0, has_side_effects=True, vmem_limit_bytes=59 << 20
            ),
            cost_estimate=pl.CostEstimate(flops=20_000_000, bytes_accessed=2 << 20, transcendentals=0),
        )(density)
        return pl.pallas_call(
            hand_out,
            out_shape=outs,
            in_specs=[pl.BlockSpec(memory_space=pltpu.VMEM)] * 4,
            out_specs=[pl.BlockSpec(memory_space=pltpu.HBM)] * 4,
            scratch_shapes=[pltpu.SemaphoreType.DMA((4,))],
            compiler_params=pltpu.CompilerParams(vmem_limit_bytes=1 << 20),
            cost_estimate=pl.CostEstimate(flops=0, bytes_accessed=2 << 20, transcendentals=0),
        )(*results)

    return jax.shard_map(
        on_device,
        mesh=mesh,
        in_specs=(P("gz", "gx", "gy"),),
        out_specs=(
            P(None, "gz", "gx", "gy"),
            P(None, "gz", "gx", "gy"),
            P(None, "gz", "gx", "gy"),
            P("gz", "gx", "gy"),
        ),
        check_vma=False,
    )
```

```python
import functools

import jax
import jax.numpy as jnp
from jax import lax
from jax.experimental import pallas as pl
from jax.experimental.pallas import tpu as pltpu
from jax.sharding import PartitionSpec as P

ALPHA = -1.586134342
BETA = -0.05298011854
GAMMA = 0.8829110762
DELTA = 0.4435068522
ZETA = 1.149604398

MESH = pl.DeviceIdType.MESH
LANES = 128
HALO = 32
F32 = jnp.float32
BF16 = jnp.bfloat16


def boundary_states(get, n):
    s0, last_s = get(0), get(n - 2)
    lead = get(1) + ALPHA * (s0 + get(2))
    trail = get(n - 3) + ALPHA * (get(n - 4) + last_s)
    return s0, s0 + BETA * lead, get(n - 1) + ALPHA * last_s, last_s + BETA * trail


def lift(get, n, from_left, from_right):
    m = n // 2
    s = [get(2 * i) for i in range(m)]
    d = [get(2 * i + 1) for i in range(m)]
    r, q = from_left
    s_next, p = from_right
    d1 = [r + ALPHA * s[0]]
    for i in range(m):
        d1.append(d[i] + ALPHA * (s[i] + (s[i + 1] if i + 1 < m else s_next)))
    s1 = [q + BETA * d1[0]]
    for i in range(m):
        s1.append(s[i] + BETA * (d1[i] + d1[i + 1]))
    s1.append(p + BETA * d1[m])
    d2 = [d1[i] + GAMMA * (s1[i] + s1[i + 1]) for i in range(m + 1)]
    low = [s1[i + 1] + DELTA * (d2[i] + d2[i + 1]) for i in range(m)]
    return low, d2[1:]


def lift_lanes(even, odd):
    width = even.shape[-1]
    after = lambda v: pltpu.roll(v, width - 1, 1)
    before = lambda v: pltpu.roll(v, 1, 1)
    d = odd + ALPHA * (even + after(even))
    s = even + BETA * (before(d) + d)
    d = d + GAMMA * (s + after(s))
    s = s + DELTA * (before(d) + d)
    return s, d


def circle(tiles):
    ends = tiles[-1]
    turned = pltpu.roll(ends, LANES // 2, 1)
    near = lax.broadcasted_iota(jnp.int32, ends.shape, 1) < LANES // 2
    even = jnp.concatenate(tiles[0:-1:2] + [jnp.where(near, ends, turned)], axis=1)
    odd = jnp.concatenate(tiles[1:-1:2] + [jnp.where(near, turned, ends)], axis=1)
    return even, odd


def exact_select(x, choose):
    parts = []
    for _ in range(3):
        parts.append(x.astype(BF16))
        x = x - parts[-1].astype(F32)
    terms = jnp.dot(jnp.concatenate(parts, axis=0), choose, preferred_element_type=F32)
    n = x.shape[0]
    return terms[:n] + terms[n:2 * n] + terms[2 * n:]


def split_matrix(depth):
    k = lax.broadcasted_iota(jnp.int32, (depth, depth), 0)
    n = lax.broadcasted_iota(jnp.int32, (depth, depth), 1)
    return (k == jnp.where(n < depth // 2, 2 * n, 2 * n - depth + 1)).astype(BF16)


class Level:
    def __init__(self, index, nz, nx, pairs, source, refs, details, sems, sem_base, peers, chunks):
        self.index, self.nz, self.nx, self.pairs = index, nz, nx, pairs
        self.source = source
        (self.split, self.zs, self.zr, self.xs, self.xr, self.cs, self.cr,
         self.own_x, self.halo_x, self.both) = refs
        self.details = details
        self.send_sems, self.recv_sems = sems
        self.peers = peers
        self.chunks = chunks
        self.sem_base = sem_base
        self.copies = [self.make_copies(c) for c in range(len(chunks))]

    def tile_range(self, c):
        start, stop = self.chunks[c]
        return 2 * start, min(2 * stop, 2 * self.pairs + 1)

    def make_copies(self, c):
        start, stop = self.tile_range(c)
        tiles = pl.ds(start, stop - start)
        p = self.peers
        side = 2 * self.nx
        moves = [
            (self.zs.at[tiles, pl.ds(sz * side, side)], self.zr.at[tiles, pl.ds((1 - sz) * side, side)], p["z"][sz])
            for sz in (0, 1)
        ]
        for sx in (0, 1):
            for sz in (0, 1):
                moves.append((self.cs.at[sx, tiles, :, pl.ds(2 * sz, 2)],
                              self.cr.at[1 - sx, tiles, :, pl.ds(2 - 2 * sz, 2)], p["xz"][sx][sz]))
        for sx in (0, 1):
            moves.append((self.xs.at[sx, tiles], self.xr.at[1 - sx, tiles], p["x"][sx]))
        return [
            pltpu.make_async_remote_copy(
                src_ref=src, dst_ref=dst,
                send_sem=self.send_sems.at[self.sem_base + 8 * c + i],
                recv_sem=self.recv_sems.at[self.sem_base + 8 * c + i],
                device_id=where, device_id_type=MESH,
            )
            for i, (src, dst, where) in enumerate(moves)
        ]

    def split_chunk(self, c):
        start, stop = self.chunks[c]
        main = min(stop, self.pairs)
        rows = self.nz * self.nx
        if start == self.pairs:
            self.split[2 * start] = exact_select(self.source[2 * start], split_matrix(LANES))
            return
        firsts = [self.source[2 * j] for j in range(start, stop)]
        seconds = [self.source[2 * j + 1 if j < main else 2 * j] for j in range(start, stop)]
        x = jnp.concatenate([jnp.concatenate(firsts, axis=0), jnp.concatenate(seconds, axis=0)], axis=1)
        both = exact_select(x, split_matrix(2 * LANES))
        for i, j in enumerate(range(start, stop)):
            even = both[i * rows:(i + 1) * rows, :LANES]
            odd = both[i * rows:(i + 1) * rows, LANES:]
            if j < main:
                self.split[2 * j] = even
                self.split[2 * j + 1] = odd
            else:
                lane = lax.broadcasted_iota(jnp.int32, (rows, LANES), 1)
                self.split[2 * j] = jnp.where(lane < LANES // 2, even, odd)

    def prepare(self, c):
        self.split_chunk(c)
        nz, nx = self.nz, self.nx
        states = boundary_states(lambda z: self.split[:, z * nx:(z + 1) * nx, :], nz)
        for i, state in enumerate(states):
            self.zs[:, i * nx:(i + 1) * nx, :] = state
        states = boundary_states(lambda x: self.split[:, pl.ds(x, nz, stride=nx), :], nx)
        for i, state in enumerate(states):
            self.xs[i // 2, :, i % 2] = state
        states = boundary_states(lambda x: self.zs[:, pl.ds(x, 4, stride=nx), :], nx)
        for i, state in enumerate(states):
            self.cs[i // 2, :, i % 2] = state

    def send(self, c):
        for copy in self.copies[c]:
            copy.start()

    def receive(self, c):
        for copy in self.copies[c]:
            copy.wait_recv()
        nz, nx = self.nz, self.nx
        mx = nx // 2
        band_rows = nz * nx // 4
        for ref, n, source, ends in ((self.own_x, nz, self.split, self.xr), (self.halo_x, 4, self.zr, self.cr)):
            bands = lift(
                lambda x: source[:, pl.ds(x, n, stride=nx), :], nx,
                (ends[0, :, 0], ends[0, :, 1]), (ends[1, :, 0], ends[1, :, 1]),
            )
            for band, lines in enumerate(bands):
                for i, line in enumerate(lines):
                    ref[band, :, pl.ds(i, n, stride=mx), :] = line
        for xb in (0, 1):
            halo = [self.halo_x[xb, :, i * mx:(i + 1) * mx, :] for i in range(4)]
            bands = lift(lambda z: self.own_x[xb, :, z * mx:(z + 1) * mx, :], nz, halo[:2], halo[2:])
            for zb, lines in enumerate(bands):
                for i, line in enumerate(lines):
                    row = (2 * zb + xb) * band_rows + i * mx
                    self.both[:, row:row + mx, :] = line

    def lines(self, bands, approx=None):
        mx, mz = self.nx // 2, self.nz // 2
        band_rows = mx * mz
        first, last = bands[0], bands[-1] + 1
        even, odd = circle([self.both[t, first * band_rows:last * band_rows, :] for t in range(2 * self.pairs + 1)])
        lows, highs = lift_lanes(even, odd)
        width = self.pairs * LANES
        for k, band in enumerate(bands):
            zb, xb = band // 2, band % 2
            rows = slice(k * band_rows, (k + 1) * band_rows)
            low = lows[rows] * ZETA ** (3 - 2 * (zb + xb))
            high = highs[rows, :width] * ZETA ** (1 - 2 * (zb + xb))
            if band == 0 and self.index < 2:
                for j in range(self.pairs + 1):
                    approx[j] = low[:, j * LANES:(j + 1) * LANES]
            for i in range(mz):
                row = low[i * mx:(i + 1) * mx, :width]
                if band > 0:
                    self.details[4 * zb + xb - 1, i] = row
                elif self.index == 2:
                    approx[i] = row
                self.details[4 * zb + 2 + xb - 1, i] = high[i * mx:(i + 1) * mx]


class FirstLevel:
    def __init__(self, nz, nx, pairs, source, refs, details, sems, sem_base, peers, chunks):
        self.nz, self.nx, self.pairs, self.source, self.details = nz, nx, pairs, source, details
        self.split, self.xs, self.xr, self.xe, self.own_x, self.flat, self.zs, self.zr = refs
        self.chunks = chunks
        send_sems, recv_sems = sems
        moves = []
        for c in range(len(chunks)):
            start, stop = self.tile_range(c)
            tiles = pl.ds(start, stop - start)
            moves.append([(self.xs.at[s, tiles], self.xr.at[1 - s, tiles], peers["x"][s]) for s in (0, 1)])
        for b in range(4):
            tiles = pl.ds(0, self.band_tiles(b))
            moves.append([
                (self.zs.at[b, s, tiles], self.zr.at[b, 1 - s, tiles], peers["z"][s]) for s in (0, 1)
            ])
        self.copies = []
        for k, pair in enumerate(moves):
            self.copies.append([
                pltpu.make_async_remote_copy(
                    src_ref=src, dst_ref=dst,
                    send_sem=send_sems.at[sem_base + 2 * k + i],
                    recv_sem=recv_sems.at[sem_base + 2 * k + i],
                    device_id=where, device_id_type=MESH,
                )
                for i, (src, dst, where) in enumerate(pair)
            ])

    tile_range = Level.tile_range
    split_chunk = Level.split_chunk

    def band_tiles(self, b):
        return self.pairs + (1 if b == 0 else 0)

    def states(self, start, stop):
        states = boundary_states(lambda x: self.source[start:stop, pl.ds(x, self.nz, stride=self.nx), :], self.nx)
        for i, state in enumerate(states):
            self.xs[i // 2, start:stop, i % 2] = state

    def split_states(self, c):
        start, stop = self.chunks[c]
        rows = 2 * self.nz
        take = lambda side, t: self.xr[side, t].reshape(rows, LANES)
        if start == self.pairs:
            x = jnp.concatenate([take(side, 2 * start) for side in (0, 1)], axis=0)
            both = exact_select(x, split_matrix(LANES))
            for side in (0, 1):
                self.xe[side, 2 * start] = both[side * rows:(side + 1) * rows].reshape(2, self.nz, LANES)
            return
        order = [(side, j) for j in range(start, stop) for side in (0, 1)]
        x = jnp.concatenate([
            jnp.concatenate([take(side, 2 * j + odd) for side, j in order], axis=0) for odd in (0, 1)
        ], axis=1)
        both = exact_select(x, split_matrix(2 * LANES))
        for i, (side, j) in enumerate(order):
            for odd in (0, 1):
                part = both[i * rows:(i + 1) * rows, odd * LANES:(odd + 1) * LANES]
                self.xe[side, 2 * j + odd] = part.reshape(2, self.nz, LANES)

    def start(self, k):
        for copy in self.copies[k]:
            copy.start()

    def lift_x(self, t):
        nz, nx = self.nz, self.nx
        bands = lift(
            lambda x: self.split[t, pl.ds(x, nz, stride=nx), :], nx,
            (self.xe[0, t, 0], self.xe[0, t, 1]), (self.xe[1, t, 0], self.xe[1, t, 1]),
        )
        for band, lines in enumerate(bands):
            for i, line in enumerate(lines):
                self.own_x[band, t, pl.ds(i, nz, stride=nx // 2), :] = line

    def receive_x(self, c):
        for copy in self.copies[c]:
            copy.wait_recv()
        self.split_states(c)
        start, stop = self.tile_range(c)
        pl.loop(start, stop, unroll=min(2, stop - start))(self.lift_x)

    def lift_y(self, xb):
        count = self.nx * self.nz // 4

        def some(k):
            rows = pl.ds(pl.multiple_of(k * count, count), count)
            even, odd = circle([self.own_x[xb, t, rows, :] for t in range(2 * self.pairs + 1)])
            low, high = lift_lanes(even, odd)
            for j in range(self.band_tiles(xb)):
                self.flat[xb, j, rows, :] = low[:, j * LANES:(j + 1) * LANES]
            for j in range(self.pairs):
                self.flat[2 + xb, j, rows, :] = high[:, j * LANES:(j + 1) * LANES]

        pl.loop(0, 2)(some)

    def states_z(self, b):
        mx, n = self.nx // 2, self.band_tiles(b)
        states = boundary_states(lambda z: self.flat[b, 0:n, z * mx:(z + 1) * mx, :], self.nz)
        for i, state in enumerate(states):
            self.zs[b, i // 2, 0:n, (i % 2) * mx:(i % 2 + 1) * mx, :] = state

    def send_z(self, b):
        self.start(len(self.chunks) + b)

    def receive_z(self, b, approx=None):
        mx = self.nx // 2
        for copy in self.copies[len(self.chunks) + b]:
            copy.wait_recv()

        n = self.band_tiles(b)
        halo = [self.zr[b, s, 0:n, i * mx:(i + 1) * mx, :] for s in (0, 1) for i in (0, 1)]
        bands = lift(lambda z: self.flat[b, 0:n, z * mx:(z + 1) * mx, :], self.nz, halo[:2], halo[2:])
        for zb, lines in enumerate(bands):
            scale = ZETA ** (3 - 2 * (zb + b // 2 + b % 2))
            for i, line in enumerate(lines):
                line = line * scale
                if zb == 0 and b == 0:
                    approx[:, i * mx:(i + 1) * mx, :] = line
                else:
                    self.details[4 * zb + b - 1, i] = jnp.concatenate([line[t] for t in range(self.pairs)], axis=1)


def first_buffers(nz, nx, pairs):
    tiles = 2 * pairs + 1
    shapes = [(tiles, nz * nx, LANES)]
    shapes += [(2, tiles, 2, nz, LANES)] * 3
    shapes += [(2, tiles, nz * nx // 2, LANES)]
    shapes += [(4, pairs + 1, nz * nx // 2, LANES)]
    shapes += [(4, 2, pairs + 1, nx, LANES)] * 2
    return [pltpu.VMEM(shape, F32) for shape in shapes]


def buffers(nz, nx, pairs):
    tiles = 2 * pairs + 1
    shapes = [(tiles, nz * nx, LANES)]
    shapes += [(tiles, 4 * nx, LANES)] * 2
    shapes += [(2, tiles, 2, nz, LANES)] * 2
    shapes += [(2, tiles, 2, 4, LANES)] * 2
    shapes += [(2, tiles, nz * nx // 2, LANES), (2, tiles, 2 * nx, LANES)]
    shapes += [(tiles, nz * nx, LANES)]
    return [pltpu.VMEM(shape, F32) for shape in shapes]


def hand_out(*refs):
    sems = refs[-1]
    n = (len(refs) - 1) // 2
    copies = [pltpu.make_async_copy(refs[i], refs[n + i], sems.at[i]) for i in range(n)]
    for copy in copies:
        copy.start()
    for copy in copies:
        copy.wait()


def kernel(sizes, axes, u_ref, one_ref, two_ref, three_ref, approx_ref, *scratch):
    scratch = list(scratch)
    send_sems, recv_sems, in_sems, raw, pack_l, pack_r, halo_l, halo_r, approx_four, approx_five = scratch[:10]
    rest = scratch[10:]
    first_refs, rest = rest[:8], rest[8:]
    per_level = len(rest) // 2
    gx, gy, gz = axes
    ix, iy, iz = (lax.axis_index(a) for a in ("gx", "gy", "gz"))
    around = lambda i, n: (lax.rem(i + n - 1, n), lax.rem(i + 1, n))
    near_x, near_y, near_z = around(ix, gx), around(iy, gy), around(iz, gz)
    peers = {
        "x": [(x, iy, iz) for x in near_x],
        "y": [(ix, y, iz) for y in near_y],
        "z": [(ix, iy, z) for z in near_z],
        "xz": [[(x, iy, z) for z in near_z] for x in near_x],
    }
    (nz, nx, pairs) = sizes[0]
    tiles = 2 * pairs

    loads = [
        pltpu.make_async_copy(u_ref.at[:, :, pl.ds(t * LANES, LANES)], raw.at[t], in_sems.at[t])
        for t in range(tiles)
    ]
    order = [0, tiles - 1] + list(range(1, tiles - 1))
    for t in order:
        loads[t].start()

    barrier = pltpu.get_barrier_semaphore()
    greeted = peers["x"] + peers["y"] + peers["z"] + peers["xz"][0] + peers["xz"][1]
    for where in greeted:
        pl.semaphore_signal(barrier, inc=1, device_id=where, device_id_type=MESH)

    half = pairs // 2
    sems = (send_sems, recv_sems)
    chunks = [(0, half), (half, pairs), (pairs, pairs + 1)]
    first = FirstLevel(nz, nx, pairs, raw.reshape(tiles + 1, nz * nx, LANES), first_refs, one_ref, sems, 2, peers, chunks)
    second, third = (
        Level(i, *sizes[i], source, rest[(i - 1) * per_level:i * per_level], details, sems, 8 + 8 * i, peers,
              [(0, sizes[i][2] + 1)])
        for i, source, details in ((1, approx_four, two_ref), (2, approx_five, three_ref))
    )

    groups = LANES // HALO
    part = nz * nx // groups
    lane = lax.broadcasted_iota(jnp.int32, (part, LANES), 1)
    loads[0].wait()
    loads[tiles - 1].wait()
    flat = first.source

    def gather(tile, offset):
        total = None
        for g in range(groups):
            rows = pltpu.roll(flat[tile, g * part:(g + 1) * part, :], (g * HALO - offset) % LANES, 1)
            total = rows if total is None else jnp.where(lane >= g * HALO, rows, total)
        return total

    pack_l[...] = gather(0, 0)
    pack_r[...] = gather(tiles - 1, LANES - HALO)
    pl.semaphore_wait(barrier, len(greeted))
    y_copies = [
        pltpu.make_async_remote_copy(src_ref=src, dst_ref=dst, send_sem=send_sems.at[i], recv_sem=recv_sems.at[i],
                                     device_id=where, device_id_type=MESH)
        for i, (src, dst, where) in enumerate(((pack_l, halo_r, peers["y"][0]), (pack_r, halo_l, peers["y"][1])))
    ]
    for copy in y_copies:
        copy.start()
    for t in range(1, tiles - 1):
        loads[t].wait()
    first.states(0, 2 * half)
    first.start(0)
    first.states(2 * half, tiles)
    first.start(1)
    first.split_chunk(0)
    for copy in y_copies:
        copy.wait_recv()
    for g in range(groups):
        after = pltpu.roll(halo_r[...], (-g * HALO) % LANES, 1)
        before = pltpu.roll(halo_l[...], (LANES - HALO - g * HALO) % LANES, 1)
        flat[tiles, g * part:(g + 1) * part, :] = jnp.where(
            lane < HALO, after, jnp.where(lane >= LANES - HALO, before, 0.0)
        )
    first.states(tiles, tiles + 1)
    first.start(2)
    first.split_chunk(1)
    first.split_chunk(2)
    for c in range(3):
        first.receive_x(c)
    first.lift_y(0)
    first.states_z(0)
    first.send_z(0)
    first.lift_y(1)
    first.states_z(2)
    first.send_z(2)
    first.receive_z(0, approx_four)

    second.prepare(0)
    second.send(0)
    first.states_z(1)
    first.states_z(3)
    first.receive_z(2)
    first.send_z(1)
    second.receive(0)
    first.send_z(3)
    second.lines([0], approx_five)

    third.prepare(0)
    third.send(0)
    second.lines([1, 2, 3])
    first.receive_z(1)
    first.receive_z(3)
    third.receive(0)
    third.lines([0, 1, 2, 3], approx_ref)

    for copy in y_copies:
        copy.wait_send()
    for level in (first, second, third):
        for copies in level.copies:
            for copy in copies:
                copy.wait_send()


def solution(mesh):
    axes = tuple(mesh.shape[a] for a in ("gx", "gy", "gz"))

    def on_device(density):
        nz, nx, ny = density.shape
        sizes = [(nz >> i, nx >> i, (ny >> i) // (2 * LANES)) for i in range(3)]
        tiles = ny // LANES
        shapes = [(7, z // 2, x // 2, p * LANES) for z, x, p in sizes]
        shapes.append(shapes[-1][1:])
        n_sems = 32
        packed = (nz * nx * HALO // LANES, LANES)
        scratch = [
            pltpu.SemaphoreType.DMA((n_sems,)),
            pltpu.SemaphoreType.DMA((n_sems,)),
            pltpu.SemaphoreType.DMA((tiles,)),
            pltpu.VMEM((tiles + 1, nz, nx, LANES), F32),
        ]
        scratch += [pltpu.VMEM(packed, F32)] * 4
        for z, x, p in sizes[:2]:
            scratch.append(pltpu.VMEM((p + 1, z * x // 4, LANES), F32))
        scratch += first_buffers(*sizes[0])
        for z, x, p in sizes[1:]:
            scratch += buffers(z, x, p)
        outs = [jax.ShapeDtypeStruct(shape, F32) for shape in shapes]
        results = pl.pallas_call(
            functools.partial(kernel, sizes, axes),
            out_shape=[pltpu.VMEM(shape, F32) for shape in shapes],
            in_specs=[pl.BlockSpec(memory_space=pltpu.HBM)],
            out_specs=[pl.BlockSpec(memory_space=pltpu.VMEM)] * 4,
            scratch_shapes=scratch,
            compiler_params=pltpu.CompilerParams(
                collective_id=0, has_side_effects=True, vmem_limit_bytes=59 << 20
            ),
            cost_estimate=pl.CostEstimate(flops=20_000_000, bytes_accessed=2 << 20, transcendentals=0),
        )(density)
        return pl.pallas_call(
            hand_out,
            out_shape=outs,
            in_specs=[pl.BlockSpec(memory_space=pltpu.VMEM)] * 4,
            out_specs=[pl.BlockSpec(memory_space=pltpu.HBM)] * 4,
            scratch_shapes=[pltpu.SemaphoreType.DMA((4,))],
            compiler_params=pltpu.CompilerParams(vmem_limit_bytes=1 << 20),
            cost_estimate=pl.CostEstimate(flops=0, bytes_accessed=2 << 20, transcendentals=0),
        )(*results)

    return jax.shard_map(
        on_device,
        mesh=mesh,
        in_specs=(P("gz", "gx", "gy"),),
        out_specs=(
            P(None, "gz", "gx", "gy"),
            P(None, "gz", "gx", "gy"),
            P(None, "gz", "gx", "gy"),
            P("gz", "gx", "gy"),
        ),
        check_vma=False,
    )
```

```python
import functools

import jax
import jax.numpy as jnp
from jax import lax
from jax.experimental import pallas as pl
from jax.experimental.pallas import tpu as pltpu
from jax.sharding import PartitionSpec as P

ALPHA = -1.586134342
BETA = -0.05298011854
GAMMA = 0.8829110762
DELTA = 0.4435068522
ZETA = 1.149604398

MESH = pl.DeviceIdType.MESH
LANES = 128
HALO = 32
F32 = jnp.float32
BF16 = jnp.bfloat16


def boundary_states(get, n):
    s0, last_s = get(0), get(n - 2)
    lead = get(1) + ALPHA * (s0 + get(2))
    trail = get(n - 3) + ALPHA * (get(n - 4) + last_s)
    return s0, s0 + BETA * lead, get(n - 1) + ALPHA * last_s, last_s + BETA * trail


def lift(get, n, from_left, from_right):
    m = n // 2
    s = [get(2 * i) for i in range(m)]
    d = [get(2 * i + 1) for i in range(m)]
    r, q = from_left
    s_next, p = from_right
    d1 = [r + ALPHA * s[0]]
    for i in range(m):
        d1.append(d[i] + ALPHA * (s[i] + (s[i + 1] if i + 1 < m else s_next)))
    s1 = [q + BETA * d1[0]]
    for i in range(m):
        s1.append(s[i] + BETA * (d1[i] + d1[i + 1]))
    s1.append(p + BETA * d1[m])
    d2 = [d1[i] + GAMMA * (s1[i] + s1[i + 1]) for i in range(m + 1)]
    low = [s1[i + 1] + DELTA * (d2[i] + d2[i + 1]) for i in range(m)]
    return low, d2[1:]


def lift_lanes(even, odd):
    width = even.shape[-1]
    after = lambda v: pltpu.roll(v, width - 1, 1)
    before = lambda v: pltpu.roll(v, 1, 1)
    d = odd + ALPHA * (even + after(even))
    s = even + BETA * (before(d) + d)
    d = d + GAMMA * (s + after(s))
    s = s + DELTA * (before(d) + d)
    return s, d


def circle(tiles):
    ends = tiles[-1]
    turned = pltpu.roll(ends, LANES // 2, 1)
    near = lax.broadcasted_iota(jnp.int32, ends.shape, 1) < LANES // 2
    even = jnp.concatenate(tiles[0:-1:2] + [jnp.where(near, ends, turned)], axis=1)
    odd = jnp.concatenate(tiles[1:-1:2] + [jnp.where(near, turned, ends)], axis=1)
    return even, odd


def exact_select(x, choose):
    parts = []
    for _ in range(3):
        parts.append(x.astype(BF16))
        x = x - parts[-1].astype(F32)
    terms = jnp.dot(jnp.concatenate(parts, axis=0), choose, preferred_element_type=F32)
    n = x.shape[0]
    return terms[:n] + terms[n:2 * n] + terms[2 * n:]


def split_matrix(depth):
    k = lax.broadcasted_iota(jnp.int32, (depth, depth), 0)
    n = lax.broadcasted_iota(jnp.int32, (depth, depth), 1)
    return (k == jnp.where(n < depth // 2, 2 * n, 2 * n - depth + 1)).astype(BF16)


class Level:
    def __init__(self, index, nz, nx, pairs, source, refs, details, sems, sem_base, peers, chunks):
        self.index, self.nz, self.nx, self.pairs = index, nz, nx, pairs
        self.source = source
        (self.split, self.zs, self.zr, self.xs, self.xr, self.cs, self.cr,
         self.own_x, self.halo_x, self.both) = refs
        self.details = details
        self.send_sems, self.recv_sems = sems
        self.peers = peers
        self.chunks = chunks
        self.sem_base = sem_base
        self.copies = [self.make_copies(c) for c in range(len(chunks))]

    def tile_range(self, c):
        start, stop = self.chunks[c]
        return 2 * start, min(2 * stop, 2 * self.pairs + 1)

    def make_copies(self, c):
        start, stop = self.tile_range(c)
        tiles = pl.ds(start, stop - start)
        p = self.peers
        side = 2 * self.nx
        moves = [
            (self.zs.at[tiles, pl.ds(sz * side, side)], self.zr.at[tiles, pl.ds((1 - sz) * side, side)], p["z"][sz])
            for sz in (0, 1)
        ]
        for sx in (0, 1):
            for sz in (0, 1):
                moves.append((self.cs.at[sx, tiles, :, pl.ds(2 * sz, 2)],
                              self.cr.at[1 - sx, tiles, :, pl.ds(2 - 2 * sz, 2)], p["xz"][sx][sz]))
        for sx in (0, 1):
            moves.append((self.xs.at[sx, tiles], self.xr.at[1 - sx, tiles], p["x"][sx]))
        return [
            pltpu.make_async_remote_copy(
                src_ref=src, dst_ref=dst,
                send_sem=self.send_sems.at[self.sem_base + 8 * c + i],
                recv_sem=self.recv_sems.at[self.sem_base + 8 * c + i],
                device_id=where, device_id_type=MESH,
            )
            for i, (src, dst, where) in enumerate(moves)
        ]

    def split_chunk(self, c):
        start, stop = self.chunks[c]
        main = min(stop, self.pairs)
        rows = self.nz * self.nx
        if start == self.pairs:
            self.split[2 * start] = exact_select(self.source[2 * start], split_matrix(LANES))
            return
        firsts = [self.source[2 * j] for j in range(start, stop)]
        seconds = [self.source[2 * j + 1 if j < main else 2 * j] for j in range(start, stop)]
        x = jnp.concatenate([jnp.concatenate(firsts, axis=0), jnp.concatenate(seconds, axis=0)], axis=1)
        both = exact_select(x, split_matrix(2 * LANES))
        for i, j in enumerate(range(start, stop)):
            even = both[i * rows:(i + 1) * rows, :LANES]
            odd = both[i * rows:(i + 1) * rows, LANES:]
            if j < main:
                self.split[2 * j] = even
                self.split[2 * j + 1] = odd
            else:
                lane = lax.broadcasted_iota(jnp.int32, (rows, LANES), 1)
                self.split[2 * j] = jnp.where(lane < LANES // 2, even, odd)

    def prepare(self, c):
        self.split_chunk(c)
        nz, nx = self.nz, self.nx
        states = boundary_states(lambda z: self.split[:, z * nx:(z + 1) * nx, :], nz)
        for i, state in enumerate(states):
            self.zs[:, i * nx:(i + 1) * nx, :] = state
        states = boundary_states(lambda x: self.split[:, pl.ds(x, nz, stride=nx), :], nx)
        for i, state in enumerate(states):
            self.xs[i // 2, :, i % 2] = state
        states = boundary_states(lambda x: self.zs[:, pl.ds(x, 4, stride=nx), :], nx)
        for i, state in enumerate(states):
            self.cs[i // 2, :, i % 2] = state

    def send(self, c):
        for copy in self.copies[c]:
            copy.start()

    def receive(self, c):
        for copy in self.copies[c]:
            copy.wait_recv()
        nz, nx = self.nz, self.nx
        mx = nx // 2
        band_rows = nz * nx // 4
        for ref, n, source, ends in ((self.own_x, nz, self.split, self.xr), (self.halo_x, 4, self.zr, self.cr)):
            bands = lift(
                lambda x: source[:, pl.ds(x, n, stride=nx), :], nx,
                (ends[0, :, 0], ends[0, :, 1]), (ends[1, :, 0], ends[1, :, 1]),
            )
            for band, lines in enumerate(bands):
                for i, line in enumerate(lines):
                    ref[band, :, pl.ds(i, n, stride=mx), :] = line
        for xb in (0, 1):
            halo = [self.halo_x[xb, :, i * mx:(i + 1) * mx, :] for i in range(4)]
            bands = lift(lambda z: self.own_x[xb, :, z * mx:(z + 1) * mx, :], nz, halo[:2], halo[2:])
            for zb, lines in enumerate(bands):
                for i, line in enumerate(lines):
                    row = (2 * zb + xb) * band_rows + i * mx
                    self.both[:, row:row + mx, :] = line

    def lines(self, bands, approx=None):
        mx, mz = self.nx // 2, self.nz // 2
        band_rows = mx * mz
        first, last = bands[0], bands[-1] + 1
        even, odd = circle([self.both[t, first * band_rows:last * band_rows, :] for t in range(2 * self.pairs + 1)])
        lows, highs = lift_lanes(even, odd)
        width = self.pairs * LANES
        for k, band in enumerate(bands):
            zb, xb = band // 2, band % 2
            rows = slice(k * band_rows, (k + 1) * band_rows)
            low = lows[rows] * ZETA ** (3 - 2 * (zb + xb))
            high = highs[rows, :width] * ZETA ** (1 - 2 * (zb + xb))
            if band == 0 and self.index < 2:
                for j in range(self.pairs + 1):
                    approx[j] = low[:, j * LANES:(j + 1) * LANES]
            for i in range(mz):
                row = low[i * mx:(i + 1) * mx, :width]
                if band > 0:
                    self.details[4 * zb + xb - 1, i] = row
                elif self.index == 2:
                    approx[i] = row
                self.details[4 * zb + 2 + xb - 1, i] = high[i * mx:(i + 1) * mx]


class FirstLevel(Level):
    def tile_states(self, t):
        nz, nx = self.nz, self.nx
        states = boundary_states(lambda z: self.split[t, z * nx:(z + 1) * nx, :], nz)
        for i, state in enumerate(states):
            self.zs[t, i * nx:(i + 1) * nx, :] = state
        states = boundary_states(lambda x: self.split[t, pl.ds(x, nz, stride=nx), :], nx)
        for i, state in enumerate(states):
            self.xs[i // 2, t, i % 2] = state
        states = boundary_states(lambda x: self.zs[t, pl.ds(x, 4, stride=nx), :], nx)
        for i, state in enumerate(states):
            self.cs[i // 2, t, i % 2] = state

    def prepare(self, c):
        self.split_chunk(c)
        start, stop = self.tile_range(c)
        pl.loop(start, stop, unroll=min(2, stop - start))(self.tile_states)

    def tile_planes(self, t):
        nz, nx = self.nz, self.nx
        mx = nx // 2
        bands = lift(
            lambda x: self.split[t, pl.ds(x, nz, stride=nx), :], nx,
            (self.xr[0, t, 0], self.xr[0, t, 1]), (self.xr[1, t, 0], self.xr[1, t, 1]),
        )
        for band, lines in enumerate(bands):
            for i, line in enumerate(lines):
                self.own_x[band, t, pl.ds(i, nz, stride=mx), :] = line
        bands = lift(
            lambda x: self.zr[t, pl.ds(x, 4, stride=nx), :], nx,
            (self.cr[0, t, 0], self.cr[0, t, 1]), (self.cr[1, t, 0], self.cr[1, t, 1]),
        )
        for band, lines in enumerate(bands):
            for i, line in enumerate(lines):
                self.halo_x[band, t, pl.ds(i, 4, stride=mx), :] = line
        for xb in (0, 1):
            halo = [self.halo_x[xb, t, i * mx:(i + 1) * mx, :] for i in range(4)]
            bands = lift(lambda z: self.own_x[xb, t, z * mx:(z + 1) * mx, :], nz, halo[:2], halo[2:])
            for zb, lines in enumerate(bands):
                for i, line in enumerate(lines):
                    row = (2 * zb + xb) * (nz * nx // 4) + i * mx
                    self.both[t, row:row + mx, :] = line

    def receive(self, c):
        for copy in self.copies[c]:
            copy.wait_recv()
        start, stop = self.tile_range(c)
        pl.loop(start, stop, unroll=min(2, stop - start))(self.tile_planes)


def buffers(nz, nx, pairs):
    tiles = 2 * pairs + 1
    shapes = [(tiles, nz * nx, LANES)]
    shapes += [(tiles, 4 * nx, LANES)] * 2
    shapes += [(2, tiles, 2, nz, LANES)] * 2
    shapes += [(2, tiles, 2, 4, LANES)] * 2
    shapes += [(2, tiles, nz * nx // 2, LANES), (2, tiles, 2 * nx, LANES)]
    shapes += [(tiles, nz * nx, LANES)]
    return [pltpu.VMEM(shape, F32) for shape in shapes]


def hand_out(*refs):
    sems = refs[-1]
    n = (len(refs) - 1) // 2
    copies = [pltpu.make_async_copy(refs[i], refs[n + i], sems.at[i]) for i in range(n)]
    for copy in copies:
        copy.start()
    for copy in copies:
        copy.wait()


def kernel(sizes, axes, u_ref, one_ref, two_ref, three_ref, approx_ref, *scratch):
    scratch = list(scratch)
    send_sems, recv_sems, in_sems, raw, pack_l, pack_r, halo_l, halo_r, approx_four, approx_five = scratch[:10]
    rest = scratch[10:]
    per_level = len(rest) // 3
    gx, gy, gz = axes
    ix, iy, iz = (lax.axis_index(a) for a in ("gx", "gy", "gz"))
    around = lambda i, n: (lax.rem(i + n - 1, n), lax.rem(i + 1, n))
    near_x, near_y, near_z = around(ix, gx), around(iy, gy), around(iz, gz)
    peers = {
        "x": [(x, iy, iz) for x in near_x],
        "y": [(ix, y, iz) for y in near_y],
        "z": [(ix, iy, z) for z in near_z],
        "xz": [[(x, iy, z) for z in near_z] for x in near_x],
    }
    (nz, nx, pairs) = sizes[0]
    tiles = 2 * pairs

    loads = [
        pltpu.make_async_copy(u_ref.at[:, :, pl.ds(t * LANES, LANES)], raw.at[t], in_sems.at[t])
        for t in range(tiles)
    ]
    order = [0, tiles - 1] + list(range(1, tiles - 1))
    for t in order:
        loads[t].start()

    barrier = pltpu.get_barrier_semaphore()
    greeted = peers["x"] + peers["y"] + peers["z"] + peers["xz"][0] + peers["xz"][1]
    for where in greeted:
        pl.semaphore_signal(barrier, inc=1, device_id=where, device_id_type=MESH)

    half = pairs // 2
    sems = (send_sems, recv_sems)
    chunks = [(0, half), (half, pairs), (pairs, pairs + 1)]
    source = raw.reshape(tiles + 1, nz * nx, LANES)
    first = FirstLevel(0, nz, nx, pairs, source, rest[:per_level], one_ref, sems, 2, peers, chunks)
    second, third = (
        Level(i, *sizes[i], source, rest[i * per_level:(i + 1) * per_level], details, sems, 18 + 8 * i, peers,
              [(0, sizes[i][2] + 1)])
        for i, source, details in ((1, approx_four, two_ref), (2, approx_five, three_ref))
    )

    groups = LANES // HALO
    part = nz * nx // groups
    lane = lax.broadcasted_iota(jnp.int32, (part, LANES), 1)
    loads[0].wait()
    loads[tiles - 1].wait()
    flat = first.source

    def gather(tile, offset):
        total = None
        for g in range(groups):
            rows = pltpu.roll(flat[tile, g * part:(g + 1) * part, :], (g * HALO - offset) % LANES, 1)
            total = rows if total is None else jnp.where(lane >= g * HALO, rows, total)
        return total

    pack_l[...] = gather(0, 0)
    pack_r[...] = gather(tiles - 1, LANES - HALO)
    pl.semaphore_wait(barrier, len(greeted))
    y_copies = [
        pltpu.make_async_remote_copy(src_ref=src, dst_ref=dst, send_sem=send_sems.at[i], recv_sem=recv_sems.at[i],
                                     device_id=where, device_id_type=MESH)
        for i, (src, dst, where) in enumerate(((pack_l, halo_r, peers["y"][0]), (pack_r, halo_l, peers["y"][1])))
    ]
    for copy in y_copies:
        copy.start()
    for t in range(1, tiles - 1):
        loads[t].wait()
    first.prepare(0)
    first.send(0)
    first.prepare(1)
    first.send(1)
    for copy in y_copies:
        copy.wait_recv()
    for g in range(groups):
        after = pltpu.roll(halo_r[...], (-g * HALO) % LANES, 1)
        before = pltpu.roll(halo_l[...], (LANES - HALO - g * HALO) % LANES, 1)
        flat[tiles, g * part:(g + 1) * part, :] = jnp.where(
            lane < HALO, after, jnp.where(lane >= LANES - HALO, before, 0.0)
        )
    first.prepare(2)
    first.send(2)
    for c in range(3):
        first.receive(c)
    first.lines([0], approx_four)

    second.prepare(0)
    second.send(0)
    for band in (1, 2, 3):
        first.lines([band])
    second.receive(0)
    second.lines([0], approx_five)

    third.prepare(0)
    third.send(0)
    second.lines([1, 2, 3])
    third.receive(0)
    third.lines([0, 1, 2, 3], approx_ref)

    for copy in y_copies:
        copy.wait_send()
    for level in (first, second, third):
        for copies in level.copies:
            for copy in copies:
                copy.wait_send()


def solution(mesh):
    axes = tuple(mesh.shape[a] for a in ("gx", "gy", "gz"))

    def on_device(density):
        nz, nx, ny = density.shape
        sizes = [(nz >> i, nx >> i, (ny >> i) // (2 * LANES)) for i in range(3)]
        tiles = ny // LANES
        shapes = [(7, z // 2, x // 2, p * LANES) for z, x, p in sizes]
        shapes.append(shapes[-1][1:])
        n_sems = 42
        packed = (nz * nx * HALO // LANES, LANES)
        scratch = [
            pltpu.SemaphoreType.DMA((n_sems,)),
            pltpu.SemaphoreType.DMA((n_sems,)),
            pltpu.SemaphoreType.DMA((tiles,)),
            pltpu.VMEM((tiles + 1, nz, nx, LANES), F32),
        ]
        scratch += [pltpu.VMEM(packed, F32)] * 4
        for z, x, p in sizes[:2]:
            scratch.append(pltpu.VMEM((p + 1, z * x // 4, LANES), F32))
        for z, x, p in sizes:
            scratch += buffers(z, x, p)
        outs = [jax.ShapeDtypeStruct(shape, F32) for shape in shapes]
        results = pl.pallas_call(
            functools.partial(kernel, sizes, axes),
            out_shape=[pltpu.VMEM(shape, F32) for shape in shapes],
            in_specs=[pl.BlockSpec(memory_space=pltpu.HBM)],
            out_specs=[pl.BlockSpec(memory_space=pltpu.VMEM)] * 4,
            scratch_shapes=scratch,
            compiler_params=pltpu.CompilerParams(
                collective_id=0, has_side_effects=True, vmem_limit_bytes=59 << 20
            ),
            cost_estimate=pl.CostEstimate(flops=20_000_000, bytes_accessed=2 << 20, transcendentals=0),
        )(density)
        return pl.pallas_call(
            hand_out,
            out_shape=outs,
            in_specs=[pl.BlockSpec(memory_space=pltpu.VMEM)] * 4,
            out_specs=[pl.BlockSpec(memory_space=pltpu.HBM)] * 4,
            scratch_shapes=[pltpu.SemaphoreType.DMA((4,))],
            compiler_params=pltpu.CompilerParams(vmem_limit_bytes=1 << 20),
            cost_estimate=pl.CostEstimate(flops=0, bytes_accessed=2 << 20, transcendentals=0),
        )(*results)

    return jax.shard_map(
        on_device,
        mesh=mesh,
        in_specs=(P("gz", "gx", "gy"),),
        out_specs=(
            P(None, "gz", "gx", "gy"),
            P(None, "gz", "gx", "gy"),
            P(None, "gz", "gx", "gy"),
            P("gz", "gx", "gy"),
        ),
        check_vma=False,
    )
```

```python
import functools

import jax
import jax.numpy as jnp
from jax import lax
from jax.experimental import pallas as pl
from jax.experimental.pallas import tpu as pltpu
from jax.sharding import PartitionSpec as P

ALPHA = -1.586134342
BETA = -0.05298011854
GAMMA = 0.8829110762
DELTA = 0.4435068522
ZETA = 1.149604398

MESH = pl.DeviceIdType.MESH
LANES = 128
HALO = 32
F32 = jnp.float32
BF16 = jnp.bfloat16


def boundary_states(get, n):
    s0, last_s = get(0), get(n - 2)
    lead = get(1) + ALPHA * (s0 + get(2))
    trail = get(n - 3) + ALPHA * (get(n - 4) + last_s)
    return s0, s0 + BETA * lead, get(n - 1) + ALPHA * last_s, last_s + BETA * trail


def lift(get, n, from_left, from_right):
    m = n // 2
    s = [get(2 * i) for i in range(m)]
    d = [get(2 * i + 1) for i in range(m)]
    r, q = from_left
    s_next, p = from_right
    d1 = [r + ALPHA * s[0]]
    for i in range(m):
        d1.append(d[i] + ALPHA * (s[i] + (s[i + 1] if i + 1 < m else s_next)))
    s1 = [q + BETA * d1[0]]
    for i in range(m):
        s1.append(s[i] + BETA * (d1[i] + d1[i + 1]))
    s1.append(p + BETA * d1[m])
    d2 = [d1[i] + GAMMA * (s1[i] + s1[i + 1]) for i in range(m + 1)]
    low = [s1[i + 1] + DELTA * (d2[i] + d2[i + 1]) for i in range(m)]
    return low, d2[1:]


def lift_lanes(even, odd):
    width = even.shape[-1]
    after = lambda v: pltpu.roll(v, width - 1, 1)
    before = lambda v: pltpu.roll(v, 1, 1)
    d = odd + ALPHA * (even + after(even))
    s = even + BETA * (before(d) + d)
    d = d + GAMMA * (s + after(s))
    s = s + DELTA * (before(d) + d)
    return s, d


def circle(tiles):
    ends = tiles[-1]
    turned = pltpu.roll(ends, LANES // 2, 1)
    near = lax.broadcasted_iota(jnp.int32, ends.shape, 1) < LANES // 2
    even = jnp.concatenate(tiles[0:-1:2] + [jnp.where(near, ends, turned)], axis=1)
    odd = jnp.concatenate(tiles[1:-1:2] + [jnp.where(near, turned, ends)], axis=1)
    return even, odd


def exact_select(x, choose):
    parts = []
    for _ in range(3):
        parts.append(x.astype(BF16))
        x = x - parts[-1].astype(F32)
    terms = jnp.dot(jnp.concatenate(parts, axis=0), choose, preferred_element_type=F32)
    n = x.shape[0]
    return terms[:n] + terms[n:2 * n] + terms[2 * n:]


def split_matrix(depth):
    k = lax.broadcasted_iota(jnp.int32, (depth, depth), 0)
    n = lax.broadcasted_iota(jnp.int32, (depth, depth), 1)
    return (k == jnp.where(n < depth // 2, 2 * n, 2 * n - depth + 1)).astype(BF16)


class Level:
    def __init__(self, index, nz, nx, pairs, source, refs, details, sems, sem_base, peers, chunks):
        self.index, self.nz, self.nx, self.pairs = index, nz, nx, pairs
        self.source = source
        (self.split, self.zs, self.zr, self.xs, self.xr, self.cs, self.cr,
         self.own_x, self.halo_x, self.both) = refs
        self.details = details
        self.send_sems, self.recv_sems = sems
        self.peers = peers
        self.chunks = chunks
        self.sem_base = sem_base
        self.copies = [self.make_copies(c) for c in range(len(chunks))]

    def tile_range(self, c):
        start, stop = self.chunks[c]
        return 2 * start, min(2 * stop, 2 * self.pairs + 1)

    def make_copies(self, c):
        start, stop = self.tile_range(c)
        tiles = pl.ds(start, stop - start)
        p = self.peers
        side = 2 * self.nx
        moves = [
            (self.zs.at[tiles, pl.ds(sz * side, side)], self.zr.at[tiles, pl.ds((1 - sz) * side, side)], p["z"][sz])
            for sz in (0, 1)
        ]
        for sx in (0, 1):
            for sz in (0, 1):
                moves.append((self.cs.at[sx, tiles, :, pl.ds(2 * sz, 2)],
                              self.cr.at[1 - sx, tiles, :, pl.ds(2 - 2 * sz, 2)], p["xz"][sx][sz]))
        for sx in (0, 1):
            moves.append((self.xs.at[sx, tiles], self.xr.at[1 - sx, tiles], p["x"][sx]))
        return [
            pltpu.make_async_remote_copy(
                src_ref=src, dst_ref=dst,
                send_sem=self.send_sems.at[self.sem_base + 8 * c + i],
                recv_sem=self.recv_sems.at[self.sem_base + 8 * c + i],
                device_id=where, device_id_type=MESH,
            )
            for i, (src, dst, where) in enumerate(moves)
        ]

    def split_chunk(self, c):
        start, stop = self.chunks[c]
        main = min(stop, self.pairs)
        rows = self.nz * self.nx
        if start == self.pairs:
            self.split[2 * start] = exact_select(self.source[2 * start], split_matrix(LANES))
            return
        firsts = [self.source[2 * j] for j in range(start, stop)]
        seconds = [self.source[2 * j + 1 if j < main else 2 * j] for j in range(start, stop)]
        x = jnp.concatenate([jnp.concatenate(firsts, axis=0), jnp.concatenate(seconds, axis=0)], axis=1)
        both = exact_select(x, split_matrix(2 * LANES))
        for i, j in enumerate(range(start, stop)):
            even = both[i * rows:(i + 1) * rows, :LANES]
            odd = both[i * rows:(i + 1) * rows, LANES:]
            if j < main:
                self.split[2 * j] = even
                self.split[2 * j + 1] = odd
            else:
                lane = lax.broadcasted_iota(jnp.int32, (rows, LANES), 1)
                self.split[2 * j] = jnp.where(lane < LANES // 2, even, odd)

    def prepare(self, c):
        self.split_chunk(c)
        nz, nx = self.nz, self.nx
        states = boundary_states(lambda z: self.split[:, z * nx:(z + 1) * nx, :], nz)
        for i, state in enumerate(states):
            self.zs[:, i * nx:(i + 1) * nx, :] = state
        states = boundary_states(lambda x: self.split[:, pl.ds(x, nz, stride=nx), :], nx)
        for i, state in enumerate(states):
            self.xs[i // 2, :, i % 2] = state
        states = boundary_states(lambda x: self.zs[:, pl.ds(x, 4, stride=nx), :], nx)
        for i, state in enumerate(states):
            self.cs[i // 2, :, i % 2] = state

    def send(self, c):
        for copy in self.copies[c]:
            copy.start()

    def receive(self, c):
        for copy in self.copies[c]:
            copy.wait_recv()
        nz, nx = self.nz, self.nx
        mx = nx // 2
        band_rows = nz * nx // 4
        for ref, n, source, ends in ((self.own_x, nz, self.split, self.xr), (self.halo_x, 4, self.zr, self.cr)):
            bands = lift(
                lambda x: source[:, pl.ds(x, n, stride=nx), :], nx,
                (ends[0, :, 0], ends[0, :, 1]), (ends[1, :, 0], ends[1, :, 1]),
            )
            for band, lines in enumerate(bands):
                for i, line in enumerate(lines):
                    ref[band, :, pl.ds(i, n, stride=mx), :] = line
        for xb in (0, 1):
            halo = [self.halo_x[xb, :, i * mx:(i + 1) * mx, :] for i in range(4)]
            bands = lift(lambda z: self.own_x[xb, :, z * mx:(z + 1) * mx, :], nz, halo[:2], halo[2:])
            for zb, lines in enumerate(bands):
                for i, line in enumerate(lines):
                    row = (2 * zb + xb) * band_rows + i * mx
                    self.both[:, row:row + mx, :] = line

    def lines(self, bands, approx=None):
        mx, mz = self.nx // 2, self.nz // 2
        band_rows = mx * mz
        first, last = bands[0], bands[-1] + 1
        even, odd = circle([self.both[t, first * band_rows:last * band_rows, :] for t in range(2 * self.pairs + 1)])
        lows, highs = lift_lanes(even, odd)
        width = self.pairs * LANES
        for k, band in enumerate(bands):
            zb, xb = band // 2, band % 2
            rows = slice(k * band_rows, (k + 1) * band_rows)
            low = lows[rows] * ZETA ** (3 - 2 * (zb + xb))
            high = highs[rows, :width] * ZETA ** (1 - 2 * (zb + xb))
            if band == 0 and self.index < 2:
                for j in range(self.pairs + 1):
                    approx[j] = low[:, j * LANES:(j + 1) * LANES]
            for i in range(mz):
                row = low[i * mx:(i + 1) * mx, :width]
                if band > 0:
                    self.details[4 * zb + xb - 1, i] = row
                elif self.index == 2:
                    approx[i] = row
                self.details[4 * zb + 2 + xb - 1, i] = high[i * mx:(i + 1) * mx]


class FirstLevel(Level):
    def tile_states(self, t):
        nz, nx = self.nz, self.nx
        states = boundary_states(lambda z: self.split[t, z * nx:(z + 1) * nx, :], nz)
        for i, state in enumerate(states):
            self.zs[t, i * nx:(i + 1) * nx, :] = state
        states = boundary_states(lambda x: self.split[t, pl.ds(x, nz, stride=nx), :], nx)
        for i, state in enumerate(states):
            self.xs[i // 2, t, i % 2] = state
        states = boundary_states(lambda x: self.zs[t, pl.ds(x, 4, stride=nx), :], nx)
        for i, state in enumerate(states):
            self.cs[i // 2, t, i % 2] = state

    def prepare(self, c):
        self.split_chunk(c)
        start, stop = self.tile_range(c)
        pl.loop(start, stop, unroll=min(2, stop - start))(self.tile_states)

    def tile_planes(self, t):
        nz, nx = self.nz, self.nx
        mx = nx // 2
        bands = lift(
            lambda x: self.split[t, pl.ds(x, nz, stride=nx), :], nx,
            (self.xr[0, t, 0], self.xr[0, t, 1]), (self.xr[1, t, 0], self.xr[1, t, 1]),
        )
        for band, lines in enumerate(bands):
            for i, line in enumerate(lines):
                self.own_x[band, t, pl.ds(i, nz, stride=mx), :] = line
        bands = lift(
            lambda x: self.zr[t, pl.ds(x, 4, stride=nx), :], nx,
            (self.cr[0, t, 0], self.cr[0, t, 1]), (self.cr[1, t, 0], self.cr[1, t, 1]),
        )
        for band, lines in enumerate(bands):
            for i, line in enumerate(lines):
                self.halo_x[band, t, pl.ds(i, 4, stride=mx), :] = line
        for xb in (0, 1):
            halo = [self.halo_x[xb, t, i * mx:(i + 1) * mx, :] for i in range(4)]
            bands = lift(lambda z: self.own_x[xb, t, z * mx:(z + 1) * mx, :], nz, halo[:2], halo[2:])
            for zb, lines in enumerate(bands):
                for i, line in enumerate(lines):
                    row = (2 * zb + xb) * (nz * nx // 4) + i * mx
                    self.both[t, row:row + mx, :] = line

    def receive(self, c):
        for copy in self.copies[c]:
            copy.wait_recv()
        start, stop = self.tile_range(c)
        pl.loop(start, stop, unroll=min(2, stop - start))(self.tile_planes)


def buffers(nz, nx, pairs):
    tiles = 2 * pairs + 1
    shapes = [(tiles, nz * nx, LANES)]
    shapes += [(tiles, 4 * nx, LANES)] * 2
    shapes += [(2, tiles, 2, nz, LANES)] * 2
    shapes += [(2, tiles, 2, 4, LANES)] * 2
    shapes += [(2, tiles, nz * nx // 2, LANES), (2, tiles, 2 * nx, LANES)]
    shapes += [(tiles, nz * nx, LANES)]
    return [pltpu.VMEM(shape, F32) for shape in shapes]


def hand_out(*refs):
    sems = refs[-1]
    n = (len(refs) - 1) // 2
    copies = [pltpu.make_async_copy(refs[i], refs[n + i], sems.at[i]) for i in range(n)]
    for copy in copies:
        copy.start()
    for copy in copies:
        copy.wait()


def kernel(sizes, axes, u_ref, one_ref, two_ref, three_ref, approx_ref, *scratch):
    scratch = list(scratch)
    send_sems, recv_sems, in_sems, raw, pack_l, pack_r, halo_l, halo_r, approx_four, approx_five = scratch[:10]
    rest = scratch[10:]
    per_level = len(rest) // 3
    gx, gy, gz = axes
    ix, iy, iz = (lax.axis_index(a) for a in ("gx", "gy", "gz"))
    around = lambda i, n: (lax.rem(i + n - 1, n), lax.rem(i + 1, n))
    near_x, near_y, near_z = around(ix, gx), around(iy, gy), around(iz, gz)
    peers = {
        "x": [(x, iy, iz) for x in near_x],
        "y": [(ix, y, iz) for y in near_y],
        "z": [(ix, iy, z) for z in near_z],
        "xz": [[(x, iy, z) for z in near_z] for x in near_x],
    }
    (nz, nx, pairs) = sizes[0]
    tiles = 2 * pairs

    loads = [
        pltpu.make_async_copy(u_ref.at[:, :, pl.ds(t * LANES, LANES)], raw.at[t], in_sems.at[t])
        for t in range(tiles)
    ]
    order = [0, tiles - 1] + list(range(1, tiles - 1))
    for t in order:
        loads[t].start()

    barrier = pltpu.get_barrier_semaphore()
    greeted = peers["x"] + peers["y"] + peers["z"] + peers["xz"][0] + peers["xz"][1]
    for where in greeted:
        pl.semaphore_signal(barrier, inc=1, device_id=where, device_id_type=MESH)

    half = pairs // 2
    sems = (send_sems, recv_sems)
    chunks = [(0, half), (half, pairs), (pairs, pairs + 1)]
    source = raw.reshape(tiles + 1, nz * nx, LANES)
    first = FirstLevel(0, nz, nx, pairs, source, rest[:per_level], one_ref, sems, 2, peers, chunks)
    second, third = (
        Level(i, *sizes[i], source, rest[i * per_level:(i + 1) * per_level], details, sems, 18 + 8 * i, peers,
              [(0, sizes[i][2] + 1)])
        for i, source, details in ((1, approx_four, two_ref), (2, approx_five, three_ref))
    )

    groups = LANES // HALO
    part = nz * nx // groups
    lane = lax.broadcasted_iota(jnp.int32, (part, LANES), 1)
    loads[0].wait()
    loads[tiles - 1].wait()
    flat = first.source

    def gather(tile, offset):
        total = None
        for g in range(groups):
            rows = pltpu.roll(flat[tile, g * part:(g + 1) * part, :], (g * HALO - offset) % LANES, 1)
            total = rows if total is None else jnp.where(lane >= g * HALO, rows, total)
        return total

    pack_l[...] = gather(0, 0)
    pack_r[...] = gather(tiles - 1, LANES - HALO)
    pl.semaphore_wait(barrier, len(greeted))
    y_copies = [
        pltpu.make_async_remote_copy(src_ref=src, dst_ref=dst, send_sem=send_sems.at[i], recv_sem=recv_sems.at[i],
                                     device_id=where, device_id_type=MESH)
        for i, (src, dst, where) in enumerate(((pack_l, halo_r, peers["y"][0]), (pack_r, halo_l, peers["y"][1])))
    ]
    for copy in y_copies:
        copy.start()
    for t in range(1, 2 * half):
        loads[t].wait()
    first.prepare(0)
    first.send(0)
    for t in range(2 * half, tiles - 1):
        loads[t].wait()
    first.prepare(1)
    first.send(1)
    for copy in y_copies:
        copy.wait_recv()
    for g in range(groups):
        after = pltpu.roll(halo_r[...], (-g * HALO) % LANES, 1)
        before = pltpu.roll(halo_l[...], (LANES - HALO - g * HALO) % LANES, 1)
        flat[tiles, g * part:(g + 1) * part, :] = jnp.where(
            lane < HALO, after, jnp.where(lane >= LANES - HALO, before, 0.0)
        )
    first.prepare(2)
    first.send(2)
    for c in range(3):
        first.receive(c)
    first.lines([0], approx_four)

    second.prepare(0)
    second.send(0)
    for band in (1, 2, 3):
        first.lines([band])
    second.receive(0)
    second.lines([0], approx_five)

    third.prepare(0)
    third.send(0)
    second.lines([1, 2, 3])
    third.receive(0)
    third.lines([0, 1, 2, 3], approx_ref)

    for copy in y_copies:
        copy.wait_send()
    for level in (first, second, third):
        for copies in level.copies:
            for copy in copies:
                copy.wait_send()


def solution(mesh):
    axes = tuple(mesh.shape[a] for a in ("gx", "gy", "gz"))

    def on_device(density):
        nz, nx, ny = density.shape
        sizes = [(nz >> i, nx >> i, (ny >> i) // (2 * LANES)) for i in range(3)]
        tiles = ny // LANES
        shapes = [(7, z // 2, x // 2, p * LANES) for z, x, p in sizes]
        shapes.append(shapes[-1][1:])
        n_sems = 42
        packed = (nz * nx * HALO // LANES, LANES)
        scratch = [
            pltpu.SemaphoreType.DMA((n_sems,)),
            pltpu.SemaphoreType.DMA((n_sems,)),
            pltpu.SemaphoreType.DMA((tiles,)),
            pltpu.VMEM((tiles + 1, nz, nx, LANES), F32),
        ]
        scratch += [pltpu.VMEM(packed, F32)] * 4
        for z, x, p in sizes[:2]:
            scratch.append(pltpu.VMEM((p + 1, z * x // 4, LANES), F32))
        for z, x, p in sizes:
            scratch += buffers(z, x, p)
        outs = [jax.ShapeDtypeStruct(shape, F32) for shape in shapes]
        results = pl.pallas_call(
            functools.partial(kernel, sizes, axes),
            out_shape=[pltpu.VMEM(shape, F32) for shape in shapes],
            in_specs=[pl.BlockSpec(memory_space=pltpu.HBM)],
            out_specs=[pl.BlockSpec(memory_space=pltpu.VMEM)] * 4,
            scratch_shapes=scratch,
            compiler_params=pltpu.CompilerParams(
                collective_id=0, has_side_effects=True, vmem_limit_bytes=59 << 20
            ),
            cost_estimate=pl.CostEstimate(flops=20_000_000, bytes_accessed=2 << 20, transcendentals=0),
        )(density)
        return pl.pallas_call(
            hand_out,
            out_shape=outs,
            in_specs=[pl.BlockSpec(memory_space=pltpu.VMEM)] * 4,
            out_specs=[pl.BlockSpec(memory_space=pltpu.HBM)] * 4,
            scratch_shapes=[pltpu.SemaphoreType.DMA((4,))],
            compiler_params=pltpu.CompilerParams(vmem_limit_bytes=1 << 20),
            cost_estimate=pl.CostEstimate(flops=0, bytes_accessed=2 << 20, transcendentals=0),
        )(*results)

    return jax.shard_map(
        on_device,
        mesh=mesh,
        in_specs=(P("gz", "gx", "gy"),),
        out_specs=(
            P(None, "gz", "gx", "gy"),
            P(None, "gz", "gx", "gy"),
            P(None, "gz", "gx", "gy"),
            P("gz", "gx", "gy"),
        ),
        check_vma=False,
    )
```

```python
import functools

import jax
import jax.numpy as jnp
from jax import lax
from jax.experimental import pallas as pl
from jax.experimental.pallas import tpu as pltpu
from jax.sharding import PartitionSpec as P

ALPHA = -1.586134342
BETA = -0.05298011854
GAMMA = 0.8829110762
DELTA = 0.4435068522
ZETA = 1.149604398

MESH = pl.DeviceIdType.MESH
LANES = 128
HALO = 32
F32 = jnp.float32
BF16 = jnp.bfloat16


def boundary_states(get, n):
    s0, last_s = get(0), get(n - 2)
    lead = get(1) + ALPHA * (s0 + get(2))
    trail = get(n - 3) + ALPHA * (get(n - 4) + last_s)
    return s0, s0 + BETA * lead, get(n - 1) + ALPHA * last_s, last_s + BETA * trail


def lift(get, n, from_left, from_right):
    m = n // 2
    s = [get(2 * i) for i in range(m)]
    d = [get(2 * i + 1) for i in range(m)]
    r, q = from_left
    s_next, p = from_right
    d1 = [r + ALPHA * s[0]]
    for i in range(m):
        d1.append(d[i] + ALPHA * (s[i] + (s[i + 1] if i + 1 < m else s_next)))
    s1 = [q + BETA * d1[0]]
    for i in range(m):
        s1.append(s[i] + BETA * (d1[i] + d1[i + 1]))
    s1.append(p + BETA * d1[m])
    d2 = [d1[i] + GAMMA * (s1[i] + s1[i + 1]) for i in range(m + 1)]
    low = [s1[i + 1] + DELTA * (d2[i] + d2[i + 1]) for i in range(m)]
    return low, d2[1:]


def lift_lanes(even, odd):
    width = even.shape[-1]
    after = lambda v: pltpu.roll(v, width - 1, 1)
    before = lambda v: pltpu.roll(v, 1, 1)
    d = odd + ALPHA * (even + after(even))
    s = even + BETA * (before(d) + d)
    d = d + GAMMA * (s + after(s))
    s = s + DELTA * (before(d) + d)
    return s, d


def circle(tiles):
    ends = tiles[-1]
    turned = pltpu.roll(ends, LANES // 2, 1)
    near = lax.broadcasted_iota(jnp.int32, ends.shape, 1) < LANES // 2
    even = jnp.concatenate(tiles[0:-1:2] + [jnp.where(near, ends, turned)], axis=1)
    odd = jnp.concatenate(tiles[1:-1:2] + [jnp.where(near, turned, ends)], axis=1)
    return even, odd


def exact_select(x, choose):
    parts = []
    for _ in range(3):
        parts.append(x.astype(BF16))
        x = x - parts[-1].astype(F32)
    terms = jnp.dot(jnp.concatenate(parts, axis=0), choose, preferred_element_type=F32)
    n = x.shape[0]
    return terms[:n] + terms[n:2 * n] + terms[2 * n:]


def split_matrix(depth):
    k = lax.broadcasted_iota(jnp.int32, (depth, depth), 0)
    n = lax.broadcasted_iota(jnp.int32, (depth, depth), 1)
    return (k == jnp.where(n < depth // 2, 2 * n, 2 * n - depth + 1)).astype(BF16)


class Level:
    def __init__(self, index, nz, nx, pairs, source, refs, details, sems, sem_base, peers, chunks):
        self.index, self.nz, self.nx, self.pairs = index, nz, nx, pairs
        self.source = source
        (self.split, self.zs, self.zr, self.xs, self.xr, self.cs, self.cr,
         self.own_x, self.halo_x, self.both) = refs
        self.details = details
        self.send_sems, self.recv_sems = sems
        self.peers = peers
        self.chunks = chunks
        self.sem_base = sem_base
        self.copies = [self.make_copies(c) for c in range(len(chunks))]

    def tile_range(self, c):
        start, stop = self.chunks[c]
        return 2 * start, min(2 * stop, 2 * self.pairs + 1)

    def make_copies(self, c):
        start, stop = self.tile_range(c)
        tiles = pl.ds(start, stop - start)
        p = self.peers
        side = 2 * self.nx
        moves = [
            (self.zs.at[tiles, pl.ds(sz * side, side)], self.zr.at[tiles, pl.ds((1 - sz) * side, side)], p["z"][sz])
            for sz in (0, 1)
        ]
        for sx in (0, 1):
            for sz in (0, 1):
                moves.append((self.cs.at[sx, tiles, :, pl.ds(2 * sz, 2)],
                              self.cr.at[1 - sx, tiles, :, pl.ds(2 - 2 * sz, 2)], p["xz"][sx][sz]))
        for sx in (0, 1):
            moves.append((self.xs.at[sx, tiles], self.xr.at[1 - sx, tiles], p["x"][sx]))
        return [
            pltpu.make_async_remote_copy(
                src_ref=src, dst_ref=dst,
                send_sem=self.send_sems.at[self.sem_base + 8 * c + i],
                recv_sem=self.recv_sems.at[self.sem_base + 8 * c + i],
                device_id=where, device_id_type=MESH,
            )
            for i, (src, dst, where) in enumerate(moves)
        ]

    def split_chunk(self, c):
        start, stop = self.chunks[c]
        main = min(stop, self.pairs)
        rows = self.nz * self.nx
        if start == self.pairs:
            self.split[2 * start] = exact_select(self.source[2 * start], split_matrix(LANES))
            return
        firsts = [self.source[2 * j] for j in range(start, stop)]
        seconds = [self.source[2 * j + 1 if j < main else 2 * j] for j in range(start, stop)]
        x = jnp.concatenate([jnp.concatenate(firsts, axis=0), jnp.concatenate(seconds, axis=0)], axis=1)
        both = exact_select(x, split_matrix(2 * LANES))
        for i, j in enumerate(range(start, stop)):
            even = both[i * rows:(i + 1) * rows, :LANES]
            odd = both[i * rows:(i + 1) * rows, LANES:]
            if j < main:
                self.split[2 * j] = even
                self.split[2 * j + 1] = odd
            else:
                lane = lax.broadcasted_iota(jnp.int32, (rows, LANES), 1)
                self.split[2 * j] = jnp.where(lane < LANES // 2, even, odd)

    def prepare(self, c):
        self.split_chunk(c)
        nz, nx = self.nz, self.nx
        states = boundary_states(lambda z: self.split[:, z * nx:(z + 1) * nx, :], nz)
        for i, state in enumerate(states):
            self.zs[:, i * nx:(i + 1) * nx, :] = state
        states = boundary_states(lambda x: self.split[:, pl.ds(x, nz, stride=nx), :], nx)
        for i, state in enumerate(states):
            self.xs[i // 2, :, i % 2] = state
        states = boundary_states(lambda x: self.zs[:, pl.ds(x, 4, stride=nx), :], nx)
        for i, state in enumerate(states):
            self.cs[i // 2, :, i % 2] = state

    def send(self, c):
        for copy in self.copies[c]:
            copy.start()

    def receive(self, c):
        for copy in self.copies[c]:
            copy.wait_recv()
        nz, nx = self.nz, self.nx
        mx = nx // 2
        band_rows = nz * nx // 4
        for ref, n, source, ends in ((self.own_x, nz, self.split, self.xr), (self.halo_x, 4, self.zr, self.cr)):
            bands = lift(
                lambda x: source[:, pl.ds(x, n, stride=nx), :], nx,
                (ends[0, :, 0], ends[0, :, 1]), (ends[1, :, 0], ends[1, :, 1]),
            )
            for band, lines in enumerate(bands):
                for i, line in enumerate(lines):
                    ref[band, :, pl.ds(i, n, stride=mx), :] = line
        for xb in (0, 1):
            halo = [self.halo_x[xb, :, i * mx:(i + 1) * mx, :] for i in range(4)]
            bands = lift(lambda z: self.own_x[xb, :, z * mx:(z + 1) * mx, :], nz, halo[:2], halo[2:])
            for zb, lines in enumerate(bands):
                for i, line in enumerate(lines):
                    row = (2 * zb + xb) * band_rows + i * mx
                    self.both[:, row:row + mx, :] = line

    def lines(self, bands, approx=None):
        mx, mz = self.nx // 2, self.nz // 2
        band_rows = mx * mz
        first, last = bands[0], bands[-1] + 1
        even, odd = circle([self.both[t, first * band_rows:last * band_rows, :] for t in range(2 * self.pairs + 1)])
        lows, highs = lift_lanes(even, odd)
        width = self.pairs * LANES
        for k, band in enumerate(bands):
            zb, xb = band // 2, band % 2
            rows = slice(k * band_rows, (k + 1) * band_rows)
            low = lows[rows] * ZETA ** (3 - 2 * (zb + xb))
            high = highs[rows, :width] * ZETA ** (1 - 2 * (zb + xb))
            if band == 0 and self.index < 2:
                for j in range(self.pairs + 1):
                    approx[j] = low[:, j * LANES:(j + 1) * LANES]
            for i in range(mz):
                row = low[i * mx:(i + 1) * mx, :width]
                if band > 0:
                    self.details[4 * zb + xb - 1, i] = row
                elif self.index == 2:
                    approx[i] = row
                self.details[4 * zb + 2 + xb - 1, i] = high[i * mx:(i + 1) * mx]


class FirstLevel(Level):
    def tile_states(self, t):
        nz, nx = self.nz, self.nx
        states = boundary_states(lambda z: self.split[t, z * nx:(z + 1) * nx, :], nz)
        for i, state in enumerate(states):
            self.zs[t, i * nx:(i + 1) * nx, :] = state
        states = boundary_states(lambda x: self.split[t, pl.ds(x, nz, stride=nx), :], nx)
        for i, state in enumerate(states):
            self.xs[i // 2, t, i % 2] = state
        states = boundary_states(lambda x: self.zs[t, pl.ds(x, 4, stride=nx), :], nx)
        for i, state in enumerate(states):
            self.cs[i // 2, t, i % 2] = state

    def prepare(self, c):
        self.split_chunk(c)
        start, stop = self.tile_range(c)
        pl.loop(start, stop, unroll=min(2, stop - start))(self.tile_states)

    def tile_planes(self, t):
        nz, nx = self.nz, self.nx
        mx = nx // 2
        bands = lift(
            lambda x: self.split[t, pl.ds(x, nz, stride=nx), :], nx,
            (self.xr[0, t, 0], self.xr[0, t, 1]), (self.xr[1, t, 0], self.xr[1, t, 1]),
        )
        for band, lines in enumerate(bands):
            for i, line in enumerate(lines):
                self.own_x[band, t, pl.ds(i, nz, stride=mx), :] = line
        bands = lift(
            lambda x: self.zr[t, pl.ds(x, 4, stride=nx), :], nx,
            (self.cr[0, t, 0], self.cr[0, t, 1]), (self.cr[1, t, 0], self.cr[1, t, 1]),
        )
        for band, lines in enumerate(bands):
            for i, line in enumerate(lines):
                self.halo_x[band, t, pl.ds(i, 4, stride=mx), :] = line
        for xb in (0, 1):
            halo = [self.halo_x[xb, t, i * mx:(i + 1) * mx, :] for i in range(4)]
            bands = lift(lambda z: self.own_x[xb, t, z * mx:(z + 1) * mx, :], nz, halo[:2], halo[2:])
            for zb, lines in enumerate(bands):
                for i, line in enumerate(lines):
                    row = (2 * zb + xb) * (nz * nx // 4) + i * mx
                    self.both[t, row:row + mx, :] = line

    def receive(self, c):
        for copy in self.copies[c]:
            copy.wait_recv()
        start, stop = self.tile_range(c)
        pl.loop(start, stop, unroll=min(2, stop - start))(self.tile_planes)


def buffers(nz, nx, pairs):
    tiles = 2 * pairs + 1
    shapes = [(tiles, nz * nx, LANES)]
    shapes += [(tiles, 4 * nx, LANES)] * 2
    shapes += [(2, tiles, 2, nz, LANES)] * 2
    shapes += [(2, tiles, 2, 4, LANES)] * 2
    shapes += [(2, tiles, nz * nx // 2, LANES), (2, tiles, 2 * nx, LANES)]
    shapes += [(tiles, nz * nx, LANES)]
    return [pltpu.VMEM(shape, F32) for shape in shapes]


def hand_out(*refs):
    sems = refs[-1]
    n = (len(refs) - 1) // 2
    copies = [pltpu.make_async_copy(refs[i], refs[n + i], sems.at[i]) for i in range(n)]
    for copy in copies:
        copy.start()
    for copy in copies:
        copy.wait()


def kernel(sizes, axes, u_ref, one_ref, two_ref, three_ref, approx_ref, *scratch):
    scratch = list(scratch)
    send_sems, recv_sems, in_sems, raw, pack_l, pack_r, halo_l, halo_r, approx_four, approx_five = scratch[:10]
    rest = scratch[10:]
    per_level = len(rest) // 3
    gx, gy, gz = axes
    ix, iy, iz = (lax.axis_index(a) for a in ("gx", "gy", "gz"))
    around = lambda i, n: (lax.rem(i + n - 1, n), lax.rem(i + 1, n))
    near_x, near_y, near_z = around(ix, gx), around(iy, gy), around(iz, gz)
    peers = {
        "x": [(x, iy, iz) for x in near_x],
        "y": [(ix, y, iz) for y in near_y],
        "z": [(ix, iy, z) for z in near_z],
        "xz": [[(x, iy, z) for z in near_z] for x in near_x],
    }
    (nz, nx, pairs) = sizes[0]
    tiles = 2 * pairs

    loads = [
        pltpu.make_async_copy(u_ref.at[:, :, pl.ds(t * LANES, LANES)], raw.at[t], in_sems.at[t])
        for t in range(tiles)
    ]
    order = [0, tiles - 1] + list(range(1, tiles - 1))
    for t in order:
        loads[t].start()

    barrier = pltpu.get_barrier_semaphore()
    greeted = peers["x"] + peers["y"] + peers["z"] + peers["xz"][0] + peers["xz"][1]
    for where in greeted:
        pl.semaphore_signal(barrier, inc=1, device_id=where, device_id_type=MESH)

    half = pairs - 1
    sems = (send_sems, recv_sems)
    chunks = [(0, half), (half, pairs), (pairs, pairs + 1)]
    source = raw.reshape(tiles + 1, nz * nx, LANES)
    first = FirstLevel(0, nz, nx, pairs, source, rest[:per_level], one_ref, sems, 2, peers, chunks)
    second, third = (
        Level(i, *sizes[i], source, rest[i * per_level:(i + 1) * per_level], details, sems, 18 + 8 * i, peers,
              [(0, sizes[i][2] + 1)])
        for i, source, details in ((1, approx_four, two_ref), (2, approx_five, three_ref))
    )

    groups = LANES // HALO
    part = nz * nx // groups
    lane = lax.broadcasted_iota(jnp.int32, (part, LANES), 1)
    loads[0].wait()
    loads[tiles - 1].wait()
    flat = first.source

    def gather(tile, offset):
        total = None
        for g in range(groups):
            rows = pltpu.roll(flat[tile, g * part:(g + 1) * part, :], (g * HALO - offset) % LANES, 1)
            total = rows if total is None else jnp.where(lane >= g * HALO, rows, total)
        return total

    pack_l[...] = gather(0, 0)
    pack_r[...] = gather(tiles - 1, LANES - HALO)
    pl.semaphore_wait(barrier, len(greeted))
    y_copies = [
        pltpu.make_async_remote_copy(src_ref=src, dst_ref=dst, send_sem=send_sems.at[i], recv_sem=recv_sems.at[i],
                                     device_id=where, device_id_type=MESH)
        for i, (src, dst, where) in enumerate(((pack_l, halo_r, peers["y"][0]), (pack_r, halo_l, peers["y"][1])))
    ]
    for copy in y_copies:
        copy.start()
    for t in range(1, 2 * half):
        loads[t].wait()
    first.prepare(0)
    first.send(0)
    for t in range(2 * half, tiles - 1):
        loads[t].wait()
    first.prepare(1)
    first.send(1)
    for copy in y_copies:
        copy.wait_recv()
    for g in range(groups):
        after = pltpu.roll(halo_r[...], (-g * HALO) % LANES, 1)
        before = pltpu.roll(halo_l[...], (LANES - HALO - g * HALO) % LANES, 1)
        flat[tiles, g * part:(g + 1) * part, :] = jnp.where(
            lane < HALO, after, jnp.where(lane >= LANES - HALO, before, 0.0)
        )
    first.prepare(2)
    first.send(2)
    for c in range(3):
        first.receive(c)
    first.lines([0], approx_four)

    second.prepare(0)
    second.send(0)
    for band in (1, 2, 3):
        first.lines([band])
    second.receive(0)
    second.lines([0], approx_five)

    third.prepare(0)
    third.send(0)
    second.lines([1, 2, 3])
    third.receive(0)
    third.lines([0, 1, 2, 3], approx_ref)

    for copy in y_copies:
        copy.wait_send()
    for level in (first, second, third):
        for copies in level.copies:
            for copy in copies:
                copy.wait_send()


def solution(mesh):
    axes = tuple(mesh.shape[a] for a in ("gx", "gy", "gz"))

    def on_device(density):
        nz, nx, ny = density.shape
        sizes = [(nz >> i, nx >> i, (ny >> i) // (2 * LANES)) for i in range(3)]
        tiles = ny // LANES
        shapes = [(7, z // 2, x // 2, p * LANES) for z, x, p in sizes]
        shapes.append(shapes[-1][1:])
        n_sems = 42
        packed = (nz * nx * HALO // LANES, LANES)
        scratch = [
            pltpu.SemaphoreType.DMA((n_sems,)),
            pltpu.SemaphoreType.DMA((n_sems,)),
            pltpu.SemaphoreType.DMA((tiles,)),
            pltpu.VMEM((tiles + 1, nz, nx, LANES), F32),
        ]
        scratch += [pltpu.VMEM(packed, F32)] * 4
        for z, x, p in sizes[:2]:
            scratch.append(pltpu.VMEM((p + 1, z * x // 4, LANES), F32))
        for z, x, p in sizes:
            scratch += buffers(z, x, p)
        outs = [jax.ShapeDtypeStruct(shape, F32) for shape in shapes]
        results = pl.pallas_call(
            functools.partial(kernel, sizes, axes),
            out_shape=[pltpu.VMEM(shape, F32) for shape in shapes],
            in_specs=[pl.BlockSpec(memory_space=pltpu.HBM)],
            out_specs=[pl.BlockSpec(memory_space=pltpu.VMEM)] * 4,
            scratch_shapes=scratch,
            compiler_params=pltpu.CompilerParams(
                collective_id=0, has_side_effects=True, vmem_limit_bytes=59 << 20
            ),
            cost_estimate=pl.CostEstimate(flops=20_000_000, bytes_accessed=2 << 20, transcendentals=0),
        )(density)
        return pl.pallas_call(
            hand_out,
            out_shape=outs,
            in_specs=[pl.BlockSpec(memory_space=pltpu.VMEM)] * 4,
            out_specs=[pl.BlockSpec(memory_space=pltpu.HBM)] * 4,
            scratch_shapes=[pltpu.SemaphoreType.DMA((4,))],
            compiler_params=pltpu.CompilerParams(vmem_limit_bytes=1 << 20),
            cost_estimate=pl.CostEstimate(flops=0, bytes_accessed=2 << 20, transcendentals=0),
        )(*results)

    return jax.shard_map(
        on_device,
        mesh=mesh,
        in_specs=(P("gz", "gx", "gy"),),
        out_specs=(
            P(None, "gz", "gx", "gy"),
            P(None, "gz", "gx", "gy"),
            P(None, "gz", "gx", "gy"),
            P("gz", "gx", "gy"),
        ),
        check_vma=False,
    )
```
